512 devices in a mesh: grid: 32 (over z_hi, y), depth: 16 (over x, z_lo, core).
Axes of the slice: x: 4, y: 8, z: 8 (z_hi: 4, z_lo: 2; z = z_hi * 2 + z_lo), core: 2. Of those that a mesh axis runs over, the one named last changes fastest.
Arguments:
- amplitudes: bfloat16 [2, 32768, 1024], P(None, 'grid', 'depth'), may hold values from -6 to 6
- first_factor: bfloat16 [2, 1024, 512], P(None, 'depth'), may hold values from -0.1875 to 0.1875
- second_factor: bfloat16 [2, 1024, 512], replicated, may hold values from -0.125 to 0.125
Outputs:
- amplitude_block: bfloat16 [2, 1024, 16, 512], P(None, ('grid', 'depth'))
The draws below stay inside these ranges and needn't reach their ends.
All inputs are finite; a program needn't handle non-finite values.
Results may differ from the reference program's by a relative error of at most 0.025.
Values may be sent and summed in bfloat16 or wider, within the bound.
A program may use at most 64 MiB of HBM per device.

```python
import jax
import jax.numpy as jnp
from jax import lax

K1 = 1024
J = 512
JHI = 32
RLO = 32
M = 512
JLO = 16
G2 = 1024
R = 32768
RHI = 1024
N_DEPTH = 16


def spiked(values, key, source, target, parts, factor):
    def block_of(position):
        return (jnp.arange(values.shape[position]) // (values.shape[position] // parts)).reshape((-1,) + (1,) * (values.ndim - 1 - position))

    first = jax.random.permutation(key, parts)[block_of(target)]
    second = (block_of(target) + parts // 2) % parts
    return jnp.where((block_of(source) == first) | (block_of(source) == second), factor * values, values)


def levels(stream_key, extent, split, smallest, high):
    level, own = 1.0, jax.random.fold_in(stream_key, 6)
    for position, blocks in split:
        heights = jnp.exp(jax.random.uniform(jax.random.fold_in(own, position), (blocks,), jnp.float32, smallest / len(split), high / len(split)))
        level = level * jnp.repeat(heights, extent[position] // blocks).reshape([-1 if axis == position else 1 for axis in range(len(extent))])
    return level


def centred(key, dims, spread, limit, cuts=(), kind=jnp.bfloat16):
    entries = spread * jax.random.normal(key, dims, jnp.float32)
    if cuts:
        entries = entries * levels(key, dims, cuts, -0.22, 0.18)
    return jnp.clip(entries, -limit, limit).astype(kind)


def noise_with(stream_key, dims, scale, most, cuts, heavy, held_as=jnp.bfloat16):
    values = scale * jax.random.normal(stream_key, dims, jnp.float32)
    if cuts:
        values = values * levels(stream_key, dims, cuts, -0.22, 0.18)
    return jnp.clip(spiked(values, jax.random.fold_in(stream_key, 3), *heavy), -most, most).astype(held_as)


def setup_inputs(seed: int = 0) -> dict:
    key_list = jax.random.split(jax.random.key(seed), 4)
    return {
        "amplitudes": centred(key_list[0], (2, R, K1), 1.0, 6.0, ((1, 32), (2, 16))),
        "first_factor": noise_with(key_list[1], (2, K1, J), (2 * K1) ** -0.5, 0.1875, ((1, 16),), (1, 2, 16, 2.0)),
        "second_factor": centred(key_list[2], (2, G2, M), (2 * G2) ** -0.5, 0.125),
    }


def complex_product(left, right):
    real_part = jnp.dot(left[0], right[0], preferred_element_type=jnp.float32) - jnp.dot(left[1], right[1], preferred_element_type=jnp.float32)
    imag_part = jnp.dot(left[0], right[1], preferred_element_type=jnp.float32) + jnp.dot(left[1], right[0], preferred_element_type=jnp.float32)
    return jnp.stack((real_part, imag_part), axis=0)


def reference(amplitudes, first_factor, second_factor):
    block_width = K1 // N_DEPTH

    def accumulate(total, block):
        start = (block * block_width).astype(jnp.int32)
        left = lax.dynamic_slice_in_dim(amplitudes, start, block_width, 2)
        right = lax.dynamic_slice_in_dim(first_factor, start, block_width, 1)
        rounded = lax.optimization_barrier(complex_product(left, right).astype(jnp.bfloat16))
        return total + rounded.astype(jnp.float32), None

    blocks = jnp.arange(N_DEPTH, dtype=jnp.int32)
    total, unused = lax.scan(accumulate, jnp.zeros((2, R, J), jnp.float32), blocks)
    contracted = total.astype(jnp.bfloat16)
    grouped = contracted.reshape(2, RHI, RLO, JHI, JLO).transpose(0, 1, 4, 2, 3).reshape(2, RHI * JLO, G2)
    result = complex_product(grouped, second_factor)
    return result.reshape(2, RHI, JLO, M).astype(jnp.bfloat16)
```

```python
import jax
import jax.numpy as jnp
from jax import lax
from jax.experimental import pallas as pl
from jax.experimental.pallas import tpu as pltpu
from jax.sharding import PartitionSpec as P

MESH = pl.DeviceIdType.MESH
XS = 4
JHI = 32
RLO = 32
JLO = 16
J = JHI * JLO
G2 = RLO * JHI
M = 512
KH = 64
KB = 128
ROWS = 128
CHUNKS = 4
CJ = J // CHUNKS
HJ = J // 2
F32 = jnp.float32
BF16 = jnp.bfloat16


def kernel(at_ref, ff_ref, sf_ref, out_ref,
           s_vmem, abuf, bbuf, bt, wbuf, acc, half_send, half_recv, z_send, z_recv, lhs,
           local_sem, a_sems, x_sems, half_sems, z_sems):
    grid = lax.axis_index("grid")
    depth = lax.axis_index("depth")
    x = depth // 4
    zl = (depth // 2) % 2
    core = depth % 2

    def device(dx):
        return grid, (lax.rem(x + dx, XS) * 2 + zl) * 2 + core

    xp, xm, x2 = device(1), device(3), device(2)
    zp = (grid, (x * 2 + 1 - zl) * 2 + core)
    sibling = (grid, (x * 2 + zl) * 2 + 1 - core)
    partners = (xp, xm, x2, zp, sibling)

    barrier = pltpu.get_barrier_semaphore()
    for partner in partners:
        pl.semaphore_signal(barrier, inc=1, device_id=partner, device_id_type=MESH)

    def rows_of(dx, z):
        return pl.ds(pl.multiple_of((lax.rem(x + dx, XS) * 2 + z) * ROWS, ROWS), ROWS)

    z_of = (1 - zl, zl)
    load_b = pltpu.make_async_copy(ff_ref, bbuf.at[0], local_sem.at[0])
    load_a = [pltpu.make_async_copy(at_ref.at[:, :, rows_of(0, z_of[s])], abuf.at[s, 0], local_sem.at[1 + s])
              for s in range(2)]
    load_s = pltpu.make_async_copy(sf_ref, s_vmem, local_sem.at[3])

    def remote(src, dst, sems, i, to):
        return pltpu.make_async_remote_copy(
            src_ref=src, dst_ref=dst, send_sem=sems.at[0, i], recv_sem=sems.at[1, i],
            device_id=to, device_id_type=MESH)

    halves = [pl.ds(h * HJ, HJ) for h in range(2)]
    from_xm = [remote(ff_ref.at[:, :, halves[h]], bbuf.at[1, :, :, halves[h]], x_sems, h, xp) for h in range(2)]
    from_xp = [remote(ff_ref.at[:, :, halves[h]], bbuf.at[3, :, :, halves[h]], x_sems, 2 + h, xm) for h in range(2)]
    relay_p = [remote(bbuf.at[1, 0, :, halves[h]], bbuf.at[2, 0, :, halves[h]], x_sems, 4 + h, xp) for h in range(2)]
    relay_m = [remote(bbuf.at[3, 1, :, halves[h]], bbuf.at[2, 1, :, halves[h]], x_sems, 6 + h, xm) for h in range(2)]

    a_copies = [{dx: remote(at_ref.at[:, :, rows_of(dx, z_of[s])], abuf.at[s, dx], a_sems, s * 3 + dx - 1, device(dx))
                 for dx in (1, 3, 2)} for s in range(2)]

    pl.semaphore_wait(barrier, len(partners))
    from_xm[0].start()
    from_xp[0].start()
    for copy in a_copies[0].values():
        copy.start()
    load_b.start()
    load_a[0].start()
    from_xm[1].start()
    from_xp[1].start()
    load_a[1].start()
    load_s.start()

    def transpose(slot, h):
        bt[halves[h], pl.ds(slot * KB, KB)] = bbuf[slot, :, :, halves[h]].reshape(KB, HJ).T

    lo = lax.broadcasted_iota(jnp.int32, (KB, ROWS), 1) < 64

    def weights(s):
        load_a[s].wait()
        for copy in a_copies[s].values():
            copy.wait_recv()
        for slot in range(XS):
            real = abuf[s, slot, 0].astype(F32)
            imag = abuf[s, slot, 1].astype(F32)
            for_real = jnp.concatenate([real, -imag], axis=0)
            for_imag = jnp.concatenate([imag, real], axis=0)
            first = jnp.where(lo, for_real, pltpu.roll(for_imag, 64, 1))
            second = jnp.where(lo, pltpu.roll(for_real, 64, 1), for_imag)
            mine = jnp.where(core == 0, first, second)
            other = jnp.where(core == 0, second, first)
            wbuf[s, pl.ds(slot * KB, KB)] = jnp.concatenate([mine, other], axis=1).astype(BF16)

    half_copies = [[], []]
    z_copies = []

    def contract(s, h):
        for chunk in range(2 * h, 2 * h + 2):
            where = pl.ds(chunk * CJ, CJ)
            total = jnp.dot(bt[where], wbuf[s], preferred_element_type=F32)
            acc[s, where] = total[:, :128]
            half_send[s, where] = total[:, 128:].astype(BF16)
            copy = remote(half_send.at[s, where], half_recv.at[s, where], half_sems, s * CHUNKS + chunk, sibling)
            copy.start()
            half_copies[s].append(copy)

    def send_z(h):
        for chunk in range(2 * h, 2 * h + 2):
            where = pl.ds(chunk * CJ, CJ)
            half_copies[0][chunk].wait_recv()
            z_send[where] = (acc[0, where] + half_recv[0, where].astype(F32)).astype(BF16)
            copy = remote(z_send.at[where], z_recv.at[where], z_sems, chunk, zp)
            copy.start()
            z_copies.append(copy)

    load_b.wait()
    transpose(0, 0)
    transpose(0, 1)
    from_xm[0].wait_recv()
    relay_p[0].start()
    from_xp[0].wait_recv()
    relay_m[0].start()
    for copy in a_copies[1].values():
        copy.start()
    transpose(1, 0)
    transpose(3, 0)
    weights(0)
    from_xm[1].wait_recv()
    relay_p[1].start()
    from_xp[1].wait_recv()
    relay_m[1].start()
    relay_p[0].wait_recv()
    relay_m[0].wait_recv()
    transpose(2, 0)
    contract(0, 0)
    transpose(1, 1)
    transpose(3, 1)
    send_z(0)
    relay_p[1].wait_recv()
    relay_m[1].wait_recv()
    transpose(2, 1)
    contract(0, 1)
    weights(1)
    send_z(1)
    contract(1, 0)
    contract(1, 1)

    sent = from_xm + from_xp + relay_p + relay_m + half_copies[0] + half_copies[1]
    for copies in a_copies:
        sent += list(copies.values())
    for copy in sent:
        copy.wait_send()

    def swap(v, tile_bit, lane_bit):
        step, width = 1 << tile_bit, 1 << lane_bit
        v = v.reshape(16 // (2 * step), 2, step, JLO, 128)
        a = v[:, 0].reshape(8, JLO, 128)
        b = v[:, 1].reshape(8, JLO, 128)
        low = (lax.broadcasted_iota(jnp.int32, a.shape, 2) // width) % 2 == 0
        a, b = (jnp.where(low, a, pltpu.roll(b, width, 2)), jnp.where(low, pltpu.roll(a, 128 - width, 2), b))
        shape = (16 // (2 * step), 1, step, JLO, 128)
        return jnp.concatenate([a.reshape(shape), b.reshape(shape)], axis=1).reshape(16, JLO, 128)

    load_s.wait()
    result = jnp.zeros((64, M), F32)
    for top in range(2):
        where = pl.ds(top * 256, 256)
        for chunk in range(2 * top, 2 * top + 2):
            half_copies[1][chunk].wait_recv()
            z_copies[chunk].wait_recv()
        value = acc[1, where] + half_recv[1, where].astype(F32) + z_recv[where].astype(F32)
        value = value.astype(BF16).reshape(16, JLO, 128)
        for tile_bit, lane_bit in ((0, 0), (1, 1), (2, 2), (3, 3), (3, 6), (2, 5)):
            value = swap(value, tile_bit, lane_bit)

        right = []
        for u in range(4):
            for p in range(2):
                at = pl.ds((u * 2 + p) * 128, 128)
                turned = pl.ds((u * 2 + 1 - p) * 128, 128)
                for rh in range(2):
                    block = value[p * 8 + rh * 4 + u]
                    lhs[top, pl.ds(rh * 16, 16), at] = block if p == 0 else -block
                    lhs[top, pl.ds(32 + rh * 16, 16), turned] = block
                for t in range(8):
                    rl = (t % 2) * 16 + (t // 4) * 8 + (t // 2 % 2) * 4 + u
                    right.append(s_vmem[p, pl.ds(rl * JHI + top * 16, 16)])
        result += jnp.dot(lhs[top], jnp.concatenate(right, axis=0), preferred_element_type=F32)
    out_ref[...] = result.astype(BF16).reshape(2, 2, JLO, M)

    for copy in z_copies:
        copy.wait_send()


def on_device(amplitudes, first_factor, second_factor):
    arguments = [pltpu.with_memory_space_constraint(a, pltpu.HBM)
                 for a in (jnp.swapaxes(amplitudes, 1, 2), first_factor, second_factor)]
    return pl.pallas_call(
        kernel,
        out_shape=pltpu.VMEM((2, 2, JLO, M), BF16),
        in_specs=[pl.BlockSpec(memory_space=pltpu.HBM)] * 3,
        out_specs=pl.BlockSpec(memory_space=pltpu.VMEM),
        scratch_shapes=[
            pltpu.VMEM((2, G2, M), BF16),
            pltpu.VMEM((2, XS, 2, KH, ROWS), BF16),
            pltpu.VMEM((XS, 2, KH, J), BF16),
            pltpu.VMEM((J, XS * KB), BF16),
            pltpu.VMEM((2, XS * KB, 256), BF16),
            pltpu.VMEM((2, J, 128), F32),
            pltpu.VMEM((2, J, 128), BF16),
            pltpu.VMEM((2, J, 128), BF16),
            pltpu.VMEM((J, 128), BF16),
            pltpu.VMEM((J, 128), BF16),
            pltpu.VMEM((2, 64, G2), BF16),
            pltpu.SemaphoreType.DMA((4,)),
            pltpu.SemaphoreType.DMA((2, 6)),
            pltpu.SemaphoreType.DMA((2, 8)),
            pltpu.SemaphoreType.DMA((2, 2 * CHUNKS)),
            pltpu.SemaphoreType.DMA((2, CHUNKS)),
        ],
        compiler_params=pltpu.CompilerParams(
            collective_id=0, has_side_effects=True, vmem_limit_bytes=32 * 1024 * 1024),
        cost_estimate=pl.CostEstimate(flops=800_000_000, bytes_accessed=2_600_000, transcendentals=0),
    )(*arguments)


def solution(mesh):
    return jax.shard_map(
        on_device, mesh=mesh,
        in_specs=(P(None, "grid", "depth"), P(None, "depth", None), P()),
        out_specs=P(None, ("grid", "depth"), None, None), check_vma=False)
```

```python
import jax
import jax.numpy as jnp
from jax import lax
from jax.experimental import pallas as pl
from jax.experimental.pallas import tpu as pltpu
from jax.sharding import PartitionSpec as P

MESH = pl.DeviceIdType.MESH
XS = 4
YS = 8
JHI = 32
RLO = 32
JLO = 16
J = JHI * JLO
G2 = RLO * JHI
M = 512
KH = 64
KB = 128
ROWS = 128
CHUNKS = 2
CJ = J // CHUNKS
F32 = jnp.float32
BF16 = jnp.bfloat16


def kernel(at_ref, ff_ref, sf_ref, out_ref,
           s_vmem, abuf, bbuf, rows_t, left, acc, half_send, half_recv, z_send, z_recv, lhs,
           local_sem, a_sems, x_sems, y_sems, half_sems, z_sems):
    grid = lax.axis_index("grid")
    depth = lax.axis_index("depth")
    x = depth // 4
    zl = (depth // 2) % 2
    core = depth % 2
    zh = grid // YS
    y = grid % YS

    def device(dx):
        return grid, (lax.rem(x + dx, XS) * 2 + zl) * 2 + (core if dx % 2 == 0 else 1 - core)

    xp, xm, x2 = device(1), device(3), device(2)
    yp = (zh * YS + lax.rem(y + 1, YS), depth)
    ym = (zh * YS + lax.rem(y + YS - 1, YS), depth)
    zp = (grid, (x * 2 + 1 - zl) * 2 + core)
    zc = (grid, (x * 2 + 1 - zl) * 2 + 1 - core)
    sibling = (grid, (x * 2 + zl) * 2 + 1 - core)
    partners = (xp, xm, yp, ym, x2, zp, zc, sibling)

    barrier = pltpu.get_barrier_semaphore()
    for partner in partners:
        pl.semaphore_signal(barrier, inc=1, device_id=partner, device_id_type=MESH)

    def rows_of(dx, z):
        return pl.ds(pl.multiple_of((lax.rem(x + dx, XS) * 2 + z) * ROWS, ROWS), ROWS)

    z_of = (1 - zl, zl)
    load_b = pltpu.make_async_copy(ff_ref, bbuf.at[0], local_sem.at[0])
    load_a = [pltpu.make_async_copy(at_ref.at[:, :, rows_of(0, z_of[s])], abuf.at[s, 0], local_sem.at[1 + s])
              for s in range(2)]
    load_s = pltpu.make_async_copy(sf_ref, s_vmem, local_sem.at[3])

    def remote(src, dst, sems, i, to):
        return pltpu.make_async_remote_copy(
            src_ref=src, dst_ref=dst, send_sem=sems.at[0, i], recv_sem=sems.at[1, i],
            device_id=to, device_id_type=MESH)

    up = y % 2
    down = 1 - up
    from_xm = remote(ff_ref.at[up], bbuf.at[1, up], x_sems, 0, xp)
    from_xp = remote(ff_ref.at[down], bbuf.at[3, down], x_sems, 1, xm)
    relay_p = remote(bbuf.at[1, up], bbuf.at[2, up], x_sems, 2, xp)
    relay_m = remote(bbuf.at[3, down], bbuf.at[2, down], x_sems, 3, xm)
    to_yp = remote(bbuf.at[1, up], bbuf.at[1, up], y_sems, 0, yp)
    to_ym = remote(bbuf.at[3, down], bbuf.at[3, down], y_sems, 1, ym)
    from_ym = remote(bbuf.at[1, down], bbuf.at[1, down], y_sems, 0, yp)
    from_yp = remote(bbuf.at[3, up], bbuf.at[3, up], y_sems, 1, ym)
    a_copies = [[remote(at_ref.at[:, :, rows_of(dx, z_of[s])], abuf.at[s, dx], a_sems, s * 3 + dx - 1, device(dx))
                 for dx in (1, 3, 2)] for s in range(2)]

    pl.semaphore_wait(barrier, len(partners))
    from_xm.start()
    from_xp.start()
    for copy in a_copies[0] + a_copies[1]:
        copy.start()
    load_b.start()
    load_a[0].start()
    load_a[1].start()

    minus = jnp.where(lax.broadcasted_iota(jnp.int32, (64, KB), 1) < KH, 1.0, -1.0)

    def weigh(s):
        load_a[s].wait()
        for copy in a_copies[s]:
            copy.wait_recv()

        @pl.loop(0, XS)
        def _(slot):
            rows_t[...] = abuf[s, slot].reshape(KB, ROWS).T.astype(F32)
            lanes = pl.ds(pl.multiple_of(slot * KB, KB), KB)
            for side in range(2):
                which = core if side == 0 else 1 - core
                value = rows_t[pl.ds(pl.multiple_of(which * 64, 64), 64)]
                left[s, pl.ds(side * 128, 64), lanes] = (value * minus).astype(BF16)
                left[s, pl.ds(side * 128 + 64, 64), lanes] = pltpu.roll(value, KH, 1).astype(BF16)

    half_copies = {(s, chunk): remote(half_send.at[s, chunk], half_recv.at[s, chunk], half_sems, 2 * s + chunk, sibling)
                   for s, chunk in ((0, 0), (1, 0), (1, 1))}
    z_copies = [[remote(z_send.at[0, 0], z_recv.at[0, 0], z_sems, 0, zp)],
                [remote(z_send.at[i, 1], z_recv.at[i, 1], z_sems, 1 + i, (zp, zc)[i]) for i in range(2)]]

    def contract(s, chunk):
        where = pl.ds(chunk * CJ, CJ)
        right = jnp.concatenate([bbuf[slot, :, :, where].reshape(KB, CJ) for slot in range(XS)], axis=0)
        return jnp.dot(left[s], right, preferred_element_type=F32)

    def halve(s, chunk):
        total = contract(s, chunk)
        acc[s, chunk] = total[:128]
        half_send[s, chunk] = total[128:].astype(BF16)
        half_copies[s, chunk].start()

    from_xm.wait_recv()
    relay_p.start()
    to_yp.start()
    from_xp.wait_recv()
    relay_m.start()
    to_ym.start()
    load_s.start()
    weigh(0)
    load_b.wait()
    for copy in (relay_p, relay_m, from_ym, from_yp):
        copy.wait_recv()
    halve(0, 0)
    total = contract(0, 1)
    z_send[0, 1] = total[:128].astype(BF16)
    z_copies[1][0].start()
    z_send[1, 1] = total[128:].astype(BF16)
    z_copies[1][1].start()
    half_copies[0, 0].wait_recv()
    z_send[0, 0] = (acc[0, 0] + half_recv[0, 0].astype(F32)).astype(BF16)
    z_copies[0][0].start()
    weigh(1)
    halve(1, 1)
    halve(1, 0)
    for copy in [from_xm, from_xp, relay_p, relay_m, to_yp, to_ym] + a_copies[0] + a_copies[1] + list(half_copies.values()):
        copy.wait_send()

    def swap(v, tile_bit, lane_bit):
        step, width = 1 << tile_bit, 1 << lane_bit
        v = v.reshape(16 // (2 * step), 2, step, JLO, 128)
        a = v[:, 0].reshape(8, JLO, 128)
        b = v[:, 1].reshape(8, JLO, 128)
        low = (lax.broadcasted_iota(jnp.int32, a.shape, 2) // width) % 2 == 0
        a, b = (jnp.where(low, a, pltpu.roll(b, width, 2)), jnp.where(low, pltpu.roll(a, 128 - width, 2), b))
        shape = (16 // (2 * step), 1, step, JLO, 128)
        return jnp.concatenate([a.reshape(shape), b.reshape(shape)], axis=1).reshape(16, JLO, 128)

    load_s.wait()

    result = jnp.zeros((64, M), F32)
    for top in (1, 0):
        half_copies[1, top].wait_recv()
        for copy in z_copies[top]:
            copy.wait_recv()
        total = acc[1, top] + half_recv[1, top].astype(F32) + z_recv[0, top].astype(F32)
        if top == 1:
            total += z_recv[1, top].astype(F32)
        value = total.astype(BF16).T.reshape(16, JLO, 128)
        for tile_bit, lane_bit in ((0, 0), (1, 1), (2, 2), (3, 3), (3, 6), (2, 5)):
            value = swap(value, tile_bit, lane_bit)
        right = []
        for u in range(4):
            for p in range(2):
                at = pl.ds((u * 2 + p) * 128, 128)
                turned = pl.ds((u * 2 + 1 - p) * 128, 128)
                for rh in range(2):
                    block = value[p * 8 + rh * 4 + u]
                    lhs[top, pl.ds(rh * 16, 16), at] = block if p == 0 else -block
                    lhs[top, pl.ds(32 + rh * 16, 16), turned] = block
                for t in range(8):
                    rl = (t % 2) * 16 + (t // 4) * 8 + (t // 2 % 2) * 4 + u
                    right.append(s_vmem[p, pl.ds(rl * JHI + top * 16, 16)])
        result += jnp.dot(lhs[top], jnp.concatenate(right, axis=0), preferred_element_type=F32)
    out_ref[...] = result.astype(BF16).reshape(2, 2, JLO, M)

    for copy in z_copies[0] + z_copies[1]:
        copy.wait_send()


def on_device(amplitudes, first_factor, second_factor):
    arguments = [pltpu.with_memory_space_constraint(a, pltpu.HBM)
                 for a in (jnp.swapaxes(amplitudes, 1, 2), first_factor, second_factor)]
    return pl.pallas_call(
        kernel,
        out_shape=pltpu.VMEM((2, 2, JLO, M), BF16),
        in_specs=[pl.BlockSpec(memory_space=pltpu.HBM)] * 3,
        out_specs=pl.BlockSpec(memory_space=pltpu.VMEM),
        scratch_shapes=[
            pltpu.VMEM((2, G2, M), BF16),
            pltpu.VMEM((2, XS, 2, KH, ROWS), BF16),
            pltpu.VMEM((XS, 2, KH, J), BF16),
            pltpu.VMEM((ROWS, KB), F32),
            pltpu.VMEM((2, 256, XS * KB), BF16),
            pltpu.VMEM((2, CHUNKS, 128, CJ), F32),
            pltpu.VMEM((2, CHUNKS, 128, CJ), BF16),
            pltpu.VMEM((2, CHUNKS, 128, CJ), BF16),
            pltpu.VMEM((2, CHUNKS, 128, CJ), BF16),
            pltpu.VMEM((2, CHUNKS, 128, CJ), BF16),
            pltpu.VMEM((2, 64, G2), BF16),
            pltpu.SemaphoreType.DMA((4,)),
            pltpu.SemaphoreType.DMA((2, 6)),
            pltpu.SemaphoreType.DMA((2, 4)),
            pltpu.SemaphoreType.DMA((2, 2)),
            pltpu.SemaphoreType.DMA((2, 2 * CHUNKS)),
            pltpu.SemaphoreType.DMA((2, 3)),
        ],
        compiler_params=pltpu.CompilerParams(
            collective_id=0, has_side_effects=True, vmem_limit_bytes=32 * 1024 * 1024),
        cost_estimate=pl.CostEstimate(flops=800_000_000, bytes_accessed=2_600_000, transcendentals=0),
    )(*arguments)


def solution(mesh):
    return jax.shard_map(
        on_device, mesh=mesh,
        in_specs=(P(None, "grid", "depth"), P(None, "depth", None), P()),
        out_specs=P(None, ("grid", "depth"), None, None), check_vma=False)
```

```python
import jax
import jax.numpy as jnp
from jax import lax
from jax.experimental import pallas as pl
from jax.experimental.pallas import tpu as pltpu
from jax.sharding import PartitionSpec as P

MESH = pl.DeviceIdType.MESH
XS = 4
YS = 8
JHI = 32
RLO = 32
JLO = 16
J = JHI * JLO
G2 = RLO * JHI
M = 512
KH = 64
KB = 128
ROWS = 128
CHUNKS = 2
CJ = J // CHUNKS
F32 = jnp.float32
BF16 = jnp.bfloat16


def kernel(at_ref, ff_ref, sf_ref, out_ref,
           s_vmem, abuf, bbuf, rows_t, left, acc, half_send, half_recv, z_send, z_recv, lhs,
           local_sem, a_sems, x_sems, y_sems, half_sems, z_sems):
    grid = lax.axis_index("grid")
    depth = lax.axis_index("depth")
    x = depth // 4
    zl = (depth // 2) % 2
    core = depth % 2
    zh = grid // YS
    y = grid % YS

    def device(dx):
        return grid, (lax.rem(x + dx, XS) * 2 + zl) * 2 + (core if dx % 2 == 0 else 1 - core)

    xp, xm, x2 = device(1), device(3), device(2)
    yp = (zh * YS + lax.rem(y + 1, YS), depth)
    ym = (zh * YS + lax.rem(y + YS - 1, YS), depth)
    zp = (grid, (x * 2 + 1 - zl) * 2 + core)
    zc = (grid, (x * 2 + 1 - zl) * 2 + 1 - core)
    sibling = (grid, (x * 2 + zl) * 2 + 1 - core)
    partners = (xp, xm, yp, ym, x2, zp, zc, sibling)

    barrier = pltpu.get_barrier_semaphore()
    for partner in partners:
        pl.semaphore_signal(barrier, inc=1, device_id=partner, device_id_type=MESH)

    def rows_of(dx, z):
        return pl.ds(pl.multiple_of((lax.rem(x + dx, XS) * 2 + z) * ROWS, ROWS), ROWS)

    z_of = (1 - zl, zl)
    load_b = pltpu.make_async_copy(ff_ref, bbuf.at[0], local_sem.at[0])
    load_a = [pltpu.make_async_copy(at_ref.at[:, :, rows_of(0, z_of[s])], abuf.at[s, 0], local_sem.at[1 + s])
              for s in range(2)]
    load_s = pltpu.make_async_copy(sf_ref, s_vmem, local_sem.at[3])

    def remote(src, dst, sems, i, to):
        return pltpu.make_async_remote_copy(
            src_ref=src, dst_ref=dst, send_sem=sems.at[0, i], recv_sem=sems.at[1, i],
            device_id=to, device_id_type=MESH)

    up = y % 2
    down = 1 - up
    from_xm = remote(ff_ref.at[up], bbuf.at[1, up], x_sems, 0, xp)
    from_xp = remote(ff_ref.at[down], bbuf.at[3, down], x_sems, 1, xm)
    relay_p = remote(bbuf.at[1, up], bbuf.at[2, up], x_sems, 2, xp)
    relay_m = remote(bbuf.at[3, down], bbuf.at[2, down], x_sems, 3, xm)
    to_yp = remote(bbuf.at[1, up], bbuf.at[1, up], y_sems, 0, yp)
    to_ym = remote(bbuf.at[3, down], bbuf.at[3, down], y_sems, 1, ym)
    from_ym = remote(bbuf.at[1, down], bbuf.at[1, down], y_sems, 0, yp)
    from_yp = remote(bbuf.at[3, up], bbuf.at[3, up], y_sems, 1, ym)
    a_copies = [[remote(at_ref.at[:, :, rows_of(dx, z_of[s])], abuf.at[s, dx], a_sems, s * 3 + dx - 1, device(dx))
                 for dx in (1, 3, 2)] for s in range(2)]

    pl.semaphore_wait(barrier, len(partners))
    from_xm.start()
    from_xp.start()
    for copy in a_copies[0]:
        copy.start()
    load_b.start()
    load_a[0].start()
    load_a[1].start()

    minus = jnp.where(lax.broadcasted_iota(jnp.int32, (64, KB), 1) < KH, 1.0, -1.0)

    def weigh(s):
        load_a[s].wait()
        for copy in a_copies[s]:
            copy.wait_recv()

        @pl.loop(0, XS)
        def _(slot):
            rows_t[...] = abuf[s, slot].reshape(KB, ROWS).T.astype(F32)
            lanes = pl.ds(pl.multiple_of(slot * KB, KB), KB)
            for side in range(2):
                which = core if side == 0 else 1 - core
                value = rows_t[pl.ds(pl.multiple_of(which * 64, 64), 64)]
                left[s, pl.ds(side * 128, 64), lanes] = (value * minus).astype(BF16)
                left[s, pl.ds(side * 128 + 64, 64), lanes] = pltpu.roll(value, KH, 1).astype(BF16)

    half_copies = {(s, chunk): remote(half_send.at[s, chunk], half_recv.at[s, chunk], half_sems, 2 * s + chunk, sibling)
                   for s, chunk in ((0, 0), (1, 0), (1, 1))}
    z_copies = [[remote(z_send.at[0, 0], z_recv.at[0, 0], z_sems, 0, zp)],
                [remote(z_send.at[i, 1], z_recv.at[i, 1], z_sems, 1 + i, (zp, zc)[i]) for i in range(2)]]

    def contract(s, chunk):
        where = pl.ds(chunk * CJ, CJ)
        right = jnp.concatenate([bbuf[slot, :, :, where].reshape(KB, CJ) for slot in range(XS)], axis=0)
        return jnp.dot(left[s], right, preferred_element_type=F32)

    def halve(s, chunk):
        total = contract(s, chunk)
        acc[s, chunk] = total[:128]
        half_send[s, chunk] = total[128:].astype(BF16)
        half_copies[s, chunk].start()

    from_xm.wait_recv()
    relay_p.start()
    to_yp.start()
    from_xp.wait_recv()
    relay_m.start()
    to_ym.start()
    for copy in a_copies[1]:
        copy.start()
    weigh(0)
    load_b.wait()
    for copy in (relay_p, relay_m, from_ym, from_yp):
        copy.wait_recv()
    halve(0, 0)
    total = contract(0, 1)
    z_send[0, 1] = total[:128].astype(BF16)
    z_copies[1][0].start()
    z_send[1, 1] = total[128:].astype(BF16)
    z_copies[1][1].start()
    half_copies[0, 0].wait_recv()
    z_send[0, 0] = (acc[0, 0] + half_recv[0, 0].astype(F32)).astype(BF16)
    z_copies[0][0].start()
    load_s.start()
    weigh(1)
    halve(1, 1)
    halve(1, 0)
    for copy in [from_xm, from_xp, relay_p, relay_m, to_yp, to_ym] + a_copies[0] + a_copies[1] + list(half_copies.values()):
        copy.wait_send()

    def swap(v, tile_bit, lane_bit):
        step, width = 1 << tile_bit, 1 << lane_bit
        v = v.reshape(16 // (2 * step), 2, step, JLO, 128)
        a = v[:, 0].reshape(8, JLO, 128)
        b = v[:, 1].reshape(8, JLO, 128)
        low = (lax.broadcasted_iota(jnp.int32, a.shape, 2) // width) % 2 == 0
        a, b = (jnp.where(low, a, pltpu.roll(b, width, 2)), jnp.where(low, pltpu.roll(a, 128 - width, 2), b))
        shape = (16 // (2 * step), 1, step, JLO, 128)
        return jnp.concatenate([a.reshape(shape), b.reshape(shape)], axis=1).reshape(16, JLO, 128)

    load_s.wait()

    result = jnp.zeros((64, M), F32)
    for top in (1, 0):
        half_copies[1, top].wait_recv()
        for copy in z_copies[top]:
            copy.wait_recv()
        total = acc[1, top] + half_recv[1, top].astype(F32) + z_recv[0, top].astype(F32)
        if top == 1:
            total += z_recv[1, top].astype(F32)
        value = total.astype(BF16).T.reshape(16, JLO, 128)
        for tile_bit, lane_bit in ((0, 0), (1, 1), (2, 2), (3, 3), (3, 6), (2, 5)):
            value = swap(value, tile_bit, lane_bit)
        right = []
        for u in range(4):
            for p in range(2):
                at = pl.ds((u * 2 + p) * 128, 128)
                turned = pl.ds((u * 2 + 1 - p) * 128, 128)
                for rh in range(2):
                    block = value[p * 8 + rh * 4 + u]
                    lhs[top, pl.ds(rh * 16, 16), at] = block if p == 0 else -block
                    lhs[top, pl.ds(32 + rh * 16, 16), turned] = block
                for t in range(8):
                    rl = (t % 2) * 16 + (t // 4) * 8 + (t // 2 % 2) * 4 + u
                    right.append(s_vmem[p, pl.ds(rl * JHI + top * 16, 16)])
        result += jnp.dot(lhs[top], jnp.concatenate(right, axis=0), preferred_element_type=F32)
    out_ref[...] = result.astype(BF16).reshape(2, 2, JLO, M)

    for copy in z_copies[0] + z_copies[1]:
        copy.wait_send()


def on_device(amplitudes, first_factor, second_factor):
    arguments = [pltpu.with_memory_space_constraint(a, pltpu.HBM)
                 for a in (jnp.swapaxes(amplitudes, 1, 2), first_factor, second_factor)]
    return pl.pallas_call(
        kernel,
        out_shape=pltpu.VMEM((2, 2, JLO, M), BF16),
        in_specs=[pl.BlockSpec(memory_space=pltpu.HBM)] * 3,
        out_specs=pl.BlockSpec(memory_space=pltpu.VMEM),
        scratch_shapes=[
            pltpu.VMEM((2, G2, M), BF16),
            pltpu.VMEM((2, XS, 2, KH, ROWS), BF16),
            pltpu.VMEM((XS, 2, KH, J), BF16),
            pltpu.VMEM((ROWS, KB), F32),
            pltpu.VMEM((2, 256, XS * KB), BF16),
            pltpu.VMEM((2, CHUNKS, 128, CJ), F32),
            pltpu.VMEM((2, CHUNKS, 128, CJ), BF16),
            pltpu.VMEM((2, CHUNKS, 128, CJ), BF16),
            pltpu.VMEM((2, CHUNKS, 128, CJ), BF16),
            pltpu.VMEM((2, CHUNKS, 128, CJ), BF16),
            pltpu.VMEM((2, 64, G2), BF16),
            pltpu.SemaphoreType.DMA((4,)),
            pltpu.SemaphoreType.DMA((2, 6)),
            pltpu.SemaphoreType.DMA((2, 4)),
            pltpu.SemaphoreType.DMA((2, 2)),
            pltpu.SemaphoreType.DMA((2, 2 * CHUNKS)),
            pltpu.SemaphoreType.DMA((2, 3)),
        ],
        compiler_params=pltpu.CompilerParams(
            collective_id=0, has_side_effects=True, vmem_limit_bytes=32 * 1024 * 1024),
        cost_estimate=pl.CostEstimate(flops=800_000_000, bytes_accessed=2_600_000, transcendentals=0),
    )(*arguments)


def solution(mesh):
    return jax.shard_map(
        on_device, mesh=mesh,
        in_specs=(P(None, "grid", "depth"), P(None, "depth", None), P()),
        out_specs=P(None, ("grid", "depth"), None, None), check_vma=False)
```

```python
import jax
import jax.numpy as jnp
from jax import lax
from jax.experimental import pallas as pl
from jax.experimental.pallas import tpu as pltpu
from jax.sharding import PartitionSpec as P

MESH = pl.DeviceIdType.MESH
XS = 4
JHI = 32
RLO = 32
JLO = 16
J = JHI * JLO
G2 = RLO * JHI
M = 512
KH = 64
KB = 128
ROWS = 128
CHUNKS = 2
CJ = J // CHUNKS
F32 = jnp.float32
BF16 = jnp.bfloat16


def kernel(at_ref, ff_ref, sf_ref, out_ref,
           s_vmem, abuf, bbuf, left, own_send, own_part, z_send, z_recv, lhs,
           local_sem, ready, b_send, b_recv, a_send, a_recv, r_sems, own_sems, z_out, z_in):
    grid = lax.axis_index("grid")
    depth = lax.axis_index("depth")
    x = depth // 4
    zl = (depth // 2) % 2
    core = depth % 2

    def device(dx, which):
        return grid, (lax.rem(x + dx, XS) * 2 + zl) * 2 + which

    def z_device(which):
        return grid, (x * 2 + 1 - zl) * 2 + which

    def rows_of(dx, z):
        return pl.ds(pl.multiple_of((lax.rem(x + dx, XS) * 2 + z) * ROWS, ROWS), ROWS)

    def remote(src, dst, send, recv, to):
        return pltpu.make_async_remote_copy(
            src_ref=src, dst_ref=dst, send_sem=send, recv_sem=recv, device_id=to, device_id_type=MESH)

    z_of = (1 - zl, zl)
    load_s = pltpu.make_async_copy(sf_ref, s_vmem, local_sem.at[3])
    barrier = pltpu.get_barrier_semaphore()

    def b_copy(c, dx, p):
        i = (0 if dx == 1 else 2) + p
        return remote(ff_ref.at[p], bbuf.at[c, dx, p], b_send.at[i], b_recv.at[c * 4 + i], device(dx, 1))

    def a_copy(c, s, dx):
        i = s * 3 + dx - 1
        return remote(at_ref.at[:, :, rows_of(dx, z_of[s])], abuf.at[s, c, dx], a_send.at[i], a_recv.at[c * 6 + i], device(dx, 1))

    b_own = remote(ff_ref, bbuf.at[0, 0], b_send.at[4], b_recv.at[8], device(0, 1))
    a_own = [remote(at_ref.at[:, :, rows_of(0, z_of[s])], abuf.at[s, 0, 0], a_send.at[6 + s], a_recv.at[12 + s], device(0, 1))
             for s in range(2)]
    own_copies = [remote(own_send.at[h], own_part.at[h], own_sems.at[0, h], own_sems.at[1, h], device(0, 0)) for h in range(2)]
    z_copies = [[remote(z_send.at[c, h], z_recv.at[h], z_out.at[2 * h + c], z_in.at[h], z_device(c)) for c in range(2)]
                for h in range(2)]

    @pl.when(core == 0)
    def _():
        pl.semaphore_wait(barrier, 5)
        for dx, p in ((1, 0), (3, 1)):
            b_copy(0, dx, p).start()
        for dx in (1, 3, 2):
            a_copy(0, 0, dx).start()
        b_own.start()
        for dx, p in ((1, 1), (3, 0)):
            b_copy(0, dx, p).start()
        a_own[0].start()
        for dx in (1, 3, 2):
            a_copy(0, 1, dx).start()
        a_own[1].start()
        for to in (device(0, 1), z_device(1)):
            pl.semaphore_signal(ready, inc=1, device_id=to, device_id_type=MESH)
        load_s.start()
        for dx in (1, 3):
            for p in range(2):
                b_copy(0, dx, p).wait_send()
        for s in range(2):
            for dx in (1, 3, 2):
                a_copy(0, s, dx).wait_send()
            a_own[s].wait_send()
        b_own.wait_send()

    minus = jnp.where(lax.broadcasted_iota(jnp.int32, (64, KB), 1) < KH, 1.0, -1.0)

    def weigh(s, c, slot):
        turned = abuf[s, c, slot].reshape(KB, ROWS).T.astype(F32)
        lanes = pl.ds((c * XS + slot) * KB, KB)
        for side in range(2):
            value = turned[side * 64:(side + 1) * 64]
            left[s, pl.ds(side * 128, 64), lanes] = (value * minus).astype(BF16)
            left[s, pl.ds(side * 128 + 64, 64), lanes] = pltpu.roll(value, KH, 1).astype(BF16)

    def contract(s, h):
        where = pl.ds(h * CJ, CJ)
        right = jnp.concatenate([bbuf[c, slot, :, :, where].reshape(KB, CJ) for c in range(2) for slot in range(XS)], axis=0)
        return jnp.dot(left[s], right, preferred_element_type=F32)

    @pl.when(core == 1)
    def _():
        for to in [device(dx, 1) for dx in (1, 3, 2)] + [z_device(1)]:
            pl.semaphore_signal(barrier, inc=1, device_id=to, device_id_type=MESH)
        for to in [device(dx, 0) for dx in range(XS)] + [z_device(0)]:
            pl.semaphore_signal(barrier, inc=1, device_id=to, device_id_type=MESH)
        load_b = pltpu.make_async_copy(ff_ref, bbuf.at[1, 0], local_sem.at[0])
        load_a = [pltpu.make_async_copy(at_ref.at[:, :, rows_of(0, z_of[s])], abuf.at[s, 1, 0], local_sem.at[1 + s])
                  for s in range(2)]
        relays = [(remote(bbuf.at[c, 1, 0], bbuf.at[c, 2, 0], r_sems.at[0, 2 * c], r_sems.at[1, 2 * c], device(1, 1)),
                   remote(bbuf.at[c, 3, 1], bbuf.at[c, 2, 1], r_sems.at[0, 2 * c + 1], r_sems.at[1, 2 * c + 1], device(3, 1)))
                  for c in range(2)]

        pl.semaphore_wait(barrier, 4)
        for dx, p in ((1, 0), (3, 1)):
            b_copy(1, dx, p).start()
        for dx in (1, 3, 2):
            a_copy(1, 0, dx).start()
        for dx, p in ((1, 1), (3, 0)):
            b_copy(1, dx, p).start()
        load_b.start()
        load_a[0].start()
        load_a[1].start()
        for c in (1, 0):
            b_copy(c, 1, 0).wait_recv()
            relays[c][0].start()
            b_copy(c, 3, 1).wait_recv()
            relays[c][1].start()
        for dx in (1, 3, 2):
            a_copy(1, 1, dx).start()
        load_s.start()
        load_a[0].wait()
        weigh(0, 1, 0)
        for c in (1, 0):
            for dx in (1, 3, 2):
                a_copy(c, 0, dx).wait_recv()
                weigh(0, c, dx)
        a_own[0].wait_recv()
        weigh(0, 0, 0)
        load_b.wait()
        b_own.wait_recv()
        for c in (1, 0):
            b_copy(c, 1, 1).wait_recv()
            b_copy(c, 3, 0).wait_recv()
        for c in (1, 0):
            relays[c][0].wait_recv()
            relays[c][1].wait_recv()
        pl.semaphore_wait(ready, 2)
        for h in range(2):
            total = contract(0, h)
            for c in range(2):
                z_send[c, h] = total[c * 128:(c + 1) * 128].astype(BF16)
                z_copies[h][c].start()
        load_a[1].wait()
        weigh(1, 1, 0)
        for c in (1, 0):
            for dx in (1, 3, 2):
                a_copy(c, 1, dx).wait_recv()
                weigh(1, c, dx)
        a_own[1].wait_recv()
        weigh(1, 0, 0)
        for h in range(2):
            total = contract(1, h)
            own_send[h] = total[:128].astype(BF16)
            own_copies[h].start()
            own_part[h] = total[128:].astype(BF16)
        for dx in (1, 3):
            for p in range(2):
                b_copy(1, dx, p).wait_send()
        for s in range(2):
            for dx in (1, 3, 2):
                a_copy(1, s, dx).wait_send()
        for c in range(2):
            relays[c][0].wait_send()
            relays[c][1].wait_send()

    def swap(v, tile_bit, lane_bit):
        step, width = 1 << tile_bit, 1 << lane_bit
        v = v.reshape(16 // (2 * step), 2, step, JLO, 128)
        a = v[:, 0].reshape(8, JLO, 128)
        b = v[:, 1].reshape(8, JLO, 128)
        low = (lax.broadcasted_iota(jnp.int32, a.shape, 2) // width) % 2 == 0
        a, b = (jnp.where(low, a, pltpu.roll(b, width, 2)), jnp.where(low, pltpu.roll(a, 128 - width, 2), b))
        shape = (16 // (2 * step), 1, step, JLO, 128)
        return jnp.concatenate([a.reshape(shape), b.reshape(shape)], axis=1).reshape(16, JLO, 128)

    load_s.wait()

    result = jnp.zeros((64, M), F32)
    for top in range(2):
        @pl.when(core == 0)
        def _(top=top):
            own_copies[top].wait_recv()

        z_copies[top][0].wait_recv()
        total = own_part[top].astype(F32) + z_recv[top].astype(F32)
        value = total.astype(BF16).T.reshape(16, JLO, 128)
        for tile_bit, lane_bit in ((0, 0), (1, 1), (2, 2), (3, 3), (3, 6), (2, 5)):
            value = swap(value, tile_bit, lane_bit)
        right = []
        for u in range(4):
            for p in range(2):
                at = pl.ds((u * 2 + p) * 128, 128)
                turned = pl.ds((u * 2 + 1 - p) * 128, 128)
                for rh in range(2):
                    block = value[p * 8 + rh * 4 + u]
                    lhs[top, pl.ds(rh * 16, 16), at] = block if p == 0 else -block
                    lhs[top, pl.ds(32 + rh * 16, 16), turned] = block
                for t in range(8):
                    rl = (t % 2) * 16 + (t // 4) * 8 + (t // 2 % 2) * 4 + u
                    right.append(s_vmem[p, pl.ds(rl * JHI + top * 16, 16)])
        result += jnp.dot(lhs[top], jnp.concatenate(right, axis=0), preferred_element_type=F32)
    out_ref[...] = result.astype(BF16).reshape(2, 2, JLO, M)

    @pl.when(core == 1)
    def _():
        for copy in own_copies + z_copies[0] + z_copies[1]:
            copy.wait_send()


def on_device(amplitudes, first_factor, second_factor):
    arguments = [pltpu.with_memory_space_constraint(a, pltpu.HBM)
                 for a in (jnp.swapaxes(amplitudes, 1, 2), first_factor, second_factor)]
    return pl.pallas_call(
        kernel,
        out_shape=pltpu.VMEM((2, 2, JLO, M), BF16),
        in_specs=[pl.BlockSpec(memory_space=pltpu.HBM)] * 3,
        out_specs=pl.BlockSpec(memory_space=pltpu.VMEM),
        scratch_shapes=[
            pltpu.VMEM((2, G2, M), BF16),
            pltpu.VMEM((2, 2, XS, 2, KH, ROWS), BF16),
            pltpu.VMEM((2, XS, 2, KH, J), BF16),
            pltpu.VMEM((2, 256, 2 * XS * KB), BF16),
            pltpu.VMEM((CHUNKS, 128, CJ), BF16),
            pltpu.VMEM((CHUNKS, 128, CJ), BF16),
            pltpu.VMEM((2, CHUNKS, 128, CJ), BF16),
            pltpu.VMEM((CHUNKS, 128, CJ), BF16),
            pltpu.VMEM((2, 64, G2), BF16),
            pltpu.SemaphoreType.DMA((4,)),
            pltpu.SemaphoreType.REGULAR,
            pltpu.SemaphoreType.DMA((5,)),
            pltpu.SemaphoreType.DMA((9,)),
            pltpu.SemaphoreType.DMA((8,)),
            pltpu.SemaphoreType.DMA((14,)),
            pltpu.SemaphoreType.DMA((2, 4)),
            pltpu.SemaphoreType.DMA((2, 2)),
            pltpu.SemaphoreType.DMA((4,)),
            pltpu.SemaphoreType.DMA((2,)),
        ],
        compiler_params=pltpu.CompilerParams(
            collective_id=0, has_side_effects=True, vmem_limit_bytes=32 * 1024 * 1024),
        cost_estimate=pl.CostEstimate(flops=800_000_000, bytes_accessed=2_600_000, transcendentals=0),
    )(*arguments)


def solution(mesh):
    return jax.shard_map(
        on_device, mesh=mesh,
        in_specs=(P(None, "grid", "depth"), P(None, "depth", None), P()),
        out_specs=P(None, ("grid", "depth"), None, None), check_vma=False)
```

```python
import jax
import jax.numpy as jnp
from jax import lax
from jax.experimental import pallas as pl
from jax.experimental.pallas import tpu as pltpu
from jax.sharding import PartitionSpec as P

MESH = pl.DeviceIdType.MESH
XS = 4
JHI = 32
RLO = 32
JLO = 16
J = JHI * JLO
G2 = RLO * JHI
M = 512
KH = 64
KB = 128
ROWS = 128
CHUNKS = 2
CJ = J // CHUNKS
F32 = jnp.float32
BF16 = jnp.bfloat16


def kernel(at_ref, ff_ref, sf_ref, out_ref,
           s_vmem, abuf, bbuf, left, acc, own_send, own_part, z_send, z_recv, lhs,
           local_sem, ready, b_send, b_recv, a_send, a_recv, r_sems, own_sems, z_out, z_in):
    grid = lax.axis_index("grid")
    depth = lax.axis_index("depth")
    x = depth // 4
    zl = (depth // 2) % 2
    core = depth % 2

    def device(dx, which):
        return grid, (lax.rem(x + dx, XS) * 2 + zl) * 2 + which

    def z_device(which):
        return grid, (x * 2 + 1 - zl) * 2 + which

    def rows_of(dx, z):
        return pl.ds(pl.multiple_of((lax.rem(x + dx, XS) * 2 + z) * ROWS, ROWS), ROWS)

    def remote(src, dst, send, recv, to):
        return pltpu.make_async_remote_copy(
            src_ref=src, dst_ref=dst, send_sem=send, recv_sem=recv, device_id=to, device_id_type=MESH)

    z_of = (1 - zl, zl)
    load_s = pltpu.make_async_copy(sf_ref, s_vmem, local_sem.at[3])
    barrier = pltpu.get_barrier_semaphore()

    def b_copy(c, dx, p):
        i = (0 if dx == 1 else 2) + p
        return remote(ff_ref.at[p], bbuf.at[c, dx, p], b_send.at[i], b_recv.at[c * 4 + i], device(dx, 1))

    def a_copy(c, s, dx):
        i = s * 3 + dx - 1
        return remote(at_ref.at[:, :, rows_of(dx, z_of[s])], abuf.at[s, c, dx], a_send.at[i], a_recv.at[c * 6 + i], device(dx, 1))

    b_own = remote(ff_ref, bbuf.at[0, 0], b_send.at[4], b_recv.at[8], device(0, 1))
    a_own = [remote(at_ref.at[:, :, rows_of(0, z_of[s])], abuf.at[s, 0, 0], a_send.at[6 + s], a_recv.at[12 + s], device(0, 1))
             for s in range(2)]
    own_copies = [remote(own_send.at[h], own_part.at[h], own_sems.at[0, h], own_sems.at[1, h], device(0, 0)) for h in range(2)]
    z_copies = [[remote(z_send.at[c, h], z_recv.at[h], z_out.at[2 * h + c], z_in.at[h], z_device(c)) for c in range(2)]
                for h in range(2)]

    @pl.when(core == 0)
    def _():
        pl.semaphore_wait(barrier, 5)
        for dx, p in ((1, 0), (3, 1)):
            b_copy(0, dx, p).start()
        for dx in (1, 3, 2):
            a_copy(0, 0, dx).start()
        b_own.start()
        for dx, p in ((1, 1), (3, 0)):
            b_copy(0, dx, p).start()
        a_own[0].start()
        for dx in (1, 3, 2):
            a_copy(0, 1, dx).start()
        a_own[1].start()
        for to in (device(0, 1), z_device(1)):
            pl.semaphore_signal(ready, inc=1, device_id=to, device_id_type=MESH)
        load_s.start()
        for dx in (1, 3):
            for p in range(2):
                b_copy(0, dx, p).wait_send()
        for s in range(2):
            for dx in (1, 3, 2):
                a_copy(0, s, dx).wait_send()
            a_own[s].wait_send()
        b_own.wait_send()

    minus = jnp.where(lax.broadcasted_iota(jnp.int32, (64, KB), 1) < KH, 1.0, -1.0).astype(BF16)

    order = [(c, slot) for slot in (0, 1, 3, 2) for c in range(2)]

    def weigh(s, c, slot):
        turned = abuf[s, c, slot].reshape(KB, ROWS).T
        lanes = pl.ds(order.index((c, slot)) * KB, KB)
        for side in range(2):
            value = turned[side * 64:(side + 1) * 64]
            left[s, pl.ds(side * 128, 64), lanes] = value * minus
            left[s, pl.ds(side * 128 + 64, 64), lanes] = pltpu.roll(value, KH, 1)

    def contract(s, h, first, last):
        where = pl.ds(h * CJ, CJ)
        right = jnp.concatenate([bbuf[c, slot, :, :, where].reshape(KB, CJ) for c, slot in order[first:last]], axis=0)
        return jnp.dot(left[s, :, pl.ds(first * KB, (last - first) * KB)], right, preferred_element_type=F32)

    @pl.when(core == 1)
    def _():
        for to in [device(dx, 1) for dx in (1, 3, 2)] + [z_device(1)]:
            pl.semaphore_signal(barrier, inc=1, device_id=to, device_id_type=MESH)
        for to in [device(dx, 0) for dx in range(XS)] + [z_device(0)]:
            pl.semaphore_signal(barrier, inc=1, device_id=to, device_id_type=MESH)
        load_b = pltpu.make_async_copy(ff_ref, bbuf.at[1, 0], local_sem.at[0])
        load_a = [pltpu.make_async_copy(at_ref.at[:, :, rows_of(0, z_of[s])], abuf.at[s, 1, 0], local_sem.at[1 + s])
                  for s in range(2)]
        relays = [(remote(bbuf.at[c, 1, 0], bbuf.at[c, 2, 0], r_sems.at[0, 2 * c], r_sems.at[1, 2 * c], device(1, 1)),
                   remote(bbuf.at[c, 3, 1], bbuf.at[c, 2, 1], r_sems.at[0, 2 * c + 1], r_sems.at[1, 2 * c + 1], device(3, 1)))
                  for c in range(2)]

        pl.semaphore_wait(barrier, 4)
        for dx, p in ((1, 0), (3, 1)):
            b_copy(1, dx, p).start()
        for dx in (1, 3, 2):
            a_copy(1, 0, dx).start()
        for dx, p in ((1, 1), (3, 0)):
            b_copy(1, dx, p).start()
        load_b.start()
        load_a[0].start()
        load_a[1].start()
        for c in (1, 0):
            b_copy(c, 1, 0).wait_recv()
            relays[c][0].start()
            b_copy(c, 3, 1).wait_recv()
            relays[c][1].start()
        for dx in (1, 3, 2):
            a_copy(1, 1, dx).start()
        load_s.start()
        load_a[0].wait()
        weigh(0, 1, 0)
        for c in (1, 0):
            for dx in (1, 3):
                a_copy(c, 0, dx).wait_recv()
                weigh(0, c, dx)
        a_own[0].wait_recv()
        weigh(0, 0, 0)
        load_b.wait()
        b_own.wait_recv()
        for c in (1, 0):
            b_copy(c, 1, 1).wait_recv()
            b_copy(c, 3, 0).wait_recv()
        for h in range(2):
            acc[h] = contract(0, h, 0, 6)
        for c in (1, 0):
            a_copy(c, 0, 2).wait_recv()
            weigh(0, c, 2)
        for c in (1, 0):
            relays[c][0].wait_recv()
            relays[c][1].wait_recv()
        pl.semaphore_wait(ready, 2)
        for h in range(2):
            total = acc[h] + contract(0, h, 6, 8)
            for c in range(2):
                z_send[c, h] = total[c * 128:(c + 1) * 128].astype(BF16)
                z_copies[h][c].start()
        load_a[1].wait()
        weigh(1, 1, 0)
        for c in (1, 0):
            for dx in (1, 3, 2):
                a_copy(c, 1, dx).wait_recv()
                weigh(1, c, dx)
        a_own[1].wait_recv()
        weigh(1, 0, 0)
        for h in range(2):
            total = contract(1, h, 0, 8)
            own_send[h] = total[:128].astype(BF16)
            own_copies[h].start()
            own_part[h] = total[128:].astype(BF16)
        for dx in (1, 3):
            for p in range(2):
                b_copy(1, dx, p).wait_send()
        for s in range(2):
            for dx in (1, 3, 2):
                a_copy(1, s, dx).wait_send()
        for c in range(2):
            relays[c][0].wait_send()
            relays[c][1].wait_send()

    def swap(v, tile_bit, lane_bit):
        step, width = 1 << tile_bit, 1 << lane_bit
        v = v.reshape(16 // (2 * step), 2, step, JLO, 128)
        a = v[:, 0].reshape(8, JLO, 128)
        b = v[:, 1].reshape(8, JLO, 128)
        low = (lax.broadcasted_iota(jnp.int32, a.shape, 2) // width) % 2 == 0
        a, b = (jnp.where(low, a, pltpu.roll(b, width, 2)), jnp.where(low, pltpu.roll(a, 128 - width, 2), b))
        shape = (16 // (2 * step), 1, step, JLO, 128)
        return jnp.concatenate([a.reshape(shape), b.reshape(shape)], axis=1).reshape(16, JLO, 128)

    load_s.wait()

    result = jnp.zeros((64, M), F32)
    for top in range(2):
        @pl.when(core == 0)
        def _(top=top):
            own_copies[top].wait_recv()

        z_copies[top][0].wait_recv()
        total = own_part[top].astype(F32) + z_recv[top].astype(F32)
        value = total.astype(BF16).T.reshape(16, JLO, 128)
        for tile_bit, lane_bit in ((0, 0), (1, 1), (2, 2), (3, 3), (3, 6), (2, 5)):
            value = swap(value, tile_bit, lane_bit)
        right = []
        for u in range(4):
            for p in range(2):
                at = pl.ds((u * 2 + p) * 128, 128)
                turned = pl.ds((u * 2 + 1 - p) * 128, 128)
                for rh in range(2):
                    block = value[p * 8 + rh * 4 + u]
                    lhs[top, pl.ds(rh * 16, 16), at] = block if p == 0 else -block
                    lhs[top, pl.ds(32 + rh * 16, 16), turned] = block
                for t in range(8):
                    rl = (t % 2) * 16 + (t // 4) * 8 + (t // 2 % 2) * 4 + u
                    right.append(s_vmem[p, pl.ds(rl * JHI + top * 16, 16)])
        result += jnp.dot(lhs[top], jnp.concatenate(right, axis=0), preferred_element_type=F32)
    out_ref[...] = result.astype(BF16).reshape(2, 2, JLO, M)

    @pl.when(core == 1)
    def _():
        for copy in own_copies + z_copies[0] + z_copies[1]:
            copy.wait_send()


def on_device(amplitudes, first_factor, second_factor):
    arguments = [pltpu.with_memory_space_constraint(a, pltpu.HBM)
                 for a in (jnp.swapaxes(amplitudes, 1, 2), first_factor, second_factor)]
    return pl.pallas_call(
        kernel,
        out_shape=pltpu.VMEM((2, 2, JLO, M), BF16),
        in_specs=[pl.BlockSpec(memory_space=pltpu.HBM)] * 3,
        out_specs=pl.BlockSpec(memory_space=pltpu.VMEM),
        scratch_shapes=[
            pltpu.VMEM((2, G2, M), BF16),
            pltpu.VMEM((2, 2, XS, 2, KH, ROWS), BF16),
            pltpu.VMEM((2, XS, 2, KH, J), BF16),
            pltpu.VMEM((2, 256, 2 * XS * KB), BF16),
            pltpu.VMEM((CHUNKS, 256, CJ), F32),
            pltpu.VMEM((CHUNKS, 128, CJ), BF16),
            pltpu.VMEM((CHUNKS, 128, CJ), BF16),
            pltpu.VMEM((2, CHUNKS, 128, CJ), BF16),
            pltpu.VMEM((CHUNKS, 128, CJ), BF16),
            pltpu.VMEM((2, 64, G2), BF16),
            pltpu.SemaphoreType.DMA((4,)),
            pltpu.SemaphoreType.REGULAR,
            pltpu.SemaphoreType.DMA((5,)),
            pltpu.SemaphoreType.DMA((9,)),
            pltpu.SemaphoreType.DMA((8,)),
            pltpu.SemaphoreType.DMA((14,)),
            pltpu.SemaphoreType.DMA((2, 4)),
            pltpu.SemaphoreType.DMA((2, 2)),
            pltpu.SemaphoreType.DMA((4,)),
            pltpu.SemaphoreType.DMA((2,)),
        ],
        compiler_params=pltpu.CompilerParams(
            collective_id=0, has_side_effects=True, vmem_limit_bytes=32 * 1024 * 1024),
        cost_estimate=pl.CostEstimate(flops=800_000_000, bytes_accessed=2_600_000, transcendentals=0),
    )(*arguments)


def solution(mesh):
    return jax.shard_map(
        on_device, mesh=mesh,
        in_specs=(P(None, "grid", "depth"), P(None, "depth", None), P()),
        out_specs=P(None, ("grid", "depth"), None, None), check_vma=False)
```

```python
import jax
import jax.numpy as jnp
from jax import lax
from jax.experimental import pallas as pl
from jax.experimental.pallas import tpu as pltpu
from jax.sharding import PartitionSpec as P

MESH = pl.DeviceIdType.MESH
XS = 4
JHI = 32
RLO = 32
JLO = 16
J = JHI * JLO
G2 = RLO * JHI
M = 512
KH = 64
KB = 128
ROWS = 128
CHUNKS = 2
CJ = J // CHUNKS
F32 = jnp.float32
BF16 = jnp.bfloat16


def kernel(at_ref, ff_ref, sf_ref, out_ref,
           s_vmem, abuf, bbuf, left, acc, own_send, own_part, z_send, z_recv, lhs,
           local_sem, ready, b_send, b_recv, a_send, a_recv, r_sems, own_sems, z_out, z_in):
    grid = lax.axis_index("grid")
    depth = lax.axis_index("depth")
    x = depth // 4
    zl = (depth // 2) % 2
    core = depth % 2

    def device(dx, which):
        return grid, (lax.rem(x + dx, XS) * 2 + zl) * 2 + which

    def z_device(which):
        return grid, (x * 2 + 1 - zl) * 2 + which

    def rows_of(dx, z):
        return pl.ds(pl.multiple_of((lax.rem(x + dx, XS) * 2 + z) * ROWS, ROWS), ROWS)

    def remote(src, dst, send, recv, to):
        return pltpu.make_async_remote_copy(
            src_ref=src, dst_ref=dst, send_sem=send, recv_sem=recv, device_id=to, device_id_type=MESH)

    z_of = (1 - zl, zl)
    load_s = pltpu.make_async_copy(sf_ref, s_vmem, local_sem.at[3])
    barrier = pltpu.get_barrier_semaphore()

    def b_copy(c, dx, p):
        i = (0 if dx == 1 else 2) + p
        return remote(ff_ref.at[p], bbuf.at[c, dx, p], b_send.at[i], b_recv.at[c * 4 + i], device(dx, 1))

    def a_copy(c, s, dx):
        i = s * 3 + dx - 1
        return remote(at_ref.at[:, :, rows_of(dx, z_of[s])], abuf.at[s, c, dx], a_send.at[i], a_recv.at[c * 6 + i], device(dx, 1))

    b_own = remote(ff_ref, bbuf.at[0, 0], b_send.at[4], b_recv.at[8], device(0, 1))
    a_own = [remote(at_ref.at[:, :, rows_of(0, z_of[s])], abuf.at[s, 0, 0], a_send.at[6 + s], a_recv.at[12 + s], device(0, 1))
             for s in range(2)]
    own_copies = [remote(own_send.at[h], own_part.at[h], own_sems.at[0, h], own_sems.at[1, h], device(0, 0)) for h in range(2)]
    z_copies = [[remote(z_send.at[c, h], z_recv.at[h], z_out.at[2 * h + c], z_in.at[h], z_device(c)) for c in range(2)]
                for h in range(2)]

    @pl.when(core == 0)
    def _():
        pl.semaphore_wait(barrier, 5)
        for dx, p in ((1, 0), (3, 1)):
            b_copy(0, dx, p).start()
        for to in (device(0, 1), z_device(1)):
            pl.semaphore_signal(ready, inc=1, device_id=to, device_id_type=MESH)
        for dx in (1, 3, 2):
            a_copy(0, 0, dx).start()
        for dx, p in ((1, 1), (3, 0)):
            b_copy(0, dx, p).start()
        b_own.start()
        a_own[0].start()
        a_own[1].start()
        for dx in (1, 3, 2):
            a_copy(0, 1, dx).start()
        load_s.start()
        for dx in (1, 3):
            for p in range(2):
                b_copy(0, dx, p).wait_send()
        for s in range(2):
            for dx in (1, 3, 2):
                a_copy(0, s, dx).wait_send()
            a_own[s].wait_send()
        b_own.wait_send()

    minus = jnp.where(lax.broadcasted_iota(jnp.int32, (64, KB), 1) < KH, 1.0, -1.0).astype(BF16)

    order = [(c, slot) for slot in (0, 1, 3, 2) for c in range(2)]

    def weigh(s, c, slot):
        turned = abuf[s, c, slot].reshape(KB, ROWS).T
        lanes = pl.ds(order.index((c, slot)) * KB, KB)
        for side in range(2):
            value = turned[side * 64:(side + 1) * 64]
            left[s, pl.ds(side * 128, 64), lanes] = value * minus
            left[s, pl.ds(side * 128 + 64, 64), lanes] = pltpu.roll(value, KH, 1)

    def contract(s, h, first, last):
        where = pl.ds(h * CJ, CJ)
        right = jnp.concatenate([bbuf[c, slot, :, :, where].reshape(KB, CJ) for c, slot in order[first:last]], axis=0)
        return jnp.dot(left[s, :, pl.ds(first * KB, (last - first) * KB)], right, preferred_element_type=F32)

    @pl.when(core == 1)
    def _():
        for to in [device(dx, 1) for dx in (1, 3, 2)] + [z_device(1)]:
            pl.semaphore_signal(barrier, inc=1, device_id=to, device_id_type=MESH)
        for to in [device(dx, 0) for dx in range(XS)] + [z_device(0)]:
            pl.semaphore_signal(barrier, inc=1, device_id=to, device_id_type=MESH)
        load_b = pltpu.make_async_copy(ff_ref, bbuf.at[1, 0], local_sem.at[0])
        load_a = [pltpu.make_async_copy(at_ref.at[:, :, rows_of(0, z_of[s])], abuf.at[s, 1, 0], local_sem.at[1 + s])
                  for s in range(2)]
        relays = [(remote(bbuf.at[c, 1, 0], bbuf.at[c, 2, 0], r_sems.at[0, 2 * c], r_sems.at[1, 2 * c], device(1, 1)),
                   remote(bbuf.at[c, 3, 1], bbuf.at[c, 2, 1], r_sems.at[0, 2 * c + 1], r_sems.at[1, 2 * c + 1], device(3, 1)))
                  for c in range(2)]

        pl.semaphore_wait(barrier, 4)
        for dx, p in ((1, 0), (3, 1)):
            b_copy(1, dx, p).start()
        for dx in (1, 3, 2):
            a_copy(1, 0, dx).start()
        for dx, p in ((1, 1), (3, 0)):
            b_copy(1, dx, p).start()
        load_b.start()
        load_a[0].start()
        load_a[1].start()
        for c in (1, 0):
            b_copy(c, 1, 0).wait_recv()
            relays[c][0].start()
            b_copy(c, 3, 1).wait_recv()
            relays[c][1].start()
        for dx in (1, 3, 2):
            a_copy(1, 1, dx).start()
        load_s.start()
        load_a[0].wait()
        weigh(0, 1, 0)
        for c in (1, 0):
            for dx in (1, 3):
                a_copy(c, 0, dx).wait_recv()
                weigh(0, c, dx)
        a_own[0].wait_recv()
        weigh(0, 0, 0)
        load_b.wait()
        b_own.wait_recv()
        for c in (1, 0):
            b_copy(c, 1, 1).wait_recv()
            b_copy(c, 3, 0).wait_recv()
        for h in range(2):
            acc[h] = contract(0, h, 0, 6)
        for c in (1, 0):
            a_copy(c, 0, 2).wait_recv()
            weigh(0, c, 2)
        for c in (1, 0):
            relays[c][0].wait_recv()
            relays[c][1].wait_recv()
        pl.semaphore_wait(ready, 2)
        for h in range(2):
            total = acc[h] + contract(0, h, 6, 8)
            for c in range(2):
                z_send[c, h] = total[c * 128:(c + 1) * 128].astype(BF16)
                z_copies[h][c].start()
        load_a[1].wait()
        weigh(1, 1, 0)
        for c in (1, 0):
            for dx in (1, 3, 2):
                a_copy(c, 1, dx).wait_recv()
                weigh(1, c, dx)
        a_own[1].wait_recv()
        weigh(1, 0, 0)
        for h in range(2):
            total = contract(1, h, 0, 8)
            own_send[h] = total[:128].astype(BF16)
            own_copies[h].start()
            own_part[h] = total[128:].astype(BF16)
        for dx in (1, 3):
            for p in range(2):
                b_copy(1, dx, p).wait_send()
        for s in range(2):
            for dx in (1, 3, 2):
                a_copy(1, s, dx).wait_send()
        for c in range(2):
            relays[c][0].wait_send()
            relays[c][1].wait_send()

    def swap(v, tile_bit, lane_bit):
        step, width = 1 << tile_bit, 1 << lane_bit
        v = v.reshape(16 // (2 * step), 2, step, JLO, 128)
        a = v[:, 0].reshape(8, JLO, 128)
        b = v[:, 1].reshape(8, JLO, 128)
        low = (lax.broadcasted_iota(jnp.int32, a.shape, 2) // width) % 2 == 0
        a, b = (jnp.where(low, a, pltpu.roll(b, width, 2)), jnp.where(low, pltpu.roll(a, 128 - width, 2), b))
        shape = (16 // (2 * step), 1, step, JLO, 128)
        return jnp.concatenate([a.reshape(shape), b.reshape(shape)], axis=1).reshape(16, JLO, 128)

    load_s.wait()

    result = jnp.zeros((64, M), F32)
    for top in range(2):
        @pl.when(core == 0)
        def _(top=top):
            own_copies[top].wait_recv()

        z_copies[top][0].wait_recv()
        total = own_part[top].astype(F32) + z_recv[top].astype(F32)
        value = total.astype(BF16).T.reshape(16, JLO, 128)
        for tile_bit, lane_bit in ((0, 0), (1, 1), (2, 2), (3, 3), (3, 6), (2, 5)):
            value = swap(value, tile_bit, lane_bit)
        right = []
        for u in range(4):
            for p in range(2):
                at = pl.ds((u * 2 + p) * 128, 128)
                turned = pl.ds((u * 2 + 1 - p) * 128, 128)
                for rh in range(2):
                    block = value[p * 8 + rh * 4 + u]
                    lhs[top, pl.ds(rh * 16, 16), at] = block if p == 0 else -block
                    lhs[top, pl.ds(32 + rh * 16, 16), turned] = block
                for t in range(8):
                    rl = (t % 2) * 16 + (t // 4) * 8 + (t // 2 % 2) * 4 + u
                    right.append(s_vmem[p, pl.ds(rl * JHI + top * 16, 16)])
        result += jnp.dot(lhs[top], jnp.concatenate(right, axis=0), preferred_element_type=F32)
    out_ref[...] = result.astype(BF16).reshape(2, 2, JLO, M)

    @pl.when(core == 1)
    def _():
        for copy in own_copies + z_copies[0] + z_copies[1]:
            copy.wait_send()


def on_device(amplitudes, first_factor, second_factor):
    arguments = [pltpu.with_memory_space_constraint(a, pltpu.HBM)
                 for a in (jnp.swapaxes(amplitudes, 1, 2), first_factor, second_factor)]
    return pl.pallas_call(
        kernel,
        out_shape=pltpu.VMEM((2, 2, JLO, M), BF16),
        in_specs=[pl.BlockSpec(memory_space=pltpu.HBM)] * 3,
        out_specs=pl.BlockSpec(memory_space=pltpu.VMEM),
        scratch_shapes=[
            pltpu.VMEM((2, G2, M), BF16),
            pltpu.VMEM((2, 2, XS, 2, KH, ROWS), BF16),
            pltpu.VMEM((2, XS, 2, KH, J), BF16),
            pltpu.VMEM((2, 256, 2 * XS * KB), BF16),
            pltpu.VMEM((CHUNKS, 256, CJ), F32),
            pltpu.VMEM((CHUNKS, 128, CJ), BF16),
            pltpu.VMEM((CHUNKS, 128, CJ), BF16),
            pltpu.VMEM((2, CHUNKS, 128, CJ), BF16),
            pltpu.VMEM((CHUNKS, 128, CJ), BF16),
            pltpu.VMEM((2, 64, G2), BF16),
            pltpu.SemaphoreType.DMA((4,)),
            pltpu.SemaphoreType.REGULAR,
            pltpu.SemaphoreType.DMA((5,)),
            pltpu.SemaphoreType.DMA((9,)),
            pltpu.SemaphoreType.DMA((8,)),
            pltpu.SemaphoreType.DMA((14,)),
            pltpu.SemaphoreType.DMA((2, 4)),
            pltpu.SemaphoreType.DMA((2, 2)),
            pltpu.SemaphoreType.DMA((4,)),
            pltpu.SemaphoreType.DMA((2,)),
        ],
        compiler_params=pltpu.CompilerParams(
            collective_id=0, has_side_effects=True, vmem_limit_bytes=32 * 1024 * 1024),
        cost_estimate=pl.CostEstimate(flops=800_000_000, bytes_accessed=2_600_000, transcendentals=0),
    )(*arguments)


def solution(mesh):
    return jax.shard_map(
        on_device, mesh=mesh,
        in_specs=(P(None, "grid", "depth"), P(None, "depth", None), P()),
        out_specs=P(None, ("grid", "depth"), None, None), check_vma=False)
```

```python
import jax
import jax.numpy as jnp
from jax import lax
from jax.experimental import pallas as pl
from jax.experimental.pallas import tpu as pltpu
from jax.sharding import PartitionSpec as P

MESH = pl.DeviceIdType.MESH
XS = 4
JHI = 32
RLO = 32
JLO = 16
J = JHI * JLO
G2 = RLO * JHI
M = 512
KH = 64
KB = 128
ROWS = 128
CHUNKS = 2
CJ = J // CHUNKS
F32 = jnp.float32
BF16 = jnp.bfloat16


def kernel(at_ref, ff_ref, sf_ref, out_ref,
           s_vmem, abuf, bbuf, left, acc, own_send, own_part, z_send, z_recv, lhs,
           local_sem, ready, b_send, b_recv, a_send, a_recv, r_sems, own_sems, z_out, z_in):
    grid = lax.axis_index("grid")
    depth = lax.axis_index("depth")
    x = depth // 4
    zl = (depth // 2) % 2
    core = depth % 2

    def device(dx, which):
        return grid, (lax.rem(x + dx, XS) * 2 + zl) * 2 + which

    def z_device(which):
        return grid, (x * 2 + 1 - zl) * 2 + which

    def rows_of(dx, z):
        return pl.ds(pl.multiple_of((lax.rem(x + dx, XS) * 2 + z) * ROWS, ROWS), ROWS)

    def remote(src, dst, send, recv, to):
        return pltpu.make_async_remote_copy(
            src_ref=src, dst_ref=dst, send_sem=send, recv_sem=recv, device_id=to, device_id_type=MESH)

    z_of = (1 - zl, zl)
    load_s = pltpu.make_async_copy(sf_ref, s_vmem, local_sem.at[3])
    barrier = pltpu.get_barrier_semaphore()

    def b_copy(c, dx, p):
        i = (0 if dx == 1 else 2) + p
        return remote(ff_ref.at[p], bbuf.at[c, dx, p], b_send.at[i], b_recv.at[c * 4 + i], device(dx, 1))

    def a_copy(c, s, dx):
        i = s * 3 + dx - 1
        return remote(at_ref.at[:, :, rows_of(dx, z_of[s])], abuf.at[s, c, dx], a_send.at[i], a_recv.at[c * 6 + i], device(dx, 1))

    b_own = remote(ff_ref, bbuf.at[0, 0], b_send.at[4], b_recv.at[8], device(0, 1))
    a_own = [remote(at_ref.at[:, :, rows_of(0, z_of[s])], abuf.at[s, 0, 0], a_send.at[6 + s], a_recv.at[12 + s], device(0, 1))
             for s in range(2)]
    own_copies = [remote(own_send.at[h], own_part.at[h], own_sems.at[0, h], own_sems.at[1, h], device(0, 0)) for h in range(2)]
    z_copies = [[remote(z_send.at[c, h], z_recv.at[h], z_out.at[2 * h + c], z_in.at[h], z_device(c)) for c in range(2)]
                for h in range(2)]

    @pl.when(core == 0)
    def _():
        pl.semaphore_wait(barrier, 5)
        for dx, p in ((1, 0), (3, 1)):
            b_copy(0, dx, p).start()
        for to in (device(0, 1), z_device(1)):
            pl.semaphore_signal(ready, inc=1, device_id=to, device_id_type=MESH)
        for dx in (1, 3, 2):
            a_copy(0, 0, dx).start()
        for dx, p in ((1, 1), (3, 0)):
            b_copy(0, dx, p).start()
        b_own.start()
        a_own[0].start()
        a_own[1].start()
        for dx in (1, 3, 2):
            a_copy(0, 1, dx).start()
        load_s.start()
        for dx in (1, 3):
            for p in range(2):
                b_copy(0, dx, p).wait_send()
        for s in range(2):
            for dx in (1, 3, 2):
                a_copy(0, s, dx).wait_send()
            a_own[s].wait_send()
        b_own.wait_send()

    minus = jnp.where(lax.broadcasted_iota(jnp.int32, (64, KB), 1) < KH, 1.0, -1.0).astype(BF16)

    order = [(c, slot) for slot in (0, 1, 3, 2) for c in range(2)]

    def weigh(s, c, slot):
        turned = abuf[s, c, slot].reshape(KB, ROWS).T
        lanes = pl.ds(order.index((c, slot)) * KB, KB)
        for side in range(2):
            value = turned[side * 64:(side + 1) * 64]
            left[s, pl.ds(side * 128, 64), lanes] = value * minus
            left[s, pl.ds(side * 128 + 64, 64), lanes] = pltpu.roll(value, KH, 1)

    def contract(s, h, first, last):
        where = pl.ds(h * CJ, CJ)
        right = jnp.concatenate([bbuf[c, slot, :, :, where].reshape(KB, CJ) for c, slot in order[first:last]], axis=0)
        return jnp.dot(left[s, :, pl.ds(first * KB, (last - first) * KB)], right, preferred_element_type=F32)

    @pl.when(core == 1)
    def _():
        for to in [device(dx, 1) for dx in (1, 3, 2)] + [z_device(1)]:
            pl.semaphore_signal(barrier, inc=1, device_id=to, device_id_type=MESH)
        for to in [device(dx, 0) for dx in range(XS)] + [z_device(0)]:
            pl.semaphore_signal(barrier, inc=1, device_id=to, device_id_type=MESH)
        load_b = pltpu.make_async_copy(ff_ref, bbuf.at[1, 0], local_sem.at[0])
        load_a = [pltpu.make_async_copy(at_ref.at[:, :, rows_of(0, z_of[s])], abuf.at[s, 1, 0], local_sem.at[1 + s])
                  for s in range(2)]
        relays = [(remote(bbuf.at[c, 1, 0], bbuf.at[c, 2, 0], r_sems.at[0, 2 * c], r_sems.at[1, 2 * c], device(1, 1)),
                   remote(bbuf.at[c, 3, 1], bbuf.at[c, 2, 1], r_sems.at[0, 2 * c + 1], r_sems.at[1, 2 * c + 1], device(3, 1)))
                  for c in range(2)]

        pl.semaphore_wait(barrier, 4)
        for dx, p in ((1, 0), (3, 1)):
            b_copy(1, dx, p).start()
        for dx in (1, 3, 2):
            a_copy(1, 0, dx).start()
        for dx, p in ((1, 1), (3, 0)):
            b_copy(1, dx, p).start()
        load_b.start()
        load_a[0].start()
        load_a[1].start()
        for c in (1, 0):
            b_copy(c, 1, 0).wait_recv()
            relays[c][0].start()
            b_copy(c, 3, 1).wait_recv()
            relays[c][1].start()
        for dx in (1, 3, 2):
            a_copy(1, 1, dx).start()
        load_s.start()
        load_a[0].wait()
        weigh(0, 1, 0)
        for c in (1, 0):
            for dx in (1, 3):
                a_copy(c, 0, dx).wait_recv()
                weigh(0, c, dx)
        a_own[0].wait_recv()
        weigh(0, 0, 0)
        load_b.wait()
        b_own.wait_recv()
        for c in (1, 0):
            b_copy(c, 1, 1).wait_recv()
            b_copy(c, 3, 0).wait_recv()
        for h in range(2):
            acc[h] = contract(0, h, 0, 6)
        for c in (1, 0):
            a_copy(c, 0, 2).wait_recv()
            weigh(0, c, 2)
        for c in (1, 0):
            relays[c][0].wait_recv()
            relays[c][1].wait_recv()
        pl.semaphore_wait(ready, 2)
        for h in range(2):
            total = acc[h] + contract(0, h, 6, 8)
            for c in range(2):
                z_send[c, h] = total[c * 128:(c + 1) * 128].astype(BF16)
                z_copies[h][c].start()
        load_a[1].wait()
        weigh(1, 1, 0)
        a_own[1].wait_recv()
        weigh(1, 0, 0)
        for c in (1, 0):
            for dx in (1, 3):
                a_copy(c, 1, dx).wait_recv()
                weigh(1, c, dx)
        for h in range(2):
            acc[h] = contract(1, h, 0, 6)
        for c in (1, 0):
            a_copy(c, 1, 2).wait_recv()
            weigh(1, c, 2)
        for h in range(2):
            total = acc[h] + contract(1, h, 6, 8)
            own_send[h] = total[:128].astype(BF16)
            own_copies[h].start()
            own_part[h] = total[128:].astype(BF16)
        for dx in (1, 3):
            for p in range(2):
                b_copy(1, dx, p).wait_send()
        for s in range(2):
            for dx in (1, 3, 2):
                a_copy(1, s, dx).wait_send()
        for c in range(2):
            relays[c][0].wait_send()
            relays[c][1].wait_send()

    def swap(v, tile_bit, lane_bit):
        step, width = 1 << tile_bit, 1 << lane_bit
        v = v.reshape(16 // (2 * step), 2, step, JLO, 128)
        a = v[:, 0].reshape(8, JLO, 128)
        b = v[:, 1].reshape(8, JLO, 128)
        low = (lax.broadcasted_iota(jnp.int32, a.shape, 2) // width) % 2 == 0
        a, b = (jnp.where(low, a, pltpu.roll(b, width, 2)), jnp.where(low, pltpu.roll(a, 128 - width, 2), b))
        shape = (16 // (2 * step), 1, step, JLO, 128)
        return jnp.concatenate([a.reshape(shape), b.reshape(shape)], axis=1).reshape(16, JLO, 128)

    load_s.wait()

    result = jnp.zeros((64, M), F32)
    for top in range(2):
        @pl.when(core == 0)
        def _(top=top):
            own_copies[top].wait_recv()

        z_copies[top][0].wait_recv()
        total = own_part[top].astype(F32) + z_recv[top].astype(F32)
        value = total.astype(BF16).T.reshape(16, JLO, 128)
        for tile_bit, lane_bit in ((0, 0), (1, 1), (2, 2), (3, 3), (3, 6), (2, 5)):
            value = swap(value, tile_bit, lane_bit)
        right = []
        for u in range(4):
            for p in range(2):
                at = pl.ds((u * 2 + p) * 128, 128)
                turned = pl.ds((u * 2 + 1 - p) * 128, 128)
                for rh in range(2):
                    block = value[p * 8 + rh * 4 + u]
                    lhs[top, pl.ds(rh * 16, 16), at] = block if p == 0 else -block
                    lhs[top, pl.ds(32 + rh * 16, 16), turned] = block
                for t in range(8):
                    rl = (t % 2) * 16 + (t // 4) * 8 + (t // 2 % 2) * 4 + u
                    right.append(s_vmem[p, pl.ds(rl * JHI + top * 16, 16)])
        result += jnp.dot(lhs[top], jnp.concatenate(right, axis=0), preferred_element_type=F32)
    out_ref[...] = result.astype(BF16).reshape(2, 2, JLO, M)

    @pl.when(core == 1)
    def _():
        for copy in own_copies + z_copies[0] + z_copies[1]:
            copy.wait_send()


def on_device(amplitudes, first_factor, second_factor):
    arguments = [pltpu.with_memory_space_constraint(a, pltpu.HBM)
                 for a in (jnp.swapaxes(amplitudes, 1, 2), first_factor, second_factor)]
    return pl.pallas_call(
        kernel,
        out_shape=pltpu.VMEM((2, 2, JLO, M), BF16),
        in_specs=[pl.BlockSpec(memory_space=pltpu.HBM)] * 3,
        out_specs=pl.BlockSpec(memory_space=pltpu.VMEM),
        scratch_shapes=[
            pltpu.VMEM((2, G2, M), BF16),
            pltpu.VMEM((2, 2, XS, 2, KH, ROWS), BF16),
            pltpu.VMEM((2, XS, 2, KH, J), BF16),
            pltpu.VMEM((2, 256, 2 * XS * KB), BF16),
            pltpu.VMEM((CHUNKS, 256, CJ), F32),
            pltpu.VMEM((CHUNKS, 128, CJ), BF16),
            pltpu.VMEM((CHUNKS, 128, CJ), BF16),
            pltpu.VMEM((2, CHUNKS, 128, CJ), BF16),
            pltpu.VMEM((CHUNKS, 128, CJ), BF16),
            pltpu.VMEM((2, 64, G2), BF16),
            pltpu.SemaphoreType.DMA((4,)),
            pltpu.SemaphoreType.REGULAR,
            pltpu.SemaphoreType.DMA((5,)),
            pltpu.SemaphoreType.DMA((9,)),
            pltpu.SemaphoreType.DMA((8,)),
            pltpu.SemaphoreType.DMA((14,)),
            pltpu.SemaphoreType.DMA((2, 4)),
            pltpu.SemaphoreType.DMA((2, 2)),
            pltpu.SemaphoreType.DMA((4,)),
            pltpu.SemaphoreType.DMA((2,)),
        ],
        compiler_params=pltpu.CompilerParams(
            collective_id=0, has_side_effects=True, vmem_limit_bytes=32 * 1024 * 1024),
        cost_estimate=pl.CostEstimate(flops=800_000_000, bytes_accessed=2_600_000, transcendentals=0),
    )(*arguments)


def solution(mesh):
    return jax.shard_map(
        on_device, mesh=mesh,
        in_specs=(P(None, "grid", "depth"), P(None, "depth", None), P()),
        out_specs=P(None, ("grid", "depth"), None, None), check_vma=False)
```

```python
import jax
import jax.numpy as jnp
from jax import lax
from jax.experimental import pallas as pl
from jax.experimental.pallas import tpu as pltpu
from jax.sharding import PartitionSpec as P

MESH = pl.DeviceIdType.MESH
XS = 4
LATE = 2
JHI = 32
RLO = 32
JLO = 16
J = JHI * JLO
G2 = RLO * JHI
M = 512
KH = 64
KB = 128
ROWS = 128
CHUNKS = 2
CJ = J // CHUNKS
F32 = jnp.float32
BF16 = jnp.bfloat16


def kernel(at_ref, ff_ref, sf_ref, out_ref,
           s_vmem, abuf, bbuf, left, acc, own_send, own_part, z_send, z_recv, lhs,
           local_sem, ready, late_in, b_send, b_recv, a_send, a_recv, r_sems, own_sems, z_out, z_in):
    grid = lax.axis_index("grid")
    depth = lax.axis_index("depth")
    x = depth // 4
    zl = (depth // 2) % 2
    core = depth % 2

    def device(dx, which):
        return grid, (lax.rem(x + dx, XS) * 2 + zl) * 2 + which

    def z_device(which):
        return grid, (x * 2 + 1 - zl) * 2 + which

    def rows_of(dx, z):
        return pl.ds(pl.multiple_of((lax.rem(x + dx, XS) * 2 + z) * ROWS, ROWS), ROWS)

    def remote(src, dst, send, recv, to):
        return pltpu.make_async_remote_copy(
            src_ref=src, dst_ref=dst, send_sem=send, recv_sem=recv, device_id=to, device_id_type=MESH)

    z_of = (1 - zl, zl)
    load_s = pltpu.make_async_copy(sf_ref, s_vmem, local_sem.at[3])
    barrier = pltpu.get_barrier_semaphore()

    def b_copy(c, dx, p):
        i = (0 if dx == 1 else 2) + p
        return remote(ff_ref.at[p], bbuf.at[c, dx, p], b_send.at[i], b_recv.at[c * 4 + i], device(dx, 1))

    def a_copy(c, s, dx):
        i = s * 3 + dx - 1
        return remote(at_ref.at[:, :, rows_of(dx, z_of[s])], abuf.at[s, c, dx], a_send.at[i], a_recv.at[c * 6 + i], device(dx, 1))

    b_own = remote(ff_ref, bbuf.at[0, 0], b_send.at[4], b_recv.at[8], device(0, 1))
    a_own = [remote(at_ref.at[:, :, rows_of(0, z_of[s])], abuf.at[s, 0, 0], a_send.at[6 + s], a_recv.at[12 + s], device(0, 1))
             for s in range(2)]
    own_copies = [remote(own_send.at[h], own_part.at[h], own_sems.at[0, h], own_sems.at[1, h], device(0, 0)) for h in range(2)]
    z_copies = [[remote(z_send.at[c, h], z_recv.at[h], z_out.at[2 * h + c], z_in.at[h], z_device(c)) for c in range(2)]
                for h in range(2)]

    def target(dx):
        return lax.rem(x + dx, XS)

    def signal(sem, to):
        pl.semaphore_signal(sem, inc=1, device_id=to, device_id_type=MESH)

    def when_start(condition, copy):
        @pl.when(condition)
        def _():
            copy.start()

    def push(c, late):
        copies = [(dx, b_copy(c, dx, p)) for dx, p in ((1, 0), (3, 1))]
        copies += [(dx, a_copy(c, 0, dx)) for dx in (1, 3, 2)]
        copies += [(dx, b_copy(c, dx, p)) for dx, p in ((1, 1), (3, 0))]
        for dx, copy in copies:
            when_start((target(dx) == LATE) == late, copy)

    @pl.when(core == 0)
    def _():
        @pl.when(x != LATE)
        def _():
            signal(barrier, (grid, (LATE * 2 + zl) * 2 + 1))
            pl.semaphore_wait(barrier, 4)

        @pl.when(x == LATE)
        def _():
            pl.semaphore_wait(barrier, 5)

        push(0, False)
        signal(ready, device(0, 1))
        signal(ready, z_device(1))
        b_own.start()
        a_own[0].start()
        a_own[1].start()
        for dx in (1, 3, 2):
            when_start(target(dx) != LATE, a_copy(0, 1, dx))

        @pl.when(x != LATE)
        def _():
            pl.semaphore_wait(late_in, 1)

        push(0, True)
        for dx in (1, 3, 2):
            when_start(target(dx) == LATE, a_copy(0, 1, dx))
        load_s.start()
        for dx in (1, 3):
            for p in range(2):
                b_copy(0, dx, p).wait_send()
        for s in range(2):
            for dx in (1, 3, 2):
                a_copy(0, s, dx).wait_send()
            a_own[s].wait_send()
        b_own.wait_send()

    minus = jnp.where(lax.broadcasted_iota(jnp.int32, (64, KB), 1) < KH, 1.0, -1.0).astype(BF16)

    order = [(c, slot) for slot in (0, 1, 3, 2) for c in range(2)]

    def weigh(s, c, slot):
        turned = abuf[s, c, slot].reshape(KB, ROWS).T
        lanes = pl.ds(order.index((c, slot)) * KB, KB)
        for side in range(2):
            value = turned[side * 64:(side + 1) * 64]
            left[s, pl.ds(side * 128, 64), lanes] = value * minus
            left[s, pl.ds(side * 128 + 64, 64), lanes] = pltpu.roll(value, KH, 1)

    def contract(s, h, first, last):
        where = pl.ds(h * CJ, CJ)
        right = jnp.concatenate([bbuf[c, slot, :, :, where].reshape(KB, CJ) for c, slot in order[first:last]], axis=0)
        return jnp.dot(left[s, :, pl.ds(first * KB, (last - first) * KB)], right, preferred_element_type=F32)

    @pl.when(core == 1)
    def _():
        @pl.when(x != LATE)
        def _():
            for dx in (1, 3, 2):
                signal(barrier, device(dx, 1))
            for dx in range(XS):
                signal(barrier, device(dx, 0))

        @pl.when(x == LATE)
        def _():
            signal(barrier, device(0, 0))

        signal(barrier, z_device(1))
        signal(barrier, z_device(0))
        load_b = pltpu.make_async_copy(ff_ref, bbuf.at[1, 0], local_sem.at[0])
        load_a = [pltpu.make_async_copy(at_ref.at[:, :, rows_of(0, z_of[s])], abuf.at[s, 1, 0], local_sem.at[1 + s])
                  for s in range(2)]
        relays = [(remote(bbuf.at[c, 1, 0], bbuf.at[c, 2, 0], r_sems.at[0, 2 * c], r_sems.at[1, 2 * c], device(1, 1)),
                   remote(bbuf.at[c, 3, 1], bbuf.at[c, 2, 1], r_sems.at[0, 2 * c + 1], r_sems.at[1, 2 * c + 1], device(3, 1)))
                  for c in range(2)]

        @pl.when(x != LATE)
        def _():
            pl.semaphore_wait(barrier, 3)

        @pl.when(x == LATE)
        def _():
            pl.semaphore_wait(barrier, 7)
            for dx in (1, 3, 2):
                signal(late_in, device(dx, 1))
                signal(late_in, device(dx, 0))

        push(1, False)
        load_b.start()
        load_a[0].start()
        load_a[1].start()
        for dx in (1, 3, 2):
            when_start((x != LATE) & (target(dx) != LATE), a_copy(1, 1, dx))

        @pl.when(x != LATE)
        def _():
            pl.semaphore_wait(late_in, 1)

        push(1, True)
        for c in (1, 0):
            b_copy(c, 1, 0).wait_recv()
            relays[c][0].start()
            b_copy(c, 3, 1).wait_recv()
            relays[c][1].start()
        for dx in (1, 3, 2):
            when_start((x == LATE) | (target(dx) == LATE), a_copy(1, 1, dx))
        load_s.start()
        load_a[0].wait()
        weigh(0, 1, 0)
        for c in (1, 0):
            for dx in (1, 3):
                a_copy(c, 0, dx).wait_recv()
                weigh(0, c, dx)
        a_own[0].wait_recv()
        weigh(0, 0, 0)
        load_b.wait()
        b_own.wait_recv()
        for c in (1, 0):
            b_copy(c, 1, 1).wait_recv()
            b_copy(c, 3, 0).wait_recv()
        for h in range(2):
            acc[h] = contract(0, h, 0, 6)
        for c in (1, 0):
            a_copy(c, 0, 2).wait_recv()
            weigh(0, c, 2)
        for c in (1, 0):
            relays[c][0].wait_recv()
            relays[c][1].wait_recv()
        pl.semaphore_wait(ready, 2)
        for h in range(2):
            total = acc[h] + contract(0, h, 6, 8)
            for c in range(2):
                z_send[c, h] = total[c * 128:(c + 1) * 128].astype(BF16)
                z_copies[h][c].start()
        load_a[1].wait()
        weigh(1, 1, 0)
        a_own[1].wait_recv()
        weigh(1, 0, 0)
        for c in (1, 0):
            for dx in (1, 3):
                a_copy(c, 1, dx).wait_recv()
                weigh(1, c, dx)
        for h in range(2):
            acc[h] = contract(1, h, 0, 6)
        for c in (1, 0):
            a_copy(c, 1, 2).wait_recv()
            weigh(1, c, 2)
        for h in range(2):
            total = acc[h] + contract(1, h, 6, 8)
            own_send[h] = total[:128].astype(BF16)
            own_copies[h].start()
            own_part[h] = total[128:].astype(BF16)
        for dx in (1, 3):
            for p in range(2):
                b_copy(1, dx, p).wait_send()
        for s in range(2):
            for dx in (1, 3, 2):
                a_copy(1, s, dx).wait_send()
        for c in range(2):
            relays[c][0].wait_send()
            relays[c][1].wait_send()

    def swap(v, tile_bit, lane_bit):
        step, width = 1 << tile_bit, 1 << lane_bit
        v = v.reshape(16 // (2 * step), 2, step, JLO, 128)
        a = v[:, 0].reshape(8, JLO, 128)
        b = v[:, 1].reshape(8, JLO, 128)
        low = (lax.broadcasted_iota(jnp.int32, a.shape, 2) // width) % 2 == 0
        a, b = (jnp.where(low, a, pltpu.roll(b, width, 2)), jnp.where(low, pltpu.roll(a, 128 - width, 2), b))
        shape = (16 // (2 * step), 1, step, JLO, 128)
        return jnp.concatenate([a.reshape(shape), b.reshape(shape)], axis=1).reshape(16, JLO, 128)

    load_s.wait()

    result = jnp.zeros((64, M), F32)
    for top in range(2):
        @pl.when(core == 0)
        def _(top=top):
            own_copies[top].wait_recv()

        z_copies[top][0].wait_recv()
        total = own_part[top].astype(F32) + z_recv[top].astype(F32)
        value = total.astype(BF16).T.reshape(16, JLO, 128)
        for tile_bit, lane_bit in ((0, 0), (1, 1), (2, 2), (3, 3), (3, 6), (2, 5)):
            value = swap(value, tile_bit, lane_bit)
        right = []
        for u in range(4):
            for p in range(2):
                at = pl.ds((u * 2 + p) * 128, 128)
                turned = pl.ds((u * 2 + 1 - p) * 128, 128)
                for rh in range(2):
                    block = value[p * 8 + rh * 4 + u]
                    lhs[top, pl.ds(rh * 16, 16), at] = block if p == 0 else -block
                    lhs[top, pl.ds(32 + rh * 16, 16), turned] = block
                for t in range(8):
                    rl = (t % 2) * 16 + (t // 4) * 8 + (t // 2 % 2) * 4 + u
                    right.append(s_vmem[p, pl.ds(rl * JHI + top * 16, 16)])
        result += jnp.dot(lhs[top], jnp.concatenate(right, axis=0), preferred_element_type=F32)
    out_ref[...] = result.astype(BF16).reshape(2, 2, JLO, M)

    @pl.when(core == 1)
    def _():
        for copy in own_copies + z_copies[0] + z_copies[1]:
            copy.wait_send()


def on_device(amplitudes, first_factor, second_factor):
    arguments = [pltpu.with_memory_space_constraint(a, pltpu.HBM)
                 for a in (jnp.swapaxes(amplitudes, 1, 2), first_factor, second_factor)]
    return pl.pallas_call(
        kernel,
        out_shape=pltpu.VMEM((2, 2, JLO, M), BF16),
        in_specs=[pl.BlockSpec(memory_space=pltpu.HBM)] * 3,
        out_specs=pl.BlockSpec(memory_space=pltpu.VMEM),
        scratch_shapes=[
            pltpu.VMEM((2, G2, M), BF16),
            pltpu.VMEM((2, 2, XS, 2, KH, ROWS), BF16),
            pltpu.VMEM((2, XS, 2, KH, J), BF16),
            pltpu.VMEM((2, 256, 2 * XS * KB), BF16),
            pltpu.VMEM((CHUNKS, 256, CJ), F32),
            pltpu.VMEM((CHUNKS, 128, CJ), BF16),
            pltpu.VMEM((CHUNKS, 128, CJ), BF16),
            pltpu.VMEM((2, CHUNKS, 128, CJ), BF16),
            pltpu.VMEM((CHUNKS, 128, CJ), BF16),
            pltpu.VMEM((2, 64, G2), BF16),
            pltpu.SemaphoreType.DMA((4,)),
            pltpu.SemaphoreType.REGULAR,
            pltpu.SemaphoreType.REGULAR,
            pltpu.SemaphoreType.DMA((5,)),
            pltpu.SemaphoreType.DMA((9,)),
            pltpu.SemaphoreType.DMA((8,)),
            pltpu.SemaphoreType.DMA((14,)),
            pltpu.SemaphoreType.DMA((2, 4)),
            pltpu.SemaphoreType.DMA((2, 2)),
            pltpu.SemaphoreType.DMA((4,)),
            pltpu.SemaphoreType.DMA((2,)),
        ],
        compiler_params=pltpu.CompilerParams(
            collective_id=0, has_side_effects=True, vmem_limit_bytes=32 * 1024 * 1024),
        cost_estimate=pl.CostEstimate(flops=800_000_000, bytes_accessed=2_600_000, transcendentals=0),
    )(*arguments)


def solution(mesh):
    return jax.shard_map(
        on_device, mesh=mesh,
        in_specs=(P(None, "grid", "depth"), P(None, "depth", None), P()),
        out_specs=P(None, ("grid", "depth"), None, None), check_vma=False)
```

```python
import jax
import jax.numpy as jnp
from jax import lax
from jax.experimental import pallas as pl
from jax.experimental.pallas import tpu as pltpu
from jax.sharding import PartitionSpec as P

MESH = pl.DeviceIdType.MESH
XS = 4
JHI = 32
RLO = 32
JLO = 16
J = JHI * JLO
G2 = RLO * JHI
M = 512
KH = 64
KB = 128
ROWS = 128
CHUNKS = 2
CJ = J // CHUNKS
F32 = jnp.float32
BF16 = jnp.bfloat16


def kernel(at_ref, ff_ref, sf_ref, out_ref,
           s_vmem, abuf, bbuf, left, acc, own_send, own_part, z_send, z_recv, lhs,
           local_sem, ready, b_send, b_recv, a_send, a_recv, r_sems, own_sems, z_out, z_in):
    grid = lax.axis_index("grid")
    depth = lax.axis_index("depth")
    x = depth // 4
    zl = (depth // 2) % 2
    core = depth % 2

    def device(dx, which):
        return grid, (lax.rem(x + dx, XS) * 2 + zl) * 2 + which

    def z_device(which):
        return grid, (x * 2 + 1 - zl) * 2 + which

    def rows_of(dx, z):
        return pl.ds(pl.multiple_of((lax.rem(x + dx, XS) * 2 + z) * ROWS, ROWS), ROWS)

    def remote(src, dst, send, recv, to):
        return pltpu.make_async_remote_copy(
            src_ref=src, dst_ref=dst, send_sem=send, recv_sem=recv, device_id=to, device_id_type=MESH)

    z_of = (1 - zl, zl)
    load_s = pltpu.make_async_copy(sf_ref, s_vmem, local_sem.at[3])
    barrier = pltpu.get_barrier_semaphore()

    def b_copy(c, dx, p):
        i = (0 if dx == 1 else 2) + p
        return remote(ff_ref.at[p], bbuf.at[c, dx, p], b_send.at[i], b_recv.at[c * 4 + i], device(dx, 1))

    def a_copy(c, s, dx):
        i = s * 3 + dx - 1
        return remote(at_ref.at[:, :, rows_of(dx, z_of[s])], abuf.at[s, c, dx], a_send.at[i], a_recv.at[c * 6 + i], device(dx, 1))

    b_own = remote(ff_ref, bbuf.at[0, 0], b_send.at[4], b_recv.at[8], device(0, 1))
    a_own = [remote(at_ref.at[:, :, rows_of(0, z_of[s])], abuf.at[s, 0, 0], a_send.at[6 + s], a_recv.at[12 + s], device(0, 1))
             for s in range(2)]
    own_copies = [remote(own_send.at[h], own_part.at[h], own_sems.at[0, h], own_sems.at[1, h], device(0, 0)) for h in range(2)]
    z_copies = [[remote(z_send.at[c, h], z_recv.at[h], z_out.at[2 * h + c], z_in.at[h], z_device(c)) for c in range(2)]
                for h in range(2)]

    @pl.when(core == 0)
    def _():
        pl.semaphore_wait(barrier, 5)
        for dx, p in ((1, 0), (3, 1)):
            b_copy(0, dx, p).start()
        for to in (device(0, 1), z_device(1)):
            pl.semaphore_signal(ready, inc=1, device_id=to, device_id_type=MESH)
        for dx in (1, 3, 2):
            a_copy(0, 0, dx).start()
        for dx, p in ((1, 1), (3, 0)):
            b_copy(0, dx, p).start()
        b_own.start()
        a_own[0].start()
        a_own[1].start()
        for dx in (1, 3, 2):
            a_copy(0, 1, dx).start()
        load_s.start()
        for dx in (1, 3):
            for p in range(2):
                b_copy(0, dx, p).wait_send()
        for s in range(2):
            for dx in (1, 3, 2):
                a_copy(0, s, dx).wait_send()
            a_own[s].wait_send()
        b_own.wait_send()

    minus = jnp.where(lax.broadcasted_iota(jnp.int32, (64, KB), 1) < KH, 1.0, -1.0).astype(BF16)

    order = [(c, slot) for slot in (0, 1, 3, 2) for c in range(2)]

    def weigh(s, c, slot):
        turned = abuf[s, c, slot].reshape(KB, ROWS).T
        lanes = pl.ds(order.index((c, slot)) * KB, KB)
        for side in range(2):
            value = turned[side * 64:(side + 1) * 64]
            left[s, pl.ds(side * 128, 64), lanes] = value * minus
            left[s, pl.ds(side * 128 + 64, 64), lanes] = pltpu.roll(value, KH, 1)

    def contract(s, h, first, last):
        where = pl.ds(h * CJ, CJ)
        right = jnp.concatenate([bbuf[c, slot, :, :, where].reshape(KB, CJ) for c, slot in order[first:last]], axis=0)
        return jnp.dot(left[s, :, pl.ds(first * KB, (last - first) * KB)], right, preferred_element_type=F32)

    @pl.when(core == 1)
    def _():
        for to in [device(dx, 1) for dx in (1, 3, 2)] + [z_device(1)]:
            pl.semaphore_signal(barrier, inc=1, device_id=to, device_id_type=MESH)
        for to in [device(dx, 0) for dx in range(XS)] + [z_device(0)]:
            pl.semaphore_signal(barrier, inc=1, device_id=to, device_id_type=MESH)
        load_b = pltpu.make_async_copy(ff_ref, bbuf.at[1, 0], local_sem.at[0])
        load_a = [pltpu.make_async_copy(at_ref.at[:, :, rows_of(0, z_of[s])], abuf.at[s, 1, 0], local_sem.at[1 + s])
                  for s in range(2)]
        relays = [(remote(bbuf.at[c, 1, 0], bbuf.at[c, 2, 0], r_sems.at[0, 2 * c], r_sems.at[1, 2 * c], device(1, 1)),
                   remote(bbuf.at[c, 3, 1], bbuf.at[c, 2, 1], r_sems.at[0, 2 * c + 1], r_sems.at[1, 2 * c + 1], device(3, 1)))
                  for c in range(2)]

        pl.semaphore_wait(barrier, 4)
        for dx, p in ((1, 0), (3, 1)):
            b_copy(1, dx, p).start()
        for dx in (1, 3, 2):
            a_copy(1, 0, dx).start()
        for dx, p in ((1, 1), (3, 0)):
            b_copy(1, dx, p).start()
        load_b.start()
        load_a[0].start()
        load_a[1].start()
        for c in (1, 0):
            b_copy(c, 1, 0).wait_recv()
            relays[c][0].start()
            b_copy(c, 3, 1).wait_recv()
            relays[c][1].start()
        for dx in (1, 3, 2):
            a_copy(1, 1, dx).start()
        load_s.start()
        load_a[0].wait()
        weigh(0, 1, 0)
        for c in (1, 0):
            for dx in (1, 3):
                a_copy(c, 0, dx).wait_recv()
                weigh(0, c, dx)
        a_own[0].wait_recv()
        weigh(0, 0, 0)
        load_b.wait()
        b_own.wait_recv()
        for c in (1, 0):
            b_copy(c, 1, 1).wait_recv()
            b_copy(c, 3, 0).wait_recv()
        for h in range(2):
            acc[h] = contract(0, h, 0, 6)
        for c in (1, 0):
            a_copy(c, 0, 2).wait_recv()
            weigh(0, c, 2)
        for c in (1, 0):
            relays[c][0].wait_recv()
            relays[c][1].wait_recv()
        pl.semaphore_wait(ready, 2)
        for h in range(2):
            total = acc[h] + contract(0, h, 6, 8)
            for c in (1, 0):
                z_send[c, h] = total[c * 128:(c + 1) * 128].astype(BF16)
                z_copies[h][c].start()
        load_a[1].wait()
        weigh(1, 1, 0)
        a_own[1].wait_recv()
        weigh(1, 0, 0)
        for c in (1, 0):
            for dx in (1, 3):
                a_copy(c, 1, dx).wait_recv()
                weigh(1, c, dx)
        for h in range(2):
            acc[h] = contract(1, h, 0, 6)
        for c in (1, 0):
            a_copy(c, 1, 2).wait_recv()
            weigh(1, c, 2)
        for h in range(2):
            total = acc[h] + contract(1, h, 6, 8)
            own_send[h] = total[:128].astype(BF16)
            own_copies[h].start()
            own_part[h] = total[128:].astype(BF16)
        for dx in (1, 3):
            for p in range(2):
                b_copy(1, dx, p).wait_send()
        for s in range(2):
            for dx in (1, 3, 2):
                a_copy(1, s, dx).wait_send()
        for c in range(2):
            relays[c][0].wait_send()
            relays[c][1].wait_send()

    def swap(v, tile_bit, lane_bit):
        step, width = 1 << tile_bit, 1 << lane_bit
        v = v.reshape(16 // (2 * step), 2, step, JLO, 128)
        a = v[:, 0].reshape(8, JLO, 128)
        b = v[:, 1].reshape(8, JLO, 128)
        low = (lax.broadcasted_iota(jnp.int32, a.shape, 2) // width) % 2 == 0
        a, b = (jnp.where(low, a, pltpu.roll(b, width, 2)), jnp.where(low, pltpu.roll(a, 128 - width, 2), b))
        shape = (16 // (2 * step), 1, step, JLO, 128)
        return jnp.concatenate([a.reshape(shape), b.reshape(shape)], axis=1).reshape(16, JLO, 128)

    load_s.wait()

    result = jnp.zeros((64, M), F32)
    for top in range(2):
        @pl.when(core == 0)
        def _(top=top):
            own_copies[top].wait_recv()

        z_copies[top][0].wait_recv()
        total = own_part[top].astype(F32) + z_recv[top].astype(F32)
        value = total.astype(BF16).T.reshape(16, JLO, 128)
        for tile_bit, lane_bit in ((0, 0), (1, 1), (2, 2), (3, 3), (3, 6), (2, 5)):
            value = swap(value, tile_bit, lane_bit)
        right = []
        for u in range(4):
            for p in range(2):
                at = pl.ds((u * 2 + p) * 128, 128)
                turned = pl.ds((u * 2 + 1 - p) * 128, 128)
                for rh in range(2):
                    block = value[p * 8 + rh * 4 + u]
                    lhs[top, pl.ds(rh * 16, 16), at] = block if p == 0 else -block
                    lhs[top, pl.ds(32 + rh * 16, 16), turned] = block
                for t in range(8):
                    rl = (t % 2) * 16 + (t // 4) * 8 + (t // 2 % 2) * 4 + u
                    right.append(s_vmem[p, pl.ds(rl * JHI + top * 16, 16)])
        result += jnp.dot(lhs[top], jnp.concatenate(right, axis=0), preferred_element_type=F32)
    out_ref[...] = result.astype(BF16).reshape(2, 2, JLO, M)

    @pl.when(core == 1)
    def _():
        for copy in own_copies + z_copies[0] + z_copies[1]:
            copy.wait_send()


def on_device(amplitudes, first_factor, second_factor):
    arguments = [pltpu.with_memory_space_constraint(a, pltpu.HBM)
                 for a in (jnp.swapaxes(amplitudes, 1, 2), first_factor, second_factor)]
    return pl.pallas_call(
        kernel,
        out_shape=pltpu.VMEM((2, 2, JLO, M), BF16),
        in_specs=[pl.BlockSpec(memory_space=pltpu.HBM)] * 3,
        out_specs=pl.BlockSpec(memory_space=pltpu.VMEM),
        scratch_shapes=[
            pltpu.VMEM((2, G2, M), BF16),
            pltpu.VMEM((2, 2, XS, 2, KH, ROWS), BF16),
            pltpu.VMEM((2, XS, 2, KH, J), BF16),
            pltpu.VMEM((2, 256, 2 * XS * KB), BF16),
            pltpu.VMEM((CHUNKS, 256, CJ), F32),
            pltpu.VMEM((CHUNKS, 128, CJ), BF16),
            pltpu.VMEM((CHUNKS, 128, CJ), BF16),
            pltpu.VMEM((2, CHUNKS, 128, CJ), BF16),
            pltpu.VMEM((CHUNKS, 128, CJ), BF16),
            pltpu.VMEM((2, 64, G2), BF16),
            pltpu.SemaphoreType.DMA((4,)),
            pltpu.SemaphoreType.REGULAR,
            pltpu.SemaphoreType.DMA((5,)),
            pltpu.SemaphoreType.DMA((9,)),
            pltpu.SemaphoreType.DMA((8,)),
            pltpu.SemaphoreType.DMA((14,)),
            pltpu.SemaphoreType.DMA((2, 4)),
            pltpu.SemaphoreType.DMA((2, 2)),
            pltpu.SemaphoreType.DMA((4,)),
            pltpu.SemaphoreType.DMA((2,)),
        ],
        compiler_params=pltpu.CompilerParams(
            collective_id=0, has_side_effects=True, vmem_limit_bytes=32 * 1024 * 1024),
        cost_estimate=pl.CostEstimate(flops=800_000_000, bytes_accessed=2_600_000, transcendentals=0),
    )(*arguments)


def solution(mesh):
    return jax.shard_map(
        on_device, mesh=mesh,
        in_specs=(P(None, "grid", "depth"), P(None, "depth", None), P()),
        out_specs=P(None, ("grid", "depth"), None, None), check_vma=False)
```

```python
import jax
import jax.numpy as jnp
from jax import lax
from jax.experimental import pallas as pl
from jax.experimental.pallas import tpu as pltpu
from jax.sharding import PartitionSpec as P

MESH = pl.DeviceIdType.MESH
XS = 4
JHI = 32
RLO = 32
JLO = 16
J = JHI * JLO
G2 = RLO * JHI
M = 512
KH = 64
KB = 128
ROWS = 128
CHUNKS = 2
CJ = J // CHUNKS
F32 = jnp.float32
BF16 = jnp.bfloat16


def kernel(at_ref, ff_ref, sf_ref, out_ref,
           s_vmem, abuf, bbuf, left, acc, own_send, own_part, z_send, z_recv, lhs,
           local_sem, ready, b_send, b_recv, a_send, a_recv, r_sems, own_sems, z_out, z_in):
    grid = lax.axis_index("grid")
    depth = lax.axis_index("depth")
    x = depth // 4
    zl = (depth // 2) % 2
    core = depth % 2

    def device(dx, which):
        return grid, (lax.rem(x + dx, XS) * 2 + zl) * 2 + which

    def z_device(which):
        return grid, (x * 2 + 1 - zl) * 2 + which

    def rows_of(dx, z):
        return pl.ds(pl.multiple_of((lax.rem(x + dx, XS) * 2 + z) * ROWS, ROWS), ROWS)

    def remote(src, dst, send, recv, to):
        return pltpu.make_async_remote_copy(
            src_ref=src, dst_ref=dst, send_sem=send, recv_sem=recv, device_id=to, device_id_type=MESH)

    z_of = (1 - zl, zl)
    load_s = pltpu.make_async_copy(sf_ref, s_vmem, local_sem.at[3])
    barrier = pltpu.get_barrier_semaphore()

    def b_copy(c, dx, p):
        i = (0 if dx == 1 else 2) + p
        return remote(ff_ref.at[p], bbuf.at[c, dx, p], b_send.at[i], b_recv.at[c * 4 + i], device(dx, 1))

    def a_copy(c, s, dx):
        i = s * 3 + dx - 1
        return remote(at_ref.at[:, :, rows_of(dx, z_of[s])], abuf.at[s, c, dx], a_send.at[i], a_recv.at[c * 6 + i], device(dx, 1))

    b_own = remote(ff_ref, bbuf.at[0, 0], b_send.at[4], b_recv.at[8], device(0, 1))
    a_own = [remote(at_ref.at[:, :, rows_of(0, z_of[s])], abuf.at[s, 0, 0], a_send.at[6 + s], a_recv.at[12 + s], device(0, 1))
             for s in range(2)]
    own_copies = [remote(own_send.at[h], own_part.at[h], own_sems.at[0, h], own_sems.at[1, h], device(0, 0)) for h in range(2)]
    z_copies = [[remote(z_send.at[c, h], z_recv.at[h], z_out.at[2 * h + c], z_in.at[h], z_device(c)) for c in range(2)]
                for h in range(2)]

    @pl.when(core == 0)
    def _():
        pl.semaphore_wait(barrier, 5)
        for dx, p in ((1, 0), (3, 1)):
            b_copy(0, dx, p).start()
        for to in (device(0, 1), z_device(1)):
            pl.semaphore_signal(ready, inc=1, device_id=to, device_id_type=MESH)
        for dx in (1, 3, 2):
            a_copy(0, 0, dx).start()
        for dx, p in ((1, 1), (3, 0)):
            b_copy(0, dx, p).start()
        b_own.start()
        a_own[0].start()
        a_own[1].start()
        for dx in (1, 3, 2):
            a_copy(0, 1, dx).start()
        load_s.start()
        for dx in (1, 3):
            for p in range(2):
                b_copy(0, dx, p).wait_send()
        for s in range(2):
            for dx in (1, 3, 2):
                a_copy(0, s, dx).wait_send()
            a_own[s].wait_send()
        b_own.wait_send()

    minus = jnp.where(lax.broadcasted_iota(jnp.int32, (64, KB), 1) < KH, 1.0, -1.0).astype(BF16)

    order = [(c, slot) for slot in (0, 1, 3, 2) for c in range(2)]

    def weigh(s, c, slot):
        turned = abuf[s, c, slot].reshape(KB, ROWS).T
        lanes = pl.ds(order.index((c, slot)) * KB, KB)
        for side in range(2):
            value = turned[side * 64:(side + 1) * 64]
            left[s, pl.ds(side * 128, 64), lanes] = value * minus
            left[s, pl.ds(side * 128 + 64, 64), lanes] = pltpu.roll(value, KH, 1)

    def contract(s, h, first, last):
        where = pl.ds(h * CJ, CJ)
        right = jnp.concatenate([bbuf[c, slot, :, :, where].reshape(KB, CJ) for c, slot in order[first:last]], axis=0)
        return jnp.dot(left[s, :, pl.ds(first * KB, (last - first) * KB)], right, preferred_element_type=F32)

    @pl.when(core == 1)
    def _():
        for to in [device(dx, 1) for dx in (1, 3, 2)] + [z_device(1)]:
            pl.semaphore_signal(barrier, inc=1, device_id=to, device_id_type=MESH)
        for to in [device(dx, 0) for dx in range(XS)] + [z_device(0)]:
            pl.semaphore_signal(barrier, inc=1, device_id=to, device_id_type=MESH)
        load_b = pltpu.make_async_copy(ff_ref, bbuf.at[1, 0], local_sem.at[0])
        load_a = [pltpu.make_async_copy(at_ref.at[:, :, rows_of(0, z_of[s])], abuf.at[s, 1, 0], local_sem.at[1 + s])
                  for s in range(2)]
        def relay(c, h):
            where = pl.ds(h * CJ, CJ)
            i = 4 * h + 2 * c
            return (remote(bbuf.at[c, 1, 0, :, where], bbuf.at[c, 2, 0, :, where], r_sems.at[0, i], r_sems.at[1, i], device(1, 1)),
                    remote(bbuf.at[c, 3, 1, :, where], bbuf.at[c, 2, 1, :, where], r_sems.at[0, i + 1], r_sems.at[1, i + 1], device(3, 1)))

        relays = [[relay(c, h) for c in range(2)] for h in range(2)]

        pl.semaphore_wait(barrier, 4)
        for dx, p in ((1, 0), (3, 1)):
            b_copy(1, dx, p).start()
        for dx in (1, 3, 2):
            a_copy(1, 0, dx).start()
        for dx, p in ((1, 1), (3, 0)):
            b_copy(1, dx, p).start()
        load_b.start()
        load_a[0].start()
        load_a[1].start()
        for c in (1, 0):
            b_copy(c, 1, 0).wait_recv()
            relays[0][c][0].start()
            b_copy(c, 3, 1).wait_recv()
            relays[0][c][1].start()
        for c in (1, 0):
            for copy in relays[1][c]:
                copy.start()
        for dx in (1, 3, 2):
            a_copy(1, 1, dx).start()
        load_s.start()
        load_a[0].wait()
        weigh(0, 1, 0)
        for c in (1, 0):
            for dx in (1, 3):
                a_copy(c, 0, dx).wait_recv()
                weigh(0, c, dx)
        a_own[0].wait_recv()
        weigh(0, 0, 0)
        load_b.wait()
        b_own.wait_recv()
        for c in (1, 0):
            b_copy(c, 1, 1).wait_recv()
            b_copy(c, 3, 0).wait_recv()
        for h in range(2):
            acc[h] = contract(0, h, 0, 6)
        for c in (1, 0):
            a_copy(c, 0, 2).wait_recv()
            weigh(0, c, 2)
        pl.semaphore_wait(ready, 2)
        for h in range(2):
            for c in (1, 0):
                for copy in relays[h][c]:
                    copy.wait_recv()
            total = acc[h] + contract(0, h, 6, 8)
            for c in (1, 0):
                z_send[c, h] = total[c * 128:(c + 1) * 128].astype(BF16)
                z_copies[h][c].start()
        load_a[1].wait()
        weigh(1, 1, 0)
        a_own[1].wait_recv()
        weigh(1, 0, 0)
        for c in (1, 0):
            for dx in (1, 3):
                a_copy(c, 1, dx).wait_recv()
                weigh(1, c, dx)
        for h in range(2):
            acc[h] = contract(1, h, 0, 6)
        for c in (1, 0):
            a_copy(c, 1, 2).wait_recv()
            weigh(1, c, 2)
        for h in range(2):
            total = acc[h] + contract(1, h, 6, 8)
            own_send[h] = total[:128].astype(BF16)
            own_copies[h].start()
            own_part[h] = total[128:].astype(BF16)
        for dx in (1, 3):
            for p in range(2):
                b_copy(1, dx, p).wait_send()
        for s in range(2):
            for dx in (1, 3, 2):
                a_copy(1, s, dx).wait_send()
        for copies in relays[0] + relays[1]:
            for copy in copies:
                copy.wait_send()

    def swap(v, tile_bit, lane_bit):
        step, width = 1 << tile_bit, 1 << lane_bit
        v = v.reshape(16 // (2 * step), 2, step, JLO, 128)
        a = v[:, 0].reshape(8, JLO, 128)
        b = v[:, 1].reshape(8, JLO, 128)
        low = (lax.broadcasted_iota(jnp.int32, a.shape, 2) // width) % 2 == 0
        a, b = (jnp.where(low, a, pltpu.roll(b, width, 2)), jnp.where(low, pltpu.roll(a, 128 - width, 2), b))
        shape = (16 // (2 * step), 1, step, JLO, 128)
        return jnp.concatenate([a.reshape(shape), b.reshape(shape)], axis=1).reshape(16, JLO, 128)

    load_s.wait()

    result = jnp.zeros((64, M), F32)
    for top in range(2):
        @pl.when(core == 0)
        def _(top=top):
            own_copies[top].wait_recv()

        z_copies[top][0].wait_recv()
        total = own_part[top].astype(F32) + z_recv[top].astype(F32)
        value = total.astype(BF16).T.reshape(16, JLO, 128)
        for tile_bit, lane_bit in ((0, 0), (1, 1), (2, 2), (3, 3), (3, 6), (2, 5)):
            value = swap(value, tile_bit, lane_bit)
        right = []
        for u in range(4):
            for p in range(2):
                at = pl.ds((u * 2 + p) * 128, 128)
                turned = pl.ds((u * 2 + 1 - p) * 128, 128)
                for rh in range(2):
                    block = value[p * 8 + rh * 4 + u]
                    lhs[top, pl.ds(rh * 16, 16), at] = block if p == 0 else -block
                    lhs[top, pl.ds(32 + rh * 16, 16), turned] = block
                for t in range(8):
                    rl = (t % 2) * 16 + (t // 4) * 8 + (t // 2 % 2) * 4 + u
                    right.append(s_vmem[p, pl.ds(rl * JHI + top * 16, 16)])
        result += jnp.dot(lhs[top], jnp.concatenate(right, axis=0), preferred_element_type=F32)
    out_ref[...] = result.astype(BF16).reshape(2, 2, JLO, M)

    @pl.when(core == 1)
    def _():
        for copy in own_copies + z_copies[0] + z_copies[1]:
            copy.wait_send()


def on_device(amplitudes, first_factor, second_factor):
    arguments = [pltpu.with_memory_space_constraint(a, pltpu.HBM)
                 for a in (jnp.swapaxes(amplitudes, 1, 2), first_factor, second_factor)]
    return pl.pallas_call(
        kernel,
        out_shape=pltpu.VMEM((2, 2, JLO, M), BF16),
        in_specs=[pl.BlockSpec(memory_space=pltpu.HBM)] * 3,
        out_specs=pl.BlockSpec(memory_space=pltpu.VMEM),
        scratch_shapes=[
            pltpu.VMEM((2, G2, M), BF16),
            pltpu.VMEM((2, 2, XS, 2, KH, ROWS), BF16),
            pltpu.VMEM((2, XS, 2, KH, J), BF16),
            pltpu.VMEM((2, 256, 2 * XS * KB), BF16),
            pltpu.VMEM((CHUNKS, 256, CJ), F32),
            pltpu.VMEM((CHUNKS, 128, CJ), BF16),
            pltpu.VMEM((CHUNKS, 128, CJ), BF16),
            pltpu.VMEM((2, CHUNKS, 128, CJ), BF16),
            pltpu.VMEM((CHUNKS, 128, CJ), BF16),
            pltpu.VMEM((2, 64, G2), BF16),
            pltpu.SemaphoreType.DMA((4,)),
            pltpu.SemaphoreType.REGULAR,
            pltpu.SemaphoreType.DMA((5,)),
            pltpu.SemaphoreType.DMA((9,)),
            pltpu.SemaphoreType.DMA((8,)),
            pltpu.SemaphoreType.DMA((14,)),
            pltpu.SemaphoreType.DMA((2, 8)),
            pltpu.SemaphoreType.DMA((2, 2)),
            pltpu.SemaphoreType.DMA((4,)),
            pltpu.SemaphoreType.DMA((2,)),
        ],
        compiler_params=pltpu.CompilerParams(
            collective_id=0, has_side_effects=True, vmem_limit_bytes=32 * 1024 * 1024),
        cost_estimate=pl.CostEstimate(flops=800_000_000, bytes_accessed=2_600_000, transcendentals=0),
    )(*arguments)


def solution(mesh):
    return jax.shard_map(
        on_device, mesh=mesh,
        in_specs=(P(None, "grid", "depth"), P(None, "depth", None), P()),
        out_specs=P(None, ("grid", "depth"), None, None), check_vma=False)
```

```python
import jax
import jax.numpy as jnp
from jax import lax
from jax.experimental import pallas as pl
from jax.experimental.pallas import tpu as pltpu
from jax.sharding import PartitionSpec as P

MESH = pl.DeviceIdType.MESH
XS = 4
JHI = 32
RLO = 32
JLO = 16
J = JHI * JLO
G2 = RLO * JHI
M = 512
KH = 64
KB = 128
ROWS = 128
CHUNKS = 2
CJ = J // CHUNKS
F32 = jnp.float32
BF16 = jnp.bfloat16


def kernel(at_ref, ff_ref, sf_ref, out_ref,
           s_vmem, abuf, bbuf, left, acc, own_send, own_part, z_send, z_recv, lhs,
           local_sem, ready, b_send, b_recv, a_send, a_recv, r_sems, own_sems, z_out, z_in):
    grid = lax.axis_index("grid")
    depth = lax.axis_index("depth")
    x = depth // 4
    zl = (depth // 2) % 2
    core = depth % 2

    def device(dx, which):
        return grid, (lax.rem(x + dx, XS) * 2 + zl) * 2 + which

    def z_device(which):
        return grid, (x * 2 + 1 - zl) * 2 + which

    def rows_of(dx, z):
        return pl.ds(pl.multiple_of((lax.rem(x + dx, XS) * 2 + z) * ROWS, ROWS), ROWS)

    def remote(src, dst, send, recv, to):
        return pltpu.make_async_remote_copy(
            src_ref=src, dst_ref=dst, send_sem=send, recv_sem=recv, device_id=to, device_id_type=MESH)

    z_of = (1 - zl, zl)
    load_s = pltpu.make_async_copy(sf_ref, s_vmem, local_sem.at[3])
    barrier = pltpu.get_barrier_semaphore()

    halves = [pl.ds(h * CJ, CJ) for h in range(2)]

    def b_copy(c, dx):
        p, i = (0, 0) if dx == 1 else (1, 1)
        return remote(ff_ref.at[p], bbuf.at[c, dx, p], b_send.at[i], b_recv.at[c * 6 + i], device(dx, 1))

    def b_rest(c, dx, h):
        p, i = (1, 2 + h) if dx == 1 else (0, 4 + h)
        return remote(ff_ref.at[p, :, halves[h]], bbuf.at[c, dx, p, :, halves[h]], b_send.at[i], b_recv.at[c * 6 + i], device(dx, 1))

    def a_copy(c, s, dx):
        i = s * 3 + dx - 1
        return remote(at_ref.at[:, :, rows_of(dx, z_of[s])], abuf.at[s, c, dx], a_send.at[i], a_recv.at[c * 6 + i], device(dx, 1))

    b_own = remote(ff_ref, bbuf.at[0, 0], b_send.at[6], b_recv.at[12], device(0, 1))
    a_own = [remote(at_ref.at[:, :, rows_of(0, z_of[s])], abuf.at[s, 0, 0], a_send.at[6 + s], a_recv.at[12 + s], device(0, 1))
             for s in range(2)]
    own_copies = [remote(own_send.at[h], own_part.at[h], own_sems.at[0, h], own_sems.at[1, h], device(0, 0)) for h in range(2)]
    z_copies = [[remote(z_send.at[c, h], z_recv.at[h], z_out.at[2 * h + c], z_in.at[h], z_device(c)) for c in range(2)]
                for h in range(2)]

    @pl.when(core == 0)
    def _():
        pl.semaphore_wait(barrier, 5)
        for dx in (1, 3):
            b_copy(0, dx).start()
        for to in (device(0, 1), z_device(1)):
            pl.semaphore_signal(ready, inc=1, device_id=to, device_id_type=MESH)
        for dx in (1, 3, 2):
            a_copy(0, 0, dx).start()
        for dx in (1, 3):
            b_rest(0, dx, 0).start()
        b_own.start()
        a_own[0].start()
        for dx in (1, 3):
            b_rest(0, dx, 1).start()
        a_own[1].start()
        for dx in (1, 3, 2):
            a_copy(0, 1, dx).start()
        load_s.start()
        for dx in (1, 3):
            b_copy(0, dx).wait_send()
            for h in range(2):
                b_rest(0, dx, h).wait_send()
        for s in range(2):
            for dx in (1, 3, 2):
                a_copy(0, s, dx).wait_send()
            a_own[s].wait_send()
        b_own.wait_send()

    minus = jnp.where(lax.broadcasted_iota(jnp.int32, (64, KB), 1) < KH, 1.0, -1.0).astype(BF16)

    order = [(c, slot) for slot in (0, 1, 3, 2) for c in range(2)]

    def weigh(s, c, slot):
        turned = abuf[s, c, slot].reshape(KB, ROWS).T
        lanes = pl.ds(order.index((c, slot)) * KB, KB)
        for side in range(2):
            value = turned[side * 64:(side + 1) * 64]
            left[s, pl.ds(side * 128, 64), lanes] = value * minus
            left[s, pl.ds(side * 128 + 64, 64), lanes] = pltpu.roll(value, KH, 1)

    def contract(s, h, first, last):
        where = pl.ds(h * CJ, CJ)
        right = jnp.concatenate([bbuf[c, slot, :, :, where].reshape(KB, CJ) for c, slot in order[first:last]], axis=0)
        return jnp.dot(left[s, :, pl.ds(first * KB, (last - first) * KB)], right, preferred_element_type=F32)

    @pl.when(core == 1)
    def _():
        for to in [device(dx, 1) for dx in (1, 3, 2)] + [z_device(1)]:
            pl.semaphore_signal(barrier, inc=1, device_id=to, device_id_type=MESH)
        for to in [device(dx, 0) for dx in range(XS)] + [z_device(0)]:
            pl.semaphore_signal(barrier, inc=1, device_id=to, device_id_type=MESH)
        load_b = pltpu.make_async_copy(ff_ref, bbuf.at[1, 0], local_sem.at[0])
        load_a = [pltpu.make_async_copy(at_ref.at[:, :, rows_of(0, z_of[s])], abuf.at[s, 1, 0], local_sem.at[1 + s])
                  for s in range(2)]
        def relay(c, h):
            where = pl.ds(h * CJ, CJ)
            i = 4 * h + 2 * c
            return (remote(bbuf.at[c, 1, 0, :, where], bbuf.at[c, 2, 0, :, where], r_sems.at[0, i], r_sems.at[1, i], device(1, 1)),
                    remote(bbuf.at[c, 3, 1, :, where], bbuf.at[c, 2, 1, :, where], r_sems.at[0, i + 1], r_sems.at[1, i + 1], device(3, 1)))

        relays = [[relay(c, h) for c in range(2)] for h in range(2)]

        pl.semaphore_wait(barrier, 4)
        for dx in (1, 3):
            b_copy(1, dx).start()
        for dx in (1, 3, 2):
            a_copy(1, 0, dx).start()
        for dx in (1, 3):
            b_rest(1, dx, 0).start()
        load_b.start()
        load_a[0].start()
        load_a[1].start()
        for c in (1, 0):
            b_copy(c, 1).wait_recv()
            relays[0][c][0].start()
            b_copy(c, 3).wait_recv()
            relays[0][c][1].start()
        for dx in (1, 3):
            b_rest(1, dx, 1).start()
        for c in (1, 0):
            for copy in relays[1][c]:
                copy.start()
        for dx in (1, 3, 2):
            a_copy(1, 1, dx).start()
        load_s.start()
        load_a[0].wait()
        weigh(0, 1, 0)
        for c in (1, 0):
            for dx in (1, 3):
                a_copy(c, 0, dx).wait_recv()
                weigh(0, c, dx)
        a_own[0].wait_recv()
        weigh(0, 0, 0)
        load_b.wait()
        b_own.wait_recv()

        def early(h):
            for c in (1, 0):
                for dx in (1, 3):
                    b_rest(c, dx, h).wait_recv()
            acc[h] = contract(0, h, 0, 6)

        early(0)
        for c in (1, 0):
            a_copy(c, 0, 2).wait_recv()
            weigh(0, c, 2)
        pl.semaphore_wait(ready, 2)
        for h in range(2):
            if h == 1:
                early(1)
            for c in (1, 0):
                for copy in relays[h][c]:
                    copy.wait_recv()
            total = acc[h] + contract(0, h, 6, 8)
            for c in (1, 0):
                z_send[c, h] = total[c * 128:(c + 1) * 128].astype(BF16)
                z_copies[h][c].start()
        load_a[1].wait()
        weigh(1, 1, 0)
        a_own[1].wait_recv()
        weigh(1, 0, 0)
        for c in (1, 0):
            for dx in (1, 3):
                a_copy(c, 1, dx).wait_recv()
                weigh(1, c, dx)
        for h in range(2):
            acc[h] = contract(1, h, 0, 6)
        for c in (1, 0):
            a_copy(c, 1, 2).wait_recv()
            weigh(1, c, 2)
        for h in range(2):
            total = acc[h] + contract(1, h, 6, 8)
            own_send[h] = total[:128].astype(BF16)
            own_copies[h].start()
            own_part[h] = total[128:].astype(BF16)
        for dx in (1, 3):
            b_copy(1, dx).wait_send()
            for h in range(2):
                b_rest(1, dx, h).wait_send()
        for s in range(2):
            for dx in (1, 3, 2):
                a_copy(1, s, dx).wait_send()
        for copies in relays[0] + relays[1]:
            for copy in copies:
                copy.wait_send()

    def swap(v, tile_bit, lane_bit):
        step, width = 1 << tile_bit, 1 << lane_bit
        v = v.reshape(16 // (2 * step), 2, step, JLO, 128)
        a = v[:, 0].reshape(8, JLO, 128)
        b = v[:, 1].reshape(8, JLO, 128)
        low = (lax.broadcasted_iota(jnp.int32, a.shape, 2) // width) % 2 == 0
        a, b = (jnp.where(low, a, pltpu.roll(b, width, 2)), jnp.where(low, pltpu.roll(a, 128 - width, 2), b))
        shape = (16 // (2 * step), 1, step, JLO, 128)
        return jnp.concatenate([a.reshape(shape), b.reshape(shape)], axis=1).reshape(16, JLO, 128)

    load_s.wait()

    result = jnp.zeros((64, M), F32)
    for top in range(2):
        @pl.when(core == 0)
        def _(top=top):
            own_copies[top].wait_recv()

        z_copies[top][0].wait_recv()
        total = own_part[top].astype(F32) + z_recv[top].astype(F32)
        value = total.astype(BF16).T.reshape(16, JLO, 128)
        for tile_bit, lane_bit in ((0, 0), (1, 1), (2, 2), (3, 3), (3, 6), (2, 5)):
            value = swap(value, tile_bit, lane_bit)
        right = []
        for u in range(4):
            for p in range(2):
                at = pl.ds((u * 2 + p) * 128, 128)
                turned = pl.ds((u * 2 + 1 - p) * 128, 128)
                for rh in range(2):
                    block = value[p * 8 + rh * 4 + u]
                    lhs[top, pl.ds(rh * 16, 16), at] = block if p == 0 else -block
                    lhs[top, pl.ds(32 + rh * 16, 16), turned] = block
                for t in range(8):
                    rl = (t % 2) * 16 + (t // 4) * 8 + (t // 2 % 2) * 4 + u
                    right.append(s_vmem[p, pl.ds(rl * JHI + top * 16, 16)])
        result += jnp.dot(lhs[top], jnp.concatenate(right, axis=0), preferred_element_type=F32)
    out_ref[...] = result.astype(BF16).reshape(2, 2, JLO, M)

    @pl.when(core == 1)
    def _():
        for copy in own_copies + z_copies[0] + z_copies[1]:
            copy.wait_send()


def on_device(amplitudes, first_factor, second_factor):
    arguments = [pltpu.with_memory_space_constraint(a, pltpu.HBM)
                 for a in (jnp.swapaxes(amplitudes, 1, 2), first_factor, second_factor)]
    return pl.pallas_call(
        kernel,
        out_shape=pltpu.VMEM((2, 2, JLO, M), BF16),
        in_specs=[pl.BlockSpec(memory_space=pltpu.HBM)] * 3,
        out_specs=pl.BlockSpec(memory_space=pltpu.VMEM),
        scratch_shapes=[
            pltpu.VMEM((2, G2, M), BF16),
            pltpu.VMEM((2, 2, XS, 2, KH, ROWS), BF16),
            pltpu.VMEM((2, XS, 2, KH, J), BF16),
            pltpu.VMEM((2, 256, 2 * XS * KB), BF16),
            pltpu.VMEM((CHUNKS, 256, CJ), F32),
            pltpu.VMEM((CHUNKS, 128, CJ), BF16),
            pltpu.VMEM((CHUNKS, 128, CJ), BF16),
            pltpu.VMEM((2, CHUNKS, 128, CJ), BF16),
            pltpu.VMEM((CHUNKS, 128, CJ), BF16),
            pltpu.VMEM((2, 64, G2), BF16),
            pltpu.SemaphoreType.DMA((4,)),
            pltpu.SemaphoreType.REGULAR,
            pltpu.SemaphoreType.DMA((7,)),
            pltpu.SemaphoreType.DMA((13,)),
            pltpu.SemaphoreType.DMA((8,)),
            pltpu.SemaphoreType.DMA((14,)),
            pltpu.SemaphoreType.DMA((2, 8)),
            pltpu.SemaphoreType.DMA((2, 2)),
            pltpu.SemaphoreType.DMA((4,)),
            pltpu.SemaphoreType.DMA((2,)),
        ],
        compiler_params=pltpu.CompilerParams(
            collective_id=0, has_side_effects=True, vmem_limit_bytes=32 * 1024 * 1024),
        cost_estimate=pl.CostEstimate(flops=800_000_000, bytes_accessed=2_600_000, transcendentals=0),
    )(*arguments)


def solution(mesh):
    return jax.shard_map(
        on_device, mesh=mesh,
        in_specs=(P(None, "grid", "depth"), P(None, "depth", None), P()),
        out_specs=P(None, ("grid", "depth"), None, None), check_vma=False)
```

```python
import jax
import jax.numpy as jnp
from jax import lax
from jax.experimental import pallas as pl
from jax.experimental.pallas import tpu as pltpu
from jax.sharding import PartitionSpec as P

MESH = pl.DeviceIdType.MESH
XS = 4
JHI = 32
RLO = 32
JLO = 16
J = JHI * JLO
G2 = RLO * JHI
M = 512
KH = 64
KB = 128
ROWS = 128
CHUNKS = 2
CJ = J // CHUNKS
F32 = jnp.float32
BF16 = jnp.bfloat16


def kernel(at_ref, ff_ref, sf_ref, out_ref,
           s_vmem, abuf, bbuf, left, acc, own_send, own_part, z_send, z_recv, lhs,
           local_sem, ready, b_send, b_recv, a_send, a_recv, r_sems, own_sems, z_out, z_in):
    grid = lax.axis_index("grid")
    depth = lax.axis_index("depth")
    x = depth // 4
    zl = (depth // 2) % 2
    core = depth % 2

    def device(dx, which):
        return grid, (lax.rem(x + dx, XS) * 2 + zl) * 2 + which

    def z_device(which):
        return grid, (x * 2 + 1 - zl) * 2 + which

    def rows_of(dx, z):
        return pl.ds(pl.multiple_of((lax.rem(x + dx, XS) * 2 + z) * ROWS, ROWS), ROWS)

    def remote(src, dst, send, recv, to):
        return pltpu.make_async_remote_copy(
            src_ref=src, dst_ref=dst, send_sem=send, recv_sem=recv, device_id=to, device_id_type=MESH)

    z_of = (1 - zl, zl)
    load_s = pltpu.make_async_copy(sf_ref, s_vmem, local_sem.at[3])
    barrier = pltpu.get_barrier_semaphore()

    halves = [pl.ds(h * CJ, CJ) for h in range(2)]

    def b_copy(c, dx):
        p, i = (0, 0) if dx == 1 else (1, 1)
        return remote(ff_ref.at[p], bbuf.at[c, dx, p], b_send.at[i], b_recv.at[c * 6 + i], device(dx, 1))

    def b_rest(c, dx, h):
        p, i = (1, 2 + h) if dx == 1 else (0, 4 + h)
        return remote(ff_ref.at[p, :, halves[h]], bbuf.at[c, dx, p, :, halves[h]], b_send.at[i], b_recv.at[c * 6 + i], device(dx, 1))

    def a_copy(c, s, dx):
        i = s * 3 + dx - 1
        return remote(at_ref.at[:, :, rows_of(dx, z_of[s])], abuf.at[s, c, dx], a_send.at[i], a_recv.at[c * 6 + i], device(dx, 1))

    b_own = remote(ff_ref, bbuf.at[0, 0], b_send.at[6], b_recv.at[12], device(0, 1))
    a_own = [remote(at_ref.at[:, :, rows_of(0, z_of[s])], abuf.at[s, 0, 0], a_send.at[6 + s], a_recv.at[12 + s], device(0, 1))
             for s in range(2)]
    own_copies = [remote(own_send.at[h], own_part.at[h], own_sems.at[0, h], own_sems.at[1, h], device(0, 0)) for h in range(2)]
    z_copies = [[remote(z_send.at[c, h], z_recv.at[h], z_out.at[2 * h + c], z_in.at[h], z_device(c)) for c in range(2)]
                for h in range(2)]

    @pl.when(core == 0)
    def _():
        pl.semaphore_wait(barrier, 5)
        for dx in (1, 3):
            b_copy(0, dx).start()
        for to in (device(0, 1), z_device(1)):
            pl.semaphore_signal(ready, inc=1, device_id=to, device_id_type=MESH)
        for dx in (1, 3, 2):
            a_copy(0, 0, dx).start()
        for dx in (1, 3):
            b_rest(0, dx, 0).start()
        b_own.start()
        a_own[0].start()
        for dx in (1, 3):
            b_rest(0, dx, 1).start()
        a_own[1].start()
        for dx in (1, 3, 2):
            a_copy(0, 1, dx).start()
        load_s.start()
        for dx in (1, 3):
            b_copy(0, dx).wait_send()
            for h in range(2):
                b_rest(0, dx, h).wait_send()
        for s in range(2):
            for dx in (1, 3, 2):
                a_copy(0, s, dx).wait_send()
            a_own[s].wait_send()
        b_own.wait_send()

    minus = jnp.where(lax.broadcasted_iota(jnp.int32, (64, KB), 1) < KH, 1.0, -1.0).astype(BF16)

    order = [(c, slot) for slot in (0, 1, 3, 2) for c in range(2)]

    def weigh(s, c, slot):
        turned = abuf[s, c, slot].reshape(KB, ROWS).T
        lanes = pl.ds(order.index((c, slot)) * KB, KB)
        for side in range(2):
            value = turned[side * 64:(side + 1) * 64]
            left[s, pl.ds(side * 128, 64), lanes] = value * minus
            left[s, pl.ds(side * 128 + 64, 64), lanes] = pltpu.roll(value, KH, 1)

    def contract(s, h, first, last):
        where = pl.ds(h * CJ, CJ)
        right = jnp.concatenate([bbuf[c, slot, :, :, where].reshape(KB, CJ) for c, slot in order[first:last]], axis=0)
        return jnp.dot(left[s, :, pl.ds(first * KB, (last - first) * KB)], right, preferred_element_type=F32)

    @pl.when(core == 1)
    def _():
        for to in [device(dx, 1) for dx in (1, 3, 2)] + [z_device(1)]:
            pl.semaphore_signal(barrier, inc=1, device_id=to, device_id_type=MESH)
        for to in [device(dx, 0) for dx in range(XS)] + [z_device(0)]:
            pl.semaphore_signal(barrier, inc=1, device_id=to, device_id_type=MESH)
        load_b = pltpu.make_async_copy(ff_ref, bbuf.at[1, 0], local_sem.at[0])
        load_a = [pltpu.make_async_copy(at_ref.at[:, :, rows_of(0, z_of[s])], abuf.at[s, 1, 0], local_sem.at[1 + s])
                  for s in range(2)]
        def relay(c, h):
            where = pl.ds(h * CJ, CJ)
            i = 4 * h + 2 * c
            return (remote(bbuf.at[c, 1, 0, :, where], bbuf.at[c, 2, 0, :, where], r_sems.at[0, i], r_sems.at[1, i], device(1, 1)),
                    remote(bbuf.at[c, 3, 1, :, where], bbuf.at[c, 2, 1, :, where], r_sems.at[0, i + 1], r_sems.at[1, i + 1], device(3, 1)))

        relays = [[relay(c, h) for c in range(2)] for h in range(2)]

        pl.semaphore_wait(barrier, 4)
        for dx in (1, 3):
            b_copy(1, dx).start()
        for dx in (1, 3, 2):
            a_copy(1, 0, dx).start()
        for dx in (1, 3):
            b_rest(1, dx, 0).start()
        load_b.start()
        load_a[0].start()
        load_a[1].start()

        def serve(first):
            steps = (first, 4 - first)
            way = {1: 0, 3: 1}

            def pass_on(c, dx, h):
                relays[h][c][way[dx]].start()

            for dx in steps:
                b_copy(1, dx).wait_recv()
                pass_on(1, dx, 0)
            b_copy(0, first).wait_recv()
            pass_on(0, first, 0)
            for dx in (1, 3):
                b_rest(1, dx, 1).start()
            pass_on(1, first, 1)
            pass_on(0, first, 1)
            pass_on(1, steps[1], 1)
            b_copy(0, steps[1]).wait_recv()
            pass_on(0, steps[1], 0)
            pass_on(0, steps[1], 1)

        @pl.when(x == 1)
        def _():
            serve(3)

        @pl.when(x != 1)
        def _():
            serve(1)

        for dx in (1, 3, 2):
            a_copy(1, 1, dx).start()
        load_s.start()
        load_a[0].wait()
        weigh(0, 1, 0)
        for c in (1, 0):
            for dx in (1, 3):
                a_copy(c, 0, dx).wait_recv()
                weigh(0, c, dx)
        a_own[0].wait_recv()
        weigh(0, 0, 0)
        load_b.wait()
        b_own.wait_recv()

        def early(h):
            for c in (1, 0):
                for dx in (1, 3):
                    b_rest(c, dx, h).wait_recv()
            acc[h] = contract(0, h, 0, 6)

        early(0)
        for c in (1, 0):
            a_copy(c, 0, 2).wait_recv()
            weigh(0, c, 2)
        pl.semaphore_wait(ready, 2)
        for h in range(2):
            if h == 1:
                early(1)
            for c in (1, 0):
                for copy in relays[h][c]:
                    copy.wait_recv()
            total = acc[h] + contract(0, h, 6, 8)
            for c in (1, 0):
                z_send[c, h] = total[c * 128:(c + 1) * 128].astype(BF16)
                z_copies[h][c].start()
        load_a[1].wait()
        weigh(1, 1, 0)
        a_own[1].wait_recv()
        weigh(1, 0, 0)
        for c in (1, 0):
            for dx in (1, 3):
                a_copy(c, 1, dx).wait_recv()
                weigh(1, c, dx)
        for h in range(2):
            acc[h] = contract(1, h, 0, 6)
        for c in (1, 0):
            a_copy(c, 1, 2).wait_recv()
            weigh(1, c, 2)
        for h in range(2):
            total = acc[h] + contract(1, h, 6, 8)
            own_send[h] = total[:128].astype(BF16)
            own_copies[h].start()
            own_part[h] = total[128:].astype(BF16)
        for dx in (1, 3):
            b_copy(1, dx).wait_send()
            for h in range(2):
                b_rest(1, dx, h).wait_send()
        for s in range(2):
            for dx in (1, 3, 2):
                a_copy(1, s, dx).wait_send()
        for copies in relays[0] + relays[1]:
            for copy in copies:
                copy.wait_send()

    def swap(v, tile_bit, lane_bit):
        step, width = 1 << tile_bit, 1 << lane_bit
        v = v.reshape(16 // (2 * step), 2, step, JLO, 128)
        a = v[:, 0].reshape(8, JLO, 128)
        b = v[:, 1].reshape(8, JLO, 128)
        low = (lax.broadcasted_iota(jnp.int32, a.shape, 2) // width) % 2 == 0
        a, b = (jnp.where(low, a, pltpu.roll(b, width, 2)), jnp.where(low, pltpu.roll(a, 128 - width, 2), b))
        shape = (16 // (2 * step), 1, step, JLO, 128)
        return jnp.concatenate([a.reshape(shape), b.reshape(shape)], axis=1).reshape(16, JLO, 128)

    load_s.wait()

    result = jnp.zeros((64, M), F32)
    for top in range(2):
        @pl.when(core == 0)
        def _(top=top):
            own_copies[top].wait_recv()

        z_copies[top][0].wait_recv()
        total = own_part[top].astype(F32) + z_recv[top].astype(F32)
        value = total.astype(BF16).T.reshape(16, JLO, 128)
        for tile_bit, lane_bit in ((0, 0), (1, 1), (2, 2), (3, 3), (3, 6), (2, 5)):
            value = swap(value, tile_bit, lane_bit)
        right = []
        for u in range(4):
            for p in range(2):
                at = pl.ds((u * 2 + p) * 128, 128)
                turned = pl.ds((u * 2 + 1 - p) * 128, 128)
                for rh in range(2):
                    block = value[p * 8 + rh * 4 + u]
                    lhs[top, pl.ds(rh * 16, 16), at] = block if p == 0 else -block
                    lhs[top, pl.ds(32 + rh * 16, 16), turned] = block
                for t in range(8):
                    rl = (t % 2) * 16 + (t // 4) * 8 + (t // 2 % 2) * 4 + u
                    right.append(s_vmem[p, pl.ds(rl * JHI + top * 16, 16)])
        result += jnp.dot(lhs[top], jnp.concatenate(right, axis=0), preferred_element_type=F32)
    out_ref[...] = result.astype(BF16).reshape(2, 2, JLO, M)

    @pl.when(core == 1)
    def _():
        for copy in own_copies + z_copies[0] + z_copies[1]:
            copy.wait_send()


def on_device(amplitudes, first_factor, second_factor):
    arguments = [pltpu.with_memory_space_constraint(a, pltpu.HBM)
                 for a in (jnp.swapaxes(amplitudes, 1, 2), first_factor, second_factor)]
    return pl.pallas_call(
        kernel,
        out_shape=pltpu.VMEM((2, 2, JLO, M), BF16),
        in_specs=[pl.BlockSpec(memory_space=pltpu.HBM)] * 3,
        out_specs=pl.BlockSpec(memory_space=pltpu.VMEM),
        scratch_shapes=[
            pltpu.VMEM((2, G2, M), BF16),
            pltpu.VMEM((2, 2, XS, 2, KH, ROWS), BF16),
            pltpu.VMEM((2, XS, 2, KH, J), BF16),
            pltpu.VMEM((2, 256, 2 * XS * KB), BF16),
            pltpu.VMEM((CHUNKS, 256, CJ), F32),
            pltpu.VMEM((CHUNKS, 128, CJ), BF16),
            pltpu.VMEM((CHUNKS, 128, CJ), BF16),
            pltpu.VMEM((2, CHUNKS, 128, CJ), BF16),
            pltpu.VMEM((CHUNKS, 128, CJ), BF16),
            pltpu.VMEM((2, 64, G2), BF16),
            pltpu.SemaphoreType.DMA((4,)),
            pltpu.SemaphoreType.REGULAR,
            pltpu.SemaphoreType.DMA((7,)),
            pltpu.SemaphoreType.DMA((13,)),
            pltpu.SemaphoreType.DMA((8,)),
            pltpu.SemaphoreType.DMA((14,)),
            pltpu.SemaphoreType.DMA((2, 8)),
            pltpu.SemaphoreType.DMA((2, 2)),
            pltpu.SemaphoreType.DMA((4,)),
            pltpu.SemaphoreType.DMA((2,)),
        ],
        compiler_params=pltpu.CompilerParams(
            collective_id=0, has_side_effects=True, vmem_limit_bytes=32 * 1024 * 1024),
        cost_estimate=pl.CostEstimate(flops=800_000_000, bytes_accessed=2_600_000, transcendentals=0),
    )(*arguments)


def solution(mesh):
    return jax.shard_map(
        on_device, mesh=mesh,
        in_specs=(P(None, "grid", "depth"), P(None, "depth", None), P()),
        out_specs=P(None, ("grid", "depth"), None, None), check_vma=False)
```

```python
import jax
import jax.numpy as jnp
from jax import lax
from jax.experimental import pallas as pl
from jax.experimental.pallas import tpu as pltpu
from jax.sharding import PartitionSpec as P

MESH = pl.DeviceIdType.MESH
XS = 4
JHI = 32
RLO = 32
JLO = 16
J = JHI * JLO
G2 = RLO * JHI
M = 512
KH = 64
KB = 128
ROWS = 128
CHUNKS = 2
CJ = J // CHUNKS
F32 = jnp.float32
BF16 = jnp.bfloat16


def kernel(at_ref, ff_ref, sf_ref, out_ref,
           s_vmem, abuf, bbuf, left, acc, own_send, own_part, z_send, z_recv, lhs,
           local_sem, ready, b_send, b_recv, a_send, a_recv, r_sems, own_sems, z_out, z_in):
    grid = lax.axis_index("grid")
    depth = lax.axis_index("depth")
    x = depth // 4
    zl = (depth // 2) % 2
    core = depth % 2

    def device(dx, which):
        return grid, (lax.rem(x + dx, XS) * 2 + zl) * 2 + which

    def z_device(which):
        return grid, (x * 2 + 1 - zl) * 2 + which

    def rows_of(dx, z):
        return pl.ds(pl.multiple_of((lax.rem(x + dx, XS) * 2 + z) * ROWS, ROWS), ROWS)

    def remote(src, dst, send, recv, to):
        return pltpu.make_async_remote_copy(
            src_ref=src, dst_ref=dst, send_sem=send, recv_sem=recv, device_id=to, device_id_type=MESH)

    z_of = (1 - zl, zl)
    load_s = pltpu.make_async_copy(sf_ref, s_vmem, local_sem.at[3])
    barrier = pltpu.get_barrier_semaphore()

    halves = [pl.ds(h * CJ, CJ) for h in range(2)]

    def b_copy(c, dx):
        p, i = (0, 0) if dx == 1 else (1, 1)
        return remote(ff_ref.at[p], bbuf.at[c, dx, p], b_send.at[i], b_recv.at[c * 6 + i], device(dx, 1))

    def b_rest(c, dx, h):
        p, i = (1, 2 + h) if dx == 1 else (0, 4 + h)
        return remote(ff_ref.at[p, :, halves[h]], bbuf.at[c, dx, p, :, halves[h]], b_send.at[i], b_recv.at[c * 6 + i], device(dx, 1))

    def a_copy(c, s, dx):
        i = s * 3 + dx - 1
        return remote(at_ref.at[:, :, rows_of(dx, z_of[s])], abuf.at[s, c, dx], a_send.at[i], a_recv.at[c * 6 + i], device(dx, 1))

    b_own = remote(ff_ref, bbuf.at[0, 0], b_send.at[6], b_recv.at[12], device(0, 1))
    a_own = [remote(at_ref.at[:, :, rows_of(0, z_of[s])], abuf.at[s, 0, 0], a_send.at[6 + s], a_recv.at[12 + s], device(0, 1))
             for s in range(2)]
    own_copies = [remote(own_send.at[h], own_part.at[h], own_sems.at[0, h], own_sems.at[1, h], device(0, 0)) for h in range(2)]
    z_copies = [[remote(z_send.at[c, h], z_recv.at[h], z_out.at[2 * h + c], z_in.at[h], z_device(c)) for c in range(2)]
                for h in range(2)]

    @pl.when(core == 0)
    def _():
        pl.semaphore_wait(barrier, 5)
        for dx in (1, 3):
            b_copy(0, dx).start()
        for to in (device(0, 1), z_device(1)):
            pl.semaphore_signal(ready, inc=1, device_id=to, device_id_type=MESH)
        for dx in (1, 3, 2):
            a_copy(0, 0, dx).start()
        for dx in (1, 3):
            b_rest(0, dx, 0).start()
        b_own.start()
        a_own[0].start()
        for dx in (1, 3):
            b_rest(0, dx, 1).start()
        a_own[1].start()
        for dx in (1, 3, 2):
            a_copy(0, 1, dx).start()
        load_s.start()
        for dx in (1, 3):
            b_copy(0, dx).wait_send()
            for h in range(2):
                b_rest(0, dx, h).wait_send()
        for s in range(2):
            for dx in (1, 3, 2):
                a_copy(0, s, dx).wait_send()
            a_own[s].wait_send()
        b_own.wait_send()

    minus = jnp.where(lax.broadcasted_iota(jnp.int32, (64, KB), 1) < KH, 1.0, -1.0).astype(BF16)

    order = [(c, slot) for slot in (0, 1, 3, 2) for c in range(2)]

    def weigh(s, c, slot):
        turned = abuf[s, c, slot].reshape(KB, ROWS).T
        lanes = pl.ds(order.index((c, slot)) * KB, KB)
        for side in range(2):
            value = turned[side * 64:(side + 1) * 64]
            left[s, pl.ds(side * 128, 64), lanes] = value * minus
            left[s, pl.ds(side * 128 + 64, 64), lanes] = pltpu.roll(value, KH, 1)

    def contract(s, h, first, last, rows=slice(0, 256)):
        where = pl.ds(h * CJ, CJ)
        right = jnp.concatenate([bbuf[c, slot, :, :, where].reshape(KB, CJ) for c, slot in order[first:last]], axis=0)
        return jnp.dot(left[s, rows, pl.ds(first * KB, (last - first) * KB)], right, preferred_element_type=F32)

    @pl.when(core == 1)
    def _():
        for to in [device(dx, 1) for dx in (1, 3, 2)] + [z_device(1)]:
            pl.semaphore_signal(barrier, inc=1, device_id=to, device_id_type=MESH)
        for to in [device(dx, 0) for dx in range(XS)] + [z_device(0)]:
            pl.semaphore_signal(barrier, inc=1, device_id=to, device_id_type=MESH)
        load_b = pltpu.make_async_copy(ff_ref, bbuf.at[1, 0], local_sem.at[0])
        load_a = [pltpu.make_async_copy(at_ref.at[:, :, rows_of(0, z_of[s])], abuf.at[s, 1, 0], local_sem.at[1 + s])
                  for s in range(2)]
        def relay(c, h):
            where = pl.ds(h * CJ, CJ)
            i = 4 * h + 2 * c
            return (remote(bbuf.at[c, 1, 0, :, where], bbuf.at[c, 2, 0, :, where], r_sems.at[0, i], r_sems.at[1, i], device(1, 1)),
                    remote(bbuf.at[c, 3, 1, :, where], bbuf.at[c, 2, 1, :, where], r_sems.at[0, i + 1], r_sems.at[1, i + 1], device(3, 1)))

        relays = [[relay(c, h) for c in range(2)] for h in range(2)]

        pl.semaphore_wait(barrier, 4)
        for dx in (1, 3):
            b_copy(1, dx).start()
        for dx in (1, 3, 2):
            a_copy(1, 0, dx).start()
        for dx in (1, 3):
            b_rest(1, dx, 0).start()
        load_b.start()
        load_a[0].start()
        load_a[1].start()

        def serve(first):
            steps = (first, 4 - first)
            way = {1: 0, 3: 1}

            def pass_on(c, dx, h):
                relays[h][c][way[dx]].start()

            for dx in steps:
                b_copy(1, dx).wait_recv()
                pass_on(1, dx, 0)
            b_copy(0, first).wait_recv()
            pass_on(0, first, 0)
            for dx in (1, 3):
                b_rest(1, dx, 1).start()
            pass_on(1, first, 1)
            pass_on(0, first, 1)
            pass_on(1, steps[1], 1)
            b_copy(0, steps[1]).wait_recv()
            pass_on(0, steps[1], 0)
            pass_on(0, steps[1], 1)

        @pl.when(x == 1)
        def _():
            serve(3)

        @pl.when(x != 1)
        def _():
            serve(1)

        for dx in (1, 3, 2):
            a_copy(1, 1, dx).start()
        load_s.start()
        load_a[0].wait()
        weigh(0, 1, 0)
        for c in (1, 0):
            for dx in (1, 3):
                a_copy(c, 0, dx).wait_recv()
                weigh(0, c, dx)
        a_own[0].wait_recv()
        weigh(0, 0, 0)
        load_b.wait()
        b_own.wait_recv()

        def early(h):
            for c in (1, 0):
                for dx in (1, 3):
                    b_rest(c, dx, h).wait_recv()
            acc[h] = contract(0, h, 0, 6)

        early(0)
        for c in (1, 0):
            a_copy(c, 0, 2).wait_recv()
            weigh(0, c, 2)
        pl.semaphore_wait(ready, 2)
        for h in range(2):
            if h == 1:
                early(1)
            for c in (1, 0):
                for copy in relays[h][c]:
                    copy.wait_recv()
            total = acc[h] + contract(0, h, 6, 8)
            for c in (1, 0):
                z_send[c, h] = total[c * 128:(c + 1) * 128].astype(BF16)
                z_copies[h][c].start()
        load_a[1].wait()
        weigh(1, 1, 0)
        a_own[1].wait_recv()
        weigh(1, 0, 0)
        for c in (1, 0):
            for dx in (1, 3):
                a_copy(c, 1, dx).wait_recv()
                weigh(1, c, dx)
        for h in range(2):
            acc[h] = contract(1, h, 0, 6)
        for c in (1, 0):
            a_copy(c, 1, 2).wait_recv()
            weigh(1, c, 2)
        for h in range(2):
            own_send[h] = (acc[h, :128] + contract(1, h, 6, 8, slice(0, 128))).astype(BF16)
            own_copies[h].start()
        for h in range(2):
            own_part[h] = (acc[h, 128:] + contract(1, h, 6, 8, slice(128, 256))).astype(BF16)
        for dx in (1, 3):
            b_copy(1, dx).wait_send()
            for h in range(2):
                b_rest(1, dx, h).wait_send()
        for s in range(2):
            for dx in (1, 3, 2):
                a_copy(1, s, dx).wait_send()
        for copies in relays[0] + relays[1]:
            for copy in copies:
                copy.wait_send()

    def swap(v, tile_bit, lane_bit):
        step, width = 1 << tile_bit, 1 << lane_bit
        v = v.reshape(16 // (2 * step), 2, step, JLO, 128)
        a = v[:, 0].reshape(8, JLO, 128)
        b = v[:, 1].reshape(8, JLO, 128)
        low = (lax.broadcasted_iota(jnp.int32, a.shape, 2) // width) % 2 == 0
        a, b = (jnp.where(low, a, pltpu.roll(b, width, 2)), jnp.where(low, pltpu.roll(a, 128 - width, 2), b))
        shape = (16 // (2 * step), 1, step, JLO, 128)
        return jnp.concatenate([a.reshape(shape), b.reshape(shape)], axis=1).reshape(16, JLO, 128)

    load_s.wait()

    result = jnp.zeros((64, M), F32)
    for top in range(2):
        @pl.when(core == 0)
        def _(top=top):
            own_copies[top].wait_recv()

        z_copies[top][0].wait_recv()
        total = own_part[top].astype(F32) + z_recv[top].astype(F32)
        value = total.astype(BF16).T.reshape(16, JLO, 128)
        for tile_bit, lane_bit in ((0, 0), (1, 1), (2, 2), (3, 3), (3, 6), (2, 5)):
            value = swap(value, tile_bit, lane_bit)
        right = []
        for u in range(4):
            for p in range(2):
                at = pl.ds((u * 2 + p) * 128, 128)
                turned = pl.ds((u * 2 + 1 - p) * 128, 128)
                for rh in range(2):
                    block = value[p * 8 + rh * 4 + u]
                    lhs[top, pl.ds(rh * 16, 16), at] = block if p == 0 else -block
                    lhs[top, pl.ds(32 + rh * 16, 16), turned] = block
                for t in range(8):
                    rl = (t % 2) * 16 + (t // 4) * 8 + (t // 2 % 2) * 4 + u
                    right.append(s_vmem[p, pl.ds(rl * JHI + top * 16, 16)])
        result += jnp.dot(lhs[top], jnp.concatenate(right, axis=0), preferred_element_type=F32)
    out_ref[...] = result.astype(BF16).reshape(2, 2, JLO, M)

    @pl.when(core == 1)
    def _():
        for copy in own_copies + z_copies[0] + z_copies[1]:
            copy.wait_send()


def on_device(amplitudes, first_factor, second_factor):
    arguments = [pltpu.with_memory_space_constraint(a, pltpu.HBM)
                 for a in (jnp.swapaxes(amplitudes, 1, 2), first_factor, second_factor)]
    return pl.pallas_call(
        kernel,
        out_shape=pltpu.VMEM((2, 2, JLO, M), BF16),
        in_specs=[pl.BlockSpec(memory_space=pltpu.HBM)] * 3,
        out_specs=pl.BlockSpec(memory_space=pltpu.VMEM),
        scratch_shapes=[
            pltpu.VMEM((2, G2, M), BF16),
            pltpu.VMEM((2, 2, XS, 2, KH, ROWS), BF16),
            pltpu.VMEM((2, XS, 2, KH, J), BF16),
            pltpu.VMEM((2, 256, 2 * XS * KB), BF16),
            pltpu.VMEM((CHUNKS, 256, CJ), F32),
            pltpu.VMEM((CHUNKS, 128, CJ), BF16),
            pltpu.VMEM((CHUNKS, 128, CJ), BF16),
            pltpu.VMEM((2, CHUNKS, 128, CJ), BF16),
            pltpu.VMEM((CHUNKS, 128, CJ), BF16),
            pltpu.VMEM((2, 64, G2), BF16),
            pltpu.SemaphoreType.DMA((4,)),
            pltpu.SemaphoreType.REGULAR,
            pltpu.SemaphoreType.DMA((7,)),
            pltpu.SemaphoreType.DMA((13,)),
            pltpu.SemaphoreType.DMA((8,)),
            pltpu.SemaphoreType.DMA((14,)),
            pltpu.SemaphoreType.DMA((2, 8)),
            pltpu.SemaphoreType.DMA((2, 2)),
            pltpu.SemaphoreType.DMA((4,)),
            pltpu.SemaphoreType.DMA((2,)),
        ],
        compiler_params=pltpu.CompilerParams(
            collective_id=0, has_side_effects=True, vmem_limit_bytes=32 * 1024 * 1024),
        cost_estimate=pl.CostEstimate(flops=800_000_000, bytes_accessed=2_600_000, transcendentals=0),
    )(*arguments)


def solution(mesh):
    return jax.shard_map(
        on_device, mesh=mesh,
        in_specs=(P(None, "grid", "depth"), P(None, "depth", None), P()),
        out_specs=P(None, ("grid", "depth"), None, None), check_vma=False)
```

```python
import jax
import jax.numpy as jnp
from jax import lax
from jax.experimental import pallas as pl
from jax.experimental.pallas import tpu as pltpu
from jax.sharding import PartitionSpec as P

MESH = pl.DeviceIdType.MESH
XS = 4
JHI = 32
RLO = 32
JLO = 16
J = JHI * JLO
G2 = RLO * JHI
M = 512
KH = 64
KB = 128
ROWS = 128
CHUNKS = 2
CJ = J // CHUNKS
F32 = jnp.float32
BF16 = jnp.bfloat16


def kernel(at_ref, ff_ref, sf_ref, out_ref,
           s_vmem, abuf, bbuf, left, acc, own_send, own_part, z_send, z_recv, lhs,
           local_sem, ready, b_send, b_recv, a_send, a_recv, r_sems, own_sems, z_out, z_in):
    grid = lax.axis_index("grid")
    depth = lax.axis_index("depth")
    x = depth // 4
    zl = (depth // 2) % 2
    core = depth % 2

    def device(dx, which):
        return grid, (lax.rem(x + dx, XS) * 2 + zl) * 2 + which

    def z_device(which):
        return grid, (x * 2 + 1 - zl) * 2 + which

    def rows_of(dx, z):
        return pl.ds(pl.multiple_of((lax.rem(x + dx, XS) * 2 + z) * ROWS, ROWS), ROWS)

    def remote(src, dst, send, recv, to):
        return pltpu.make_async_remote_copy(
            src_ref=src, dst_ref=dst, send_sem=send, recv_sem=recv, device_id=to, device_id_type=MESH)

    z_of = (1 - zl, zl)
    load_s = pltpu.make_async_copy(sf_ref, s_vmem, local_sem.at[3])
    barrier = pltpu.get_barrier_semaphore()

    halves = [pl.ds(h * CJ, CJ) for h in range(2)]

    def b_copy(c, dx):
        p, i = (0, 0) if dx == 1 else (1, 1)
        return remote(ff_ref.at[p], bbuf.at[c, dx, p], b_send.at[i], b_recv.at[c * 6 + i], device(dx, 1))

    def b_rest(c, dx, h):
        p, i = (1, 2 + h) if dx == 1 else (0, 4 + h)
        return remote(ff_ref.at[p, :, halves[h]], bbuf.at[c, dx, p, :, halves[h]], b_send.at[i], b_recv.at[c * 6 + i], device(dx, 1))

    def a_copy(c, s, dx):
        i = s * 3 + dx - 1
        return remote(at_ref.at[:, :, rows_of(dx, z_of[s])], abuf.at[s, c, dx], a_send.at[i], a_recv.at[c * 6 + i], device(dx, 1))

    b_own = remote(ff_ref, bbuf.at[0, 0], b_send.at[6], b_recv.at[12], device(0, 1))
    a_own = [remote(at_ref.at[:, :, rows_of(0, z_of[s])], abuf.at[s, 0, 0], a_send.at[6 + s], a_recv.at[12 + s], device(0, 1))
             for s in range(2)]
    own_copies = [remote(own_send.at[h], own_part.at[h], own_sems.at[0, h], own_sems.at[1, h], device(0, 0)) for h in range(2)]
    z_copies = [[remote(z_send.at[c, h], z_recv.at[h], z_out.at[2 * h + c], z_in.at[h], z_device(c)) for c in range(2)]
                for h in range(2)]

    @pl.when(core == 0)
    def _():
        pl.semaphore_wait(barrier, 5)
        for dx in (1, 3):
            b_copy(0, dx).start()
        for to in (device(0, 1), z_device(1)):
            pl.semaphore_signal(ready, inc=1, device_id=to, device_id_type=MESH)
        for dx in (1, 3, 2):
            a_copy(0, 0, dx).start()
        for dx in (1, 3):
            b_rest(0, dx, 0).start()
        b_own.start()
        a_own[0].start()
        for dx in (1, 3):
            b_rest(0, dx, 1).start()
        a_own[1].start()
        for dx in (1, 3, 2):
            a_copy(0, 1, dx).start()
        load_s.start()
        for dx in (1, 3):
            b_copy(0, dx).wait_send()
            for h in range(2):
                b_rest(0, dx, h).wait_send()
        for s in range(2):
            for dx in (1, 3, 2):
                a_copy(0, s, dx).wait_send()
            a_own[s].wait_send()
        b_own.wait_send()

    minus = jnp.where(lax.broadcasted_iota(jnp.int32, (64, KB), 1) < KH, 1.0, -1.0).astype(BF16)

    order = [(c, slot) for slot in (0, 1, 3, 2) for c in range(2)]

    def weigh(s, c, slot):
        turned = abuf[s, c, slot].reshape(KB, ROWS).T
        lanes = pl.ds(order.index((c, slot)) * KB, KB)
        for side in range(2):
            value = turned[side * 64:(side + 1) * 64]
            left[s, pl.ds(side * 128, 64), lanes] = value * minus
            left[s, pl.ds(side * 128 + 64, 64), lanes] = pltpu.roll(value, KH, 1)

    def contract(s, h, first, last):
        where = pl.ds(h * CJ, CJ)
        right = jnp.concatenate([bbuf[c, slot, :, :, where].reshape(KB, CJ) for c, slot in order[first:last]], axis=0)
        return jnp.dot(left[s, :, pl.ds(first * KB, (last - first) * KB)], right, preferred_element_type=F32)

    @pl.when(core == 1)
    def _():
        for to in [device(dx, 1) for dx in (1, 3, 2)] + [z_device(1)]:
            pl.semaphore_signal(barrier, inc=1, device_id=to, device_id_type=MESH)
        for to in [device(dx, 0) for dx in range(XS)] + [z_device(0)]:
            pl.semaphore_signal(barrier, inc=1, device_id=to, device_id_type=MESH)
        load_b = pltpu.make_async_copy(ff_ref, bbuf.at[1, 0], local_sem.at[0])
        load_a = [pltpu.make_async_copy(at_ref.at[:, :, rows_of(0, z_of[s])], abuf.at[s, 1, 0], local_sem.at[1 + s])
                  for s in range(2)]
        def relay(c, h):
            where = pl.ds(h * CJ, CJ)
            i = 4 * h + 2 * c
            return (remote(bbuf.at[c, 1, 0, :, where], bbuf.at[c, 2, 0, :, where], r_sems.at[0, i], r_sems.at[1, i], device(1, 1)),
                    remote(bbuf.at[c, 3, 1, :, where], bbuf.at[c, 2, 1, :, where], r_sems.at[0, i + 1], r_sems.at[1, i + 1], device(3, 1)))

        relays = [[relay(c, h) for c in range(2)] for h in range(2)]

        pl.semaphore_wait(barrier, 4)
        for dx in (1, 3):
            b_copy(1, dx).start()
        for dx in (1, 3, 2):
            a_copy(1, 0, dx).start()
        for dx in (1, 3):
            b_rest(1, dx, 0).start()
        load_b.start()
        load_a[0].start()
        load_a[1].start()

        def serve(first):
            steps = (first, 4 - first)
            way = {1: 0, 3: 1}

            def pass_on(c, dx, h):
                relays[h][c][way[dx]].start()

            for dx in steps:
                b_copy(1, dx).wait_recv()
                pass_on(1, dx, 0)
            b_copy(0, first).wait_recv()
            pass_on(0, first, 0)
            for dx in (1, 3):
                b_rest(1, dx, 1).start()
            pass_on(1, first, 1)
            pass_on(0, first, 1)
            pass_on(1, steps[1], 1)
            b_copy(0, steps[1]).wait_recv()
            pass_on(0, steps[1], 0)
            pass_on(0, steps[1], 1)

        @pl.when(x == 1)
        def _():
            serve(3)

        @pl.when(x != 1)
        def _():
            serve(1)

        for dx in (1, 3, 2):
            a_copy(1, 1, dx).start()
        load_s.start()
        load_a[0].wait()
        weigh(0, 1, 0)
        for c in (1, 0):
            for dx in (1, 3):
                a_copy(c, 0, dx).wait_recv()
                weigh(0, c, dx)
        a_own[0].wait_recv()
        weigh(0, 0, 0)
        load_b.wait()
        b_own.wait_recv()

        def early(h):
            for c in (1, 0):
                for dx in (1, 3):
                    b_rest(c, dx, h).wait_recv()
            acc[h] = contract(0, h, 0, 6)

        early(0)
        for c in (1, 0):
            a_copy(c, 0, 2).wait_recv()
            weigh(0, c, 2)
        pl.semaphore_wait(ready, 2)
        for h in range(2):
            if h == 1:
                early(1)
            for c in (1, 0):
                for copy in relays[h][c]:
                    copy.wait_recv()
            total = acc[h] + contract(0, h, 6, 8)
            for c in ((1, 0), (0, 1))[h]:
                z_send[c, h] = total[c * 128:(c + 1) * 128].astype(BF16)
                z_copies[h][c].start()
        load_a[1].wait()
        weigh(1, 1, 0)
        a_own[1].wait_recv()
        weigh(1, 0, 0)
        for c in (1, 0):
            for dx in (1, 3):
                a_copy(c, 1, dx).wait_recv()
                weigh(1, c, dx)
        for h in range(2):
            acc[h] = contract(1, h, 0, 6)
        for c in (1, 0):
            a_copy(c, 1, 2).wait_recv()
            weigh(1, c, 2)
        for h in range(2):
            total = acc[h] + contract(1, h, 6, 8)
            own_send[h] = total[:128].astype(BF16)
            own_copies[h].start()
            own_part[h] = total[128:].astype(BF16)
        for dx in (1, 3):
            b_copy(1, dx).wait_send()
            for h in range(2):
                b_rest(1, dx, h).wait_send()
        for s in range(2):
            for dx in (1, 3, 2):
                a_copy(1, s, dx).wait_send()
        for copies in relays[0] + relays[1]:
            for copy in copies:
                copy.wait_send()

    def swap(v, tile_bit, lane_bit):
        step, width = 1 << tile_bit, 1 << lane_bit
        v = v.reshape(16 // (2 * step), 2, step, JLO, 128)
        a = v[:, 0].reshape(8, JLO, 128)
        b = v[:, 1].reshape(8, JLO, 128)
        low = (lax.broadcasted_iota(jnp.int32, a.shape, 2) // width) % 2 == 0
        a, b = (jnp.where(low, a, pltpu.roll(b, width, 2)), jnp.where(low, pltpu.roll(a, 128 - width, 2), b))
        shape = (16 // (2 * step), 1, step, JLO, 128)
        return jnp.concatenate([a.reshape(shape), b.reshape(shape)], axis=1).reshape(16, JLO, 128)

    load_s.wait()

    result = jnp.zeros((64, M), F32)
    for top in range(2):
        @pl.when(core == 0)
        def _(top=top):
            own_copies[top].wait_recv()

        z_copies[top][0].wait_recv()
        total = own_part[top].astype(F32) + z_recv[top].astype(F32)
        value = total.astype(BF16).T.reshape(16, JLO, 128)
        for tile_bit, lane_bit in ((0, 0), (1, 1), (2, 2), (3, 3), (3, 6), (2, 5)):
            value = swap(value, tile_bit, lane_bit)
        right = []
        for u in range(4):
            for p in range(2):
                at = pl.ds((u * 2 + p) * 128, 128)
                turned = pl.ds((u * 2 + 1 - p) * 128, 128)
                for rh in range(2):
                    block = value[p * 8 + rh * 4 + u]
                    lhs[top, pl.ds(rh * 16, 16), at] = block if p == 0 else -block
                    lhs[top, pl.ds(32 + rh * 16, 16), turned] = block
                for t in range(8):
                    rl = (t % 2) * 16 + (t // 4) * 8 + (t // 2 % 2) * 4 + u
                    right.append(s_vmem[p, pl.ds(rl * JHI + top * 16, 16)])
        result += jnp.dot(lhs[top], jnp.concatenate(right, axis=0), preferred_element_type=F32)
    out_ref[...] = result.astype(BF16).reshape(2, 2, JLO, M)

    @pl.when(core == 1)
    def _():
        for copy in own_copies + z_copies[0] + z_copies[1]:
            copy.wait_send()


def on_device(amplitudes, first_factor, second_factor):
    arguments = [pltpu.with_memory_space_constraint(a, pltpu.HBM)
                 for a in (jnp.swapaxes(amplitudes, 1, 2), first_factor, second_factor)]
    return pl.pallas_call(
        kernel,
        out_shape=pltpu.VMEM((2, 2, JLO, M), BF16),
        in_specs=[pl.BlockSpec(memory_space=pltpu.HBM)] * 3,
        out_specs=pl.BlockSpec(memory_space=pltpu.VMEM),
        scratch_shapes=[
            pltpu.VMEM((2, G2, M), BF16),
            pltpu.VMEM((2, 2, XS, 2, KH, ROWS), BF16),
            pltpu.VMEM((2, XS, 2, KH, J), BF16),
            pltpu.VMEM((2, 256, 2 * XS * KB), BF16),
            pltpu.VMEM((CHUNKS, 256, CJ), F32),
            pltpu.VMEM((CHUNKS, 128, CJ), BF16),
            pltpu.VMEM((CHUNKS, 128, CJ), BF16),
            pltpu.VMEM((2, CHUNKS, 128, CJ), BF16),
            pltpu.VMEM((CHUNKS, 128, CJ), BF16),
            pltpu.VMEM((2, 64, G2), BF16),
            pltpu.SemaphoreType.DMA((4,)),
            pltpu.SemaphoreType.REGULAR,
            pltpu.SemaphoreType.DMA((7,)),
            pltpu.SemaphoreType.DMA((13,)),
            pltpu.SemaphoreType.DMA((8,)),
            pltpu.SemaphoreType.DMA((14,)),
            pltpu.SemaphoreType.DMA((2, 8)),
            pltpu.SemaphoreType.DMA((2, 2)),
            pltpu.SemaphoreType.DMA((4,)),
            pltpu.SemaphoreType.DMA((2,)),
        ],
        compiler_params=pltpu.CompilerParams(
            collective_id=0, has_side_effects=True, vmem_limit_bytes=32 * 1024 * 1024),
        cost_estimate=pl.CostEstimate(flops=800_000_000, bytes_accessed=2_600_000, transcendentals=0),
    )(*arguments)


def solution(mesh):
    return jax.shard_map(
        on_device, mesh=mesh,
        in_specs=(P(None, "grid", "depth"), P(None, "depth", None), P()),
        out_specs=P(None, ("grid", "depth"), None, None), check_vma=False)
```

```python
import jax
import jax.numpy as jnp
from jax import lax
from jax.experimental import pallas as pl
from jax.experimental.pallas import tpu as pltpu
from jax.sharding import PartitionSpec as P

MESH = pl.DeviceIdType.MESH
XS = 4
JHI = 32
RLO = 32
JLO = 16
J = JHI * JLO
G2 = RLO * JHI
M = 512
KH = 64
KB = 128
ROWS = 128
CHUNKS = 2
CJ = J // CHUNKS
F32 = jnp.float32
BF16 = jnp.bfloat16


def kernel(at_ref, ff_ref, sf_ref, out_ref,
           s_vmem, abuf, bbuf, left, acc, own_send, own_part, z_send, z_recv, lhs,
           local_sem, ready, b_send, b_recv, a_send, a_recv, r_sems, own_sems, z_out, z_in):
    grid = lax.axis_index("grid")
    depth = lax.axis_index("depth")
    x = depth // 4
    zl = (depth // 2) % 2
    core = depth % 2

    def device(dx, which):
        return grid, (lax.rem(x + dx, XS) * 2 + zl) * 2 + which

    def z_device(which):
        return grid, (x * 2 + 1 - zl) * 2 + which

    def rows_of(dx, z):
        return pl.ds(pl.multiple_of((lax.rem(x + dx, XS) * 2 + z) * ROWS, ROWS), ROWS)

    def remote(src, dst, send, recv, to):
        return pltpu.make_async_remote_copy(
            src_ref=src, dst_ref=dst, send_sem=send, recv_sem=recv, device_id=to, device_id_type=MESH)

    z_of = (1 - zl, zl)
    load_s = pltpu.make_async_copy(sf_ref, s_vmem, local_sem.at[3])
    barrier = pltpu.get_barrier_semaphore()

    halves = [pl.ds(h * CJ, CJ) for h in range(2)]

    def b_copy(c, dx):
        p, i = (0, 0) if dx == 1 else (1, 1)
        return remote(ff_ref.at[p], bbuf.at[c, dx, p], b_send.at[i], b_recv.at[c * 6 + i], device(dx, 1))

    def b_rest(c, dx, h):
        p, i = (1, 2 + h) if dx == 1 else (0, 4 + h)
        return remote(ff_ref.at[p, :, halves[h]], bbuf.at[c, dx, p, :, halves[h]], b_send.at[i], b_recv.at[c * 6 + i], device(dx, 1))

    def a_copy(c, s, dx):
        i = s * 3 + dx - 1
        return remote(at_ref.at[:, :, rows_of(dx, z_of[s])], abuf.at[s, c, dx], a_send.at[i], a_recv.at[c * 6 + i], device(dx, 1))

    b_own = remote(ff_ref, bbuf.at[0, 0], b_send.at[6], b_recv.at[12], device(0, 1))
    a_own = [remote(at_ref.at[:, :, rows_of(0, z_of[s])], abuf.at[s, 0, 0], a_send.at[6 + s], a_recv.at[12 + s], device(0, 1))
             for s in range(2)]
    own_copies = [remote(own_send.at[h], own_part.at[h], own_sems.at[0, h], own_sems.at[1, h], device(0, 0)) for h in range(2)]
    z_copies = [[remote(z_send.at[c, h], z_recv.at[h], z_out.at[2 * h + c], z_in.at[h], z_device(c)) for c in range(2)]
                for h in range(2)]

    @pl.when(core == 0)
    def _():
        pl.semaphore_wait(barrier, 5)
        for dx in (1, 3):
            b_copy(0, dx).start()
        for to in (device(0, 1), z_device(1)):
            pl.semaphore_signal(ready, inc=1, device_id=to, device_id_type=MESH)
        for dx in (2, 1, 3):
            a_copy(0, 0, dx).start()
        for dx in (1, 3):
            b_rest(0, dx, 0).start()
        b_own.start()
        a_own[0].start()
        for dx in (1, 3):
            b_rest(0, dx, 1).start()
        a_own[1].start()
        for dx in (1, 3, 2):
            a_copy(0, 1, dx).start()
        load_s.start()
        for dx in (1, 3):
            b_copy(0, dx).wait_send()
            for h in range(2):
                b_rest(0, dx, h).wait_send()
        for s in range(2):
            for dx in (1, 3, 2):
                a_copy(0, s, dx).wait_send()
            a_own[s].wait_send()
        b_own.wait_send()

    minus = jnp.where(lax.broadcasted_iota(jnp.int32, (64, KB), 1) < KH, 1.0, -1.0).astype(BF16)

    order = [(c, slot) for slot in (0, 1, 3, 2) for c in range(2)]

    def weigh(s, c, slot):
        turned = abuf[s, c, slot].reshape(KB, ROWS).T
        lanes = pl.ds(order.index((c, slot)) * KB, KB)
        for side in range(2):
            value = turned[side * 64:(side + 1) * 64]
            left[s, pl.ds(side * 128, 64), lanes] = value * minus
            left[s, pl.ds(side * 128 + 64, 64), lanes] = pltpu.roll(value, KH, 1)

    def contract(s, h, first, last):
        where = pl.ds(h * CJ, CJ)
        right = jnp.concatenate([bbuf[c, slot, :, :, where].reshape(KB, CJ) for c, slot in order[first:last]], axis=0)
        return jnp.dot(left[s, :, pl.ds(first * KB, (last - first) * KB)], right, preferred_element_type=F32)

    @pl.when(core == 1)
    def _():
        for to in [device(dx, 1) for dx in (1, 3, 2)] + [z_device(1)]:
            pl.semaphore_signal(barrier, inc=1, device_id=to, device_id_type=MESH)
        for to in [device(dx, 0) for dx in range(XS)] + [z_device(0)]:
            pl.semaphore_signal(barrier, inc=1, device_id=to, device_id_type=MESH)
        load_b = pltpu.make_async_copy(ff_ref, bbuf.at[1, 0], local_sem.at[0])
        load_a = [pltpu.make_async_copy(at_ref.at[:, :, rows_of(0, z_of[s])], abuf.at[s, 1, 0], local_sem.at[1 + s])
                  for s in range(2)]
        def relay(c, h):
            where = pl.ds(h * CJ, CJ)
            i = 4 * h + 2 * c
            return (remote(bbuf.at[c, 1, 0, :, where], bbuf.at[c, 2, 0, :, where], r_sems.at[0, i], r_sems.at[1, i], device(1, 1)),
                    remote(bbuf.at[c, 3, 1, :, where], bbuf.at[c, 2, 1, :, where], r_sems.at[0, i + 1], r_sems.at[1, i + 1], device(3, 1)))

        relays = [[relay(c, h) for c in range(2)] for h in range(2)]

        pl.semaphore_wait(barrier, 4)
        for dx in (1, 3):
            b_copy(1, dx).start()
        for dx in (2, 1, 3):
            a_copy(1, 0, dx).start()
        for dx in (1, 3):
            b_rest(1, dx, 0).start()
        load_b.start()
        load_a[0].start()
        load_a[1].start()

        def serve(first):
            steps = (first, 4 - first)
            way = {1: 0, 3: 1}

            def pass_on(c, dx, h):
                relays[h][c][way[dx]].start()

            for dx in steps:
                b_copy(1, dx).wait_recv()
                pass_on(1, dx, 0)
            b_copy(0, first).wait_recv()
            pass_on(0, first, 0)
            for dx in (1, 3):
                b_rest(1, dx, 1).start()
            pass_on(1, first, 1)
            pass_on(0, first, 1)
            pass_on(1, steps[1], 1)
            b_copy(0, steps[1]).wait_recv()
            pass_on(0, steps[1], 0)
            pass_on(0, steps[1], 1)

        @pl.when(x == 1)
        def _():
            serve(3)

        @pl.when(x != 1)
        def _():
            serve(1)

        for dx in (1, 3, 2):
            a_copy(1, 1, dx).start()
        load_s.start()
        load_a[0].wait()
        weigh(0, 1, 0)
        for c in (1, 0):
            for dx in (1, 3):
                a_copy(c, 0, dx).wait_recv()
                weigh(0, c, dx)
        a_own[0].wait_recv()
        weigh(0, 0, 0)
        load_b.wait()
        b_own.wait_recv()

        def early(h):
            for c in (1, 0):
                for dx in (1, 3):
                    b_rest(c, dx, h).wait_recv()
            acc[h] = contract(0, h, 0, 6)

        early(0)
        for c in (1, 0):
            a_copy(c, 0, 2).wait_recv()
            weigh(0, c, 2)
        pl.semaphore_wait(ready, 2)
        for h in range(2):
            if h == 1:
                early(1)
            for c in (1, 0):
                for copy in relays[h][c]:
                    copy.wait_recv()
            total = acc[h] + contract(0, h, 6, 8)
            for c in (1, 0):
                z_send[c, h] = total[c * 128:(c + 1) * 128].astype(BF16)
                z_copies[h][c].start()
        load_a[1].wait()
        weigh(1, 1, 0)
        a_own[1].wait_recv()
        weigh(1, 0, 0)
        for c in (1, 0):
            for dx in (1, 3):
                a_copy(c, 1, dx).wait_recv()
                weigh(1, c, dx)
        for h in range(2):
            acc[h] = contract(1, h, 0, 6)
        for c in (1, 0):
            a_copy(c, 1, 2).wait_recv()
            weigh(1, c, 2)
        for h in range(2):
            total = acc[h] + contract(1, h, 6, 8)
            own_send[h] = total[:128].astype(BF16)
            own_copies[h].start()
            own_part[h] = total[128:].astype(BF16)
        for dx in (1, 3):
            b_copy(1, dx).wait_send()
            for h in range(2):
                b_rest(1, dx, h).wait_send()
        for s in range(2):
            for dx in (1, 3, 2):
                a_copy(1, s, dx).wait_send()
        for copies in relays[0] + relays[1]:
            for copy in copies:
                copy.wait_send()

    def swap(v, tile_bit, lane_bit):
        step, width = 1 << tile_bit, 1 << lane_bit
        v = v.reshape(16 // (2 * step), 2, step, JLO, 128)
        a = v[:, 0].reshape(8, JLO, 128)
        b = v[:, 1].reshape(8, JLO, 128)
        low = (lax.broadcasted_iota(jnp.int32, a.shape, 2) // width) % 2 == 0
        a, b = (jnp.where(low, a, pltpu.roll(b, width, 2)), jnp.where(low, pltpu.roll(a, 128 - width, 2), b))
        shape = (16 // (2 * step), 1, step, JLO, 128)
        return jnp.concatenate([a.reshape(shape), b.reshape(shape)], axis=1).reshape(16, JLO, 128)

    load_s.wait()

    result = jnp.zeros((64, M), F32)
    for top in range(2):
        @pl.when(core == 0)
        def _(top=top):
            own_copies[top].wait_recv()

        z_copies[top][0].wait_recv()
        total = own_part[top].astype(F32) + z_recv[top].astype(F32)
        value = total.astype(BF16).T.reshape(16, JLO, 128)
        for tile_bit, lane_bit in ((0, 0), (1, 1), (2, 2), (3, 3), (3, 6), (2, 5)):
            value = swap(value, tile_bit, lane_bit)
        right = []
        for u in range(4):
            for p in range(2):
                at = pl.ds((u * 2 + p) * 128, 128)
                turned = pl.ds((u * 2 + 1 - p) * 128, 128)
                for rh in range(2):
                    block = value[p * 8 + rh * 4 + u]
                    lhs[top, pl.ds(rh * 16, 16), at] = block if p == 0 else -block
                    lhs[top, pl.ds(32 + rh * 16, 16), turned] = block
                for t in range(8):
                    rl = (t % 2) * 16 + (t // 4) * 8 + (t // 2 % 2) * 4 + u
                    right.append(s_vmem[p, pl.ds(rl * JHI + top * 16, 16)])
        result += jnp.dot(lhs[top], jnp.concatenate(right, axis=0), preferred_element_type=F32)
    out_ref[...] = result.astype(BF16).reshape(2, 2, JLO, M)

    @pl.when(core == 1)
    def _():
        for copy in own_copies + z_copies[0] + z_copies[1]:
            copy.wait_send()


def on_device(amplitudes, first_factor, second_factor):
    arguments = [pltpu.with_memory_space_constraint(a, pltpu.HBM)
                 for a in (jnp.swapaxes(amplitudes, 1, 2), first_factor, second_factor)]
    return pl.pallas_call(
        kernel,
        out_shape=pltpu.VMEM((2, 2, JLO, M), BF16),
        in_specs=[pl.BlockSpec(memory_space=pltpu.HBM)] * 3,
        out_specs=pl.BlockSpec(memory_space=pltpu.VMEM),
        scratch_shapes=[
            pltpu.VMEM((2, G2, M), BF16),
            pltpu.VMEM((2, 2, XS, 2, KH, ROWS), BF16),
            pltpu.VMEM((2, XS, 2, KH, J), BF16),
            pltpu.VMEM((2, 256, 2 * XS * KB), BF16),
            pltpu.VMEM((CHUNKS, 256, CJ), F32),
            pltpu.VMEM((CHUNKS, 128, CJ), BF16),
            pltpu.VMEM((CHUNKS, 128, CJ), BF16),
            pltpu.VMEM((2, CHUNKS, 128, CJ), BF16),
            pltpu.VMEM((CHUNKS, 128, CJ), BF16),
            pltpu.VMEM((2, 64, G2), BF16),
            pltpu.SemaphoreType.DMA((4,)),
            pltpu.SemaphoreType.REGULAR,
            pltpu.SemaphoreType.DMA((7,)),
            pltpu.SemaphoreType.DMA((13,)),
            pltpu.SemaphoreType.DMA((8,)),
            pltpu.SemaphoreType.DMA((14,)),
            pltpu.SemaphoreType.DMA((2, 8)),
            pltpu.SemaphoreType.DMA((2, 2)),
            pltpu.SemaphoreType.DMA((4,)),
            pltpu.SemaphoreType.DMA((2,)),
        ],
        compiler_params=pltpu.CompilerParams(
            collective_id=0, has_side_effects=True, vmem_limit_bytes=32 * 1024 * 1024),
        cost_estimate=pl.CostEstimate(flops=800_000_000, bytes_accessed=2_600_000, transcendentals=0),
    )(*arguments)


def solution(mesh):
    return jax.shard_map(
        on_device, mesh=mesh,
        in_specs=(P(None, "grid", "depth"), P(None, "depth", None), P()),
        out_specs=P(None, ("grid", "depth"), None, None), check_vma=False)
```

```python
import jax
import jax.numpy as jnp
from jax import lax
from jax.experimental import pallas as pl
from jax.experimental.pallas import tpu as pltpu
from jax.sharding import PartitionSpec as P

MESH = pl.DeviceIdType.MESH
XS = 4
JHI = 32
RLO = 32
JLO = 16
J = JHI * JLO
G2 = RLO * JHI
M = 512
KH = 64
KB = 128
ROWS = 128
CHUNKS = 2
CJ = J // CHUNKS
F32 = jnp.float32
BF16 = jnp.bfloat16


def kernel(at_ref, ff_ref, sf_ref, out_ref,
           s_vmem, abuf, bbuf, left, acc, own_send, own_part, z_send, z_recv, lhs,
           local_sem, ready, b_send, b_recv, a_send, a_recv, r_sems, own_sems, z_out, z_in):
    grid = lax.axis_index("grid")
    depth = lax.axis_index("depth")
    x = depth // 4
    zl = (depth // 2) % 2
    core = depth % 2

    def device(dx, which):
        return grid, (lax.rem(x + dx, XS) * 2 + zl) * 2 + which

    def z_device(which):
        return grid, (x * 2 + 1 - zl) * 2 + which

    def rows_of(dx, z):
        return pl.ds(pl.multiple_of((lax.rem(x + dx, XS) * 2 + z) * ROWS, ROWS), ROWS)

    def remote(src, dst, send, recv, to):
        return pltpu.make_async_remote_copy(
            src_ref=src, dst_ref=dst, send_sem=send, recv_sem=recv, device_id=to, device_id_type=MESH)

    z_of = (1 - zl, zl)
    load_s = pltpu.make_async_copy(sf_ref, s_vmem, local_sem.at[3])
    barrier = pltpu.get_barrier_semaphore()

    halves = [pl.ds(h * CJ, CJ) for h in range(2)]

    def b_copy(c, dx):
        p, i = (0, 0) if dx == 1 else (1, 1)
        return remote(ff_ref.at[p], bbuf.at[c, dx, p], b_send.at[i], b_recv.at[c * 6 + i], device(dx, 1))

    def b_rest(c, dx, h):
        p, i = (1, 2 + h) if dx == 1 else (0, 4 + h)
        return remote(ff_ref.at[p, :, halves[h]], bbuf.at[c, dx, p, :, halves[h]], b_send.at[i], b_recv.at[c * 6 + i], device(dx, 1))

    def a_copy(c, s, dx):
        i = s * 3 + dx - 1
        return remote(at_ref.at[:, :, rows_of(dx, z_of[s])], abuf.at[s, c, dx], a_send.at[i], a_recv.at[c * 6 + i], device(dx, 1))

    b_own = remote(ff_ref, bbuf.at[0, 0], b_send.at[6], b_recv.at[12], device(0, 1))
    a_own = [remote(at_ref.at[:, :, rows_of(0, z_of[s])], abuf.at[s, 0, 0], a_send.at[6 + s], a_recv.at[12 + s], device(0, 1))
             for s in range(2)]
    own_copies = [remote(own_send.at[h], own_part.at[h], own_sems.at[0, h], own_sems.at[1, h], device(0, 0)) for h in range(2)]
    z_copies = [[remote(z_send.at[c, h], z_recv.at[h], z_out.at[2 * h + c], z_in.at[h], z_device(c)) for c in range(2)]
                for h in range(2)]

    @pl.when(core == 0)
    def _():
        pl.semaphore_wait(barrier, 5)
        for dx in (1, 3):
            b_copy(0, dx).start()
        for to in (device(0, 1), z_device(1)):
            pl.semaphore_signal(ready, inc=1, device_id=to, device_id_type=MESH)
        for dx in (1, 3, 2):
            a_copy(0, 0, dx).start()
        for dx in (1, 3):
            b_rest(0, dx, 0).start()
        b_own.start()
        a_own[0].start()
        for dx in (1, 3):
            b_rest(0, dx, 1).start()
        a_own[1].start()
        for dx in (1, 3, 2):
            a_copy(0, 1, dx).start()
        load_s.start()
        for dx in (1, 3):
            b_copy(0, dx).wait_send()
            for h in range(2):
                b_rest(0, dx, h).wait_send()
        for s in range(2):
            for dx in (1, 3, 2):
                a_copy(0, s, dx).wait_send()
            a_own[s].wait_send()
        b_own.wait_send()

    minus = jnp.where(lax.broadcasted_iota(jnp.int32, (64, KB), 1) < KH, 1.0, -1.0).astype(BF16)

    order = [(c, slot) for slot in (0, 1, 3, 2) for c in range(2)]

    def weigh(s, c, slot):
        turned = abuf[s, c, slot].reshape(KB, ROWS).T
        lanes = pl.ds(order.index((c, slot)) * KB, KB)
        for side in range(2):
            value = turned[side * 64:(side + 1) * 64]
            left[s, pl.ds(side * 128, 64), lanes] = value * minus
            left[s, pl.ds(side * 128 + 64, 64), lanes] = pltpu.roll(value, KH, 1)

    def contract(s, h, first, last, rows=slice(0, 256)):
        where = pl.ds(h * CJ, CJ)
        right = jnp.concatenate([bbuf[c, slot, :, :, where].reshape(KB, CJ) for c, slot in order[first:last]], axis=0)
        return jnp.dot(left[s, rows, pl.ds(first * KB, (last - first) * KB)], right, preferred_element_type=F32)

    @pl.when(core == 1)
    def _():
        for to in [device(dx, 1) for dx in (1, 3, 2)] + [z_device(1)]:
            pl.semaphore_signal(barrier, inc=1, device_id=to, device_id_type=MESH)
        for to in [device(dx, 0) for dx in range(XS)] + [z_device(0)]:
            pl.semaphore_signal(barrier, inc=1, device_id=to, device_id_type=MESH)
        load_b = pltpu.make_async_copy(ff_ref, bbuf.at[1, 0], local_sem.at[0])
        load_a = [pltpu.make_async_copy(at_ref.at[:, :, rows_of(0, z_of[s])], abuf.at[s, 1, 0], local_sem.at[1 + s])
                  for s in range(2)]
        def relay(c, h):
            where = pl.ds(h * CJ, CJ)
            i = 4 * h + 2 * c
            return (remote(bbuf.at[c, 1, 0, :, where], bbuf.at[c, 2, 0, :, where], r_sems.at[0, i], r_sems.at[1, i], device(1, 1)),
                    remote(bbuf.at[c, 3, 1, :, where], bbuf.at[c, 2, 1, :, where], r_sems.at[0, i + 1], r_sems.at[1, i + 1], device(3, 1)))

        relays = [[relay(c, h) for c in range(2)] for h in range(2)]

        pl.semaphore_wait(barrier, 4)
        for dx in (1, 3):
            b_copy(1, dx).start()
        for dx in (1, 3, 2):
            a_copy(1, 0, dx).start()
        for dx in (1, 3):
            b_rest(1, dx, 0).start()
        load_b.start()
        load_a[0].start()
        load_a[1].start()

        def serve(first):
            steps = (first, 4 - first)
            way = {1: 0, 3: 1}

            def pass_on(c, dx, h):
                relays[h][c][way[dx]].start()

            for dx in steps:
                b_copy(1, dx).wait_recv()
                pass_on(1, dx, 0)
            b_copy(0, first).wait_recv()
            pass_on(0, first, 0)
            for dx in (1, 3):
                b_rest(1, dx, 1).start()
            pass_on(1, first, 1)
            pass_on(0, first, 1)
            pass_on(1, steps[1], 1)
            b_copy(0, steps[1]).wait_recv()
            pass_on(0, steps[1], 0)
            pass_on(0, steps[1], 1)

        @pl.when(x == 1)
        def _():
            serve(3)

        @pl.when(x != 1)
        def _():
            serve(1)

        for dx in (1, 3, 2):
            a_copy(1, 1, dx).start()
        load_s.start()
        load_a[0].wait()
        weigh(0, 1, 0)
        for c in (1, 0):
            for dx in (1, 3):
                a_copy(c, 0, dx).wait_recv()
                weigh(0, c, dx)
        a_own[0].wait_recv()
        weigh(0, 0, 0)
        load_b.wait()
        b_own.wait_recv()

        def early(h):
            for c in (1, 0):
                for dx in (1, 3):
                    b_rest(c, dx, h).wait_recv()
            acc[h] = contract(0, h, 0, 6)

        early(0)
        for c in (1, 0):
            a_copy(c, 0, 2).wait_recv()
            weigh(0, c, 2)
        pl.semaphore_wait(ready, 2)
        for h in range(2):
            if h == 1:
                early(1)
            for c in (1, 0):
                for copy in relays[h][c]:
                    copy.wait_recv()

            def send(cores, h=h):
                for c in cores:
                    rows = slice(c * 128, (c + 1) * 128)
                    z_send[c, h] = (acc[h, rows] + contract(0, h, 6, 8, rows)).astype(BF16)
                    z_copies[h][c].start()

            if h == 0:
                send((1, 0))
            else:
                pl.when(x == 0)(lambda: send((1, 0)))
                pl.when(x != 0)(lambda: send((0, 1)))
        load_a[1].wait()
        weigh(1, 1, 0)
        a_own[1].wait_recv()
        weigh(1, 0, 0)
        for c in (1, 0):
            for dx in (1, 3):
                a_copy(c, 1, dx).wait_recv()
                weigh(1, c, dx)
        for h in range(2):
            acc[h] = contract(1, h, 0, 6)
        for c in (1, 0):
            a_copy(c, 1, 2).wait_recv()
            weigh(1, c, 2)
        for h in range(2):
            total = acc[h] + contract(1, h, 6, 8)
            own_send[h] = total[:128].astype(BF16)
            own_copies[h].start()
            own_part[h] = total[128:].astype(BF16)
        for dx in (1, 3):
            b_copy(1, dx).wait_send()
            for h in range(2):
                b_rest(1, dx, h).wait_send()
        for s in range(2):
            for dx in (1, 3, 2):
                a_copy(1, s, dx).wait_send()
        for copies in relays[0] + relays[1]:
            for copy in copies:
                copy.wait_send()

    def swap(v, tile_bit, lane_bit):
        step, width = 1 << tile_bit, 1 << lane_bit
        v = v.reshape(16 // (2 * step), 2, step, JLO, 128)
        a = v[:, 0].reshape(8, JLO, 128)
        b = v[:, 1].reshape(8, JLO, 128)
        low = (lax.broadcasted_iota(jnp.int32, a.shape, 2) // width) % 2 == 0
        a, b = (jnp.where(low, a, pltpu.roll(b, width, 2)), jnp.where(low, pltpu.roll(a, 128 - width, 2), b))
        shape = (16 // (2 * step), 1, step, JLO, 128)
        return jnp.concatenate([a.reshape(shape), b.reshape(shape)], axis=1).reshape(16, JLO, 128)

    load_s.wait()

    result = jnp.zeros((64, M), F32)
    for top in range(2):
        @pl.when(core == 0)
        def _(top=top):
            own_copies[top].wait_recv()

        z_copies[top][0].wait_recv()
        total = own_part[top].astype(F32) + z_recv[top].astype(F32)
        value = total.astype(BF16).T.reshape(16, JLO, 128)
        for tile_bit, lane_bit in ((0, 0), (1, 1), (2, 2), (3, 3), (3, 6), (2, 5)):
            value = swap(value, tile_bit, lane_bit)
        right = []
        for u in range(4):
            for p in range(2):
                at = pl.ds((u * 2 + p) * 128, 128)
                turned = pl.ds((u * 2 + 1 - p) * 128, 128)
                for rh in range(2):
                    block = value[p * 8 + rh * 4 + u]
                    lhs[top, pl.ds(rh * 16, 16), at] = block if p == 0 else -block
                    lhs[top, pl.ds(32 + rh * 16, 16), turned] = block
                for t in range(8):
                    rl = (t % 2) * 16 + (t // 4) * 8 + (t // 2 % 2) * 4 + u
                    right.append(s_vmem[p, pl.ds(rl * JHI + top * 16, 16)])
        result += jnp.dot(lhs[top], jnp.concatenate(right, axis=0), preferred_element_type=F32)
    out_ref[...] = result.astype(BF16).reshape(2, 2, JLO, M)

    @pl.when(core == 1)
    def _():
        for copy in own_copies + z_copies[0] + z_copies[1]:
            copy.wait_send()


def on_device(amplitudes, first_factor, second_factor):
    arguments = [pltpu.with_memory_space_constraint(a, pltpu.HBM)
                 for a in (jnp.swapaxes(amplitudes, 1, 2), first_factor, second_factor)]
    return pl.pallas_call(
        kernel,
        out_shape=pltpu.VMEM((2, 2, JLO, M), BF16),
        in_specs=[pl.BlockSpec(memory_space=pltpu.HBM)] * 3,
        out_specs=pl.BlockSpec(memory_space=pltpu.VMEM),
        scratch_shapes=[
            pltpu.VMEM((2, G2, M), BF16),
            pltpu.VMEM((2, 2, XS, 2, KH, ROWS), BF16),
            pltpu.VMEM((2, XS, 2, KH, J), BF16),
            pltpu.VMEM((2, 256, 2 * XS * KB), BF16),
            pltpu.VMEM((CHUNKS, 256, CJ), F32),
            pltpu.VMEM((CHUNKS, 128, CJ), BF16),
            pltpu.VMEM((CHUNKS, 128, CJ), BF16),
            pltpu.VMEM((2, CHUNKS, 128, CJ), BF16),
            pltpu.VMEM((CHUNKS, 128, CJ), BF16),
            pltpu.VMEM((2, 64, G2), BF16),
            pltpu.SemaphoreType.DMA((4,)),
            pltpu.SemaphoreType.REGULAR,
            pltpu.SemaphoreType.DMA((7,)),
            pltpu.SemaphoreType.DMA((13,)),
            pltpu.SemaphoreType.DMA((8,)),
            pltpu.SemaphoreType.DMA((14,)),
            pltpu.SemaphoreType.DMA((2, 8)),
            pltpu.SemaphoreType.DMA((2, 2)),
            pltpu.SemaphoreType.DMA((4,)),
            pltpu.SemaphoreType.DMA((2,)),
        ],
        compiler_params=pltpu.CompilerParams(
            collective_id=0, has_side_effects=True, vmem_limit_bytes=32 * 1024 * 1024),
        cost_estimate=pl.CostEstimate(flops=800_000_000, bytes_accessed=2_600_000, transcendentals=0),
    )(*arguments)


def solution(mesh):
    return jax.shard_map(
        on_device, mesh=mesh,
        in_specs=(P(None, "grid", "depth"), P(None, "depth", None), P()),
        out_specs=P(None, ("grid", "depth"), None, None), check_vma=False)
```

```python
import jax
import jax.numpy as jnp
from jax import lax
from jax.experimental import pallas as pl
from jax.experimental.pallas import tpu as pltpu
from jax.sharding import PartitionSpec as P

MESH = pl.DeviceIdType.MESH
XS = 4
JHI = 32
RLO = 32
JLO = 16
J = JHI * JLO
G2 = RLO * JHI
M = 512
KH = 64
KB = 128
ROWS = 128
CHUNKS = 2
CJ = J // CHUNKS
F32 = jnp.float32
BF16 = jnp.bfloat16


def kernel(at_ref, ff_ref, sf_ref, out_ref,
           s_vmem, abuf, bbuf, left, acc, own_send, own_part, z_send, z_recv, lhs,
           local_sem, ready, b_send, b_recv, a_send, a_recv, r_sems, own_sems, z_out, z_in):
    grid = lax.axis_index("grid")
    depth = lax.axis_index("depth")
    x = depth // 4
    zl = (depth // 2) % 2
    core = depth % 2

    def device(dx, which):
        return grid, (lax.rem(x + dx, XS) * 2 + zl) * 2 + which

    def z_device(which):
        return grid, (x * 2 + 1 - zl) * 2 + which

    def rows_of(dx, z):
        return pl.ds(pl.multiple_of((lax.rem(x + dx, XS) * 2 + z) * ROWS, ROWS), ROWS)

    def remote(src, dst, send, recv, to):
        return pltpu.make_async_remote_copy(
            src_ref=src, dst_ref=dst, send_sem=send, recv_sem=recv, device_id=to, device_id_type=MESH)

    z_of = (1 - zl, zl)
    load_s = pltpu.make_async_copy(sf_ref, s_vmem, local_sem.at[3])
    barrier = pltpu.get_barrier_semaphore()

    halves = [pl.ds(h * CJ, CJ) for h in range(2)]

    def b_copy(c, dx):
        p, i = (0, 0) if dx == 1 else (1, 1)
        return remote(ff_ref.at[p], bbuf.at[c, dx, p], b_send.at[i], b_recv.at[c * 6 + i], device(dx, 1))

    def b_rest(c, dx, h):
        p, i = (1, 2 + h) if dx == 1 else (0, 4 + h)
        return remote(ff_ref.at[p, :, halves[h]], bbuf.at[c, dx, p, :, halves[h]], b_send.at[i], b_recv.at[c * 6 + i], device(dx, 1))

    def a_copy(c, s, dx):
        i = s * 3 + dx - 1
        return remote(at_ref.at[:, :, rows_of(dx, z_of[s])], abuf.at[s, c, dx], a_send.at[i], a_recv.at[c * 6 + i], device(dx, 1))

    b_own = remote(ff_ref, bbuf.at[0, 0], b_send.at[6], b_recv.at[12], device(0, 1))
    a_own = [remote(at_ref.at[:, :, rows_of(0, z_of[s])], abuf.at[s, 0, 0], a_send.at[6 + s], a_recv.at[12 + s], device(0, 1))
             for s in range(2)]
    own_copies = [remote(own_send.at[h], own_part.at[h], own_sems.at[0, h], own_sems.at[1, h], device(0, 0)) for h in range(2)]
    z_copies = [[remote(z_send.at[c, h], z_recv.at[h], z_out.at[2 * h + c], z_in.at[h], z_device(c)) for c in range(2)]
                for h in range(2)]

    @pl.when(core == 0)
    def _():
        pl.semaphore_wait(barrier, 5)
        for dx in (1, 3):
            b_copy(0, dx).start()
        for to in (device(0, 1), z_device(1)):
            pl.semaphore_signal(ready, inc=1, device_id=to, device_id_type=MESH)
        for dx in (1, 3, 2):
            a_copy(0, 0, dx).start()
        b_own.start()
        a_own[0].start()
        for dx in (1, 3):
            b_rest(0, dx, 0).start()
        for dx in (1, 3):
            b_rest(0, dx, 1).start()
        a_own[1].start()
        for dx in (1, 3, 2):
            a_copy(0, 1, dx).start()
        load_s.start()
        for dx in (1, 3):
            b_copy(0, dx).wait_send()
            for h in range(2):
                b_rest(0, dx, h).wait_send()
        for s in range(2):
            for dx in (1, 3, 2):
                a_copy(0, s, dx).wait_send()
            a_own[s].wait_send()
        b_own.wait_send()

    minus = jnp.where(lax.broadcasted_iota(jnp.int32, (64, KB), 1) < KH, 1.0, -1.0).astype(BF16)

    order = [(c, slot) for slot in (0, 1, 3, 2) for c in range(2)]

    def weigh(s, c, slot):
        turned = abuf[s, c, slot].reshape(KB, ROWS).T
        lanes = pl.ds(order.index((c, slot)) * KB, KB)
        for side in range(2):
            value = turned[side * 64:(side + 1) * 64]
            left[s, pl.ds(side * 128, 64), lanes] = value * minus
            left[s, pl.ds(side * 128 + 64, 64), lanes] = pltpu.roll(value, KH, 1)

    def contract(s, h, first, last):
        where = pl.ds(h * CJ, CJ)
        right = jnp.concatenate([bbuf[c, slot, :, :, where].reshape(KB, CJ) for c, slot in order[first:last]], axis=0)
        return jnp.dot(left[s, :, pl.ds(first * KB, (last - first) * KB)], right, preferred_element_type=F32)

    @pl.when(core == 1)
    def _():
        for to in [device(dx, 1) for dx in (1, 3, 2)] + [z_device(1)]:
            pl.semaphore_signal(barrier, inc=1, device_id=to, device_id_type=MESH)
        for to in [device(dx, 0) for dx in range(XS)] + [z_device(0)]:
            pl.semaphore_signal(barrier, inc=1, device_id=to, device_id_type=MESH)
        load_b = pltpu.make_async_copy(ff_ref, bbuf.at[1, 0], local_sem.at[0])
        load_a = [pltpu.make_async_copy(at_ref.at[:, :, rows_of(0, z_of[s])], abuf.at[s, 1, 0], local_sem.at[1 + s])
                  for s in range(2)]
        def relay(c, h):
            where = pl.ds(h * CJ, CJ)
            i = 4 * h + 2 * c
            return (remote(bbuf.at[c, 1, 0, :, where], bbuf.at[c, 2, 0, :, where], r_sems.at[0, i], r_sems.at[1, i], device(1, 1)),
                    remote(bbuf.at[c, 3, 1, :, where], bbuf.at[c, 2, 1, :, where], r_sems.at[0, i + 1], r_sems.at[1, i + 1], device(3, 1)))

        relays = [[relay(c, h) for c in range(2)] for h in range(2)]

        pl.semaphore_wait(barrier, 4)
        for dx in (1, 3):
            b_copy(1, dx).start()
        for dx in (1, 3, 2):
            a_copy(1, 0, dx).start()
        for dx in (1, 3):
            b_rest(1, dx, 0).start()
        load_b.start()
        load_a[0].start()
        load_a[1].start()

        def serve(first):
            steps = (first, 4 - first)
            way = {1: 0, 3: 1}

            def pass_on(c, dx, h):
                relays[h][c][way[dx]].start()

            for dx in steps:
                b_copy(1, dx).wait_recv()
                pass_on(1, dx, 0)
            b_copy(0, first).wait_recv()
            pass_on(0, first, 0)
            for dx in (1, 3):
                b_rest(1, dx, 1).start()
            pass_on(1, first, 1)
            pass_on(0, first, 1)
            pass_on(1, steps[1], 1)
            b_copy(0, steps[1]).wait_recv()
            pass_on(0, steps[1], 0)
            pass_on(0, steps[1], 1)

        @pl.when(x == 1)
        def _():
            serve(3)

        @pl.when(x != 1)
        def _():
            serve(1)

        for dx in (1, 3, 2):
            a_copy(1, 1, dx).start()
        load_s.start()
        load_a[0].wait()
        weigh(0, 1, 0)
        for c in (1, 0):
            for dx in (1, 3):
                a_copy(c, 0, dx).wait_recv()
                weigh(0, c, dx)
        a_own[0].wait_recv()
        weigh(0, 0, 0)
        load_b.wait()
        b_own.wait_recv()

        def early(h):
            for c in (1, 0):
                for dx in (1, 3):
                    b_rest(c, dx, h).wait_recv()
            acc[h] = contract(0, h, 0, 6)

        early(0)
        for c in (1, 0):
            a_copy(c, 0, 2).wait_recv()
            weigh(0, c, 2)
        pl.semaphore_wait(ready, 2)
        for h in range(2):
            if h == 1:
                early(1)
            for c in (1, 0):
                for copy in relays[h][c]:
                    copy.wait_recv()
            total = acc[h] + contract(0, h, 6, 8)
            for c in (1, 0):
                z_send[c, h] = total[c * 128:(c + 1) * 128].astype(BF16)
                z_copies[h][c].start()
        load_a[1].wait()
        weigh(1, 1, 0)
        a_own[1].wait_recv()
        weigh(1, 0, 0)
        for c in (1, 0):
            for dx in (1, 3):
                a_copy(c, 1, dx).wait_recv()
                weigh(1, c, dx)
        for h in range(2):
            acc[h] = contract(1, h, 0, 6)
        for c in (1, 0):
            a_copy(c, 1, 2).wait_recv()
            weigh(1, c, 2)
        for h in range(2):
            total = acc[h] + contract(1, h, 6, 8)
            own_send[h] = total[:128].astype(BF16)
            own_copies[h].start()
            own_part[h] = total[128:].astype(BF16)
        for dx in (1, 3):
            b_copy(1, dx).wait_send()
            for h in range(2):
                b_rest(1, dx, h).wait_send()
        for s in range(2):
            for dx in (1, 3, 2):
                a_copy(1, s, dx).wait_send()
        for copies in relays[0] + relays[1]:
            for copy in copies:
                copy.wait_send()

    def swap(v, tile_bit, lane_bit):
        step, width = 1 << tile_bit, 1 << lane_bit
        v = v.reshape(16 // (2 * step), 2, step, JLO, 128)
        a = v[:, 0].reshape(8, JLO, 128)
        b = v[:, 1].reshape(8, JLO, 128)
        low = (lax.broadcasted_iota(jnp.int32, a.shape, 2) // width) % 2 == 0
        a, b = (jnp.where(low, a, pltpu.roll(b, width, 2)), jnp.where(low, pltpu.roll(a, 128 - width, 2), b))
        shape = (16 // (2 * step), 1, step, JLO, 128)
        return jnp.concatenate([a.reshape(shape), b.reshape(shape)], axis=1).reshape(16, JLO, 128)

    load_s.wait()

    result = jnp.zeros((64, M), F32)
    for top in range(2):
        @pl.when(core == 0)
        def _(top=top):
            own_copies[top].wait_recv()

        z_copies[top][0].wait_recv()
        total = own_part[top].astype(F32) + z_recv[top].astype(F32)
        value = total.astype(BF16).T.reshape(16, JLO, 128)
        for tile_bit, lane_bit in ((0, 0), (1, 1), (2, 2), (3, 3), (3, 6), (2, 5)):
            value = swap(value, tile_bit, lane_bit)
        right = []
        for u in range(4):
            for p in range(2):
                at = pl.ds((u * 2 + p) * 128, 128)
                turned = pl.ds((u * 2 + 1 - p) * 128, 128)
                for rh in range(2):
                    block = value[p * 8 + rh * 4 + u]
                    lhs[top, pl.ds(rh * 16, 16), at] = block if p == 0 else -block
                    lhs[top, pl.ds(32 + rh * 16, 16), turned] = block
                for t in range(8):
                    rl = (t % 2) * 16 + (t // 4) * 8 + (t // 2 % 2) * 4 + u
                    right.append(s_vmem[p, pl.ds(rl * JHI + top * 16, 16)])
        result += jnp.dot(lhs[top], jnp.concatenate(right, axis=0), preferred_element_type=F32)
    out_ref[...] = result.astype(BF16).reshape(2, 2, JLO, M)

    @pl.when(core == 1)
    def _():
        for copy in own_copies + z_copies[0] + z_copies[1]:
            copy.wait_send()


def on_device(amplitudes, first_factor, second_factor):
    arguments = [pltpu.with_memory_space_constraint(a, pltpu.HBM)
                 for a in (jnp.swapaxes(amplitudes, 1, 2), first_factor, second_factor)]
    return pl.pallas_call(
        kernel,
        out_shape=pltpu.VMEM((2, 2, JLO, M), BF16),
        in_specs=[pl.BlockSpec(memory_space=pltpu.HBM)] * 3,
        out_specs=pl.BlockSpec(memory_space=pltpu.VMEM),
        scratch_shapes=[
            pltpu.VMEM((2, G2, M), BF16),
            pltpu.VMEM((2, 2, XS, 2, KH, ROWS), BF16),
            pltpu.VMEM((2, XS, 2, KH, J), BF16),
            pltpu.VMEM((2, 256, 2 * XS * KB), BF16),
            pltpu.VMEM((CHUNKS, 256, CJ), F32),
            pltpu.VMEM((CHUNKS, 128, CJ), BF16),
            pltpu.VMEM((CHUNKS, 128, CJ), BF16),
            pltpu.VMEM((2, CHUNKS, 128, CJ), BF16),
            pltpu.VMEM((CHUNKS, 128, CJ), BF16),
            pltpu.VMEM((2, 64, G2), BF16),
            pltpu.SemaphoreType.DMA((4,)),
            pltpu.SemaphoreType.REGULAR,
            pltpu.SemaphoreType.DMA((7,)),
            pltpu.SemaphoreType.DMA((13,)),
            pltpu.SemaphoreType.DMA((8,)),
            pltpu.SemaphoreType.DMA((14,)),
            pltpu.SemaphoreType.DMA((2, 8)),
            pltpu.SemaphoreType.DMA((2, 2)),
            pltpu.SemaphoreType.DMA((4,)),
            pltpu.SemaphoreType.DMA((2,)),
        ],
        compiler_params=pltpu.CompilerParams(
            collective_id=0, has_side_effects=True, vmem_limit_bytes=32 * 1024 * 1024),
        cost_estimate=pl.CostEstimate(flops=800_000_000, bytes_accessed=2_600_000, transcendentals=0),
    )(*arguments)


def solution(mesh):
    return jax.shard_map(
        on_device, mesh=mesh,
        in_specs=(P(None, "grid", "depth"), P(None, "depth", None), P()),
        out_specs=P(None, ("grid", "depth"), None, None), check_vma=False)
```
